32 devices in a mesh: section: 2 (over core), dp: 4 (over y, x), ctx: 4 (over z).
Axes of the slice: x: 2, y: 2, z: 4, core: 2. Of those that a mesh axis runs over, the one named last changes fastest.
Arguments:
- ends: bfloat16 [2, 8, 1024, 768], P('section', 'dp', 'ctx'), may hold values from -6 to 6
- char_ends: bfloat16 [2, 8, 2048, 768], P('section', 'dp', 'ctx'), may hold values from -6 to 6
- char_ids: int32 [8, 2048], P('dp', 'ctx'), may hold values from 0 to 999
- groups: int32 [8, 2048], P('dp', 'ctx'), may hold values from -1 to 1023, as said below
- lengths: int32 [8], P('dp'), may hold values from 512 to 1024, as said below
- w_qkv: bfloat16 [2, 768, 2304], P('section'), may hold values from -0.21875 to 0.21875
- biases: float32 [2, 5, 768], P('section'), may hold values from -2 to 2
- w_out: bfloat16 [2, 768, 768], P('section'), may hold values from -1.75 to 1.75
- w_up: bfloat16 [2, 768, 3072], P('section'), may hold values from -0.21875 to 0.21875
- b_up: float32 [2, 3072], P('section'), may hold values from -2 to 2
- w_down: bfloat16 [2, 3072, 768], P('section'), may hold values from -0.109375 to 0.109375
- ln_gain: float32 [2, 4, 768], P('section'), may hold values from 0.5 to 1.5
- ln_shift: float32 [2, 4, 768], P('section'), may hold values from -1.2 to 1.2
- char_table: bfloat16 [2, 1000, 768], P('section'), may hold values from -3 to 3
- w_gru: bfloat16 [2, 768, 1536], P('section'), may hold values from -0.21875 to 0.21875
- b_gru: float32 [2, 1536], P('section')
- w_conv: bfloat16 [2, 3, 1536, 768], P('section'), may hold values from -0.09375 to 0.09375
Outputs:
- ends_out: bfloat16 [2, 8, 1024, 768], P('section', 'dp', 'ctx')
- char_ends_out: bfloat16 [2, 8, 2048, 768], P('section', 'dp', 'ctx')
- grad_w_qkv: float32 [2, 768, 2304], P('section', ('dp', 'ctx'))
- grad_biases: float32 [2, 5, 768], P('section', None, ('dp', 'ctx'))
- grad_w_out: float32 [2, 768, 768], P('section', ('dp', 'ctx'))
- grad_w_up: float32 [2, 768, 3072], P('section', ('dp', 'ctx'))
- grad_b_up: float32 [2, 3072], P('section', ('dp', 'ctx'))
- grad_w_down: float32 [2, 3072, 768], P('section', ('dp', 'ctx'))
- grad_ln_gain: float32 [2, 4, 768], P('section', None, ('dp', 'ctx'))
- grad_ln_shift: float32 [2, 4, 768], P('section', None, ('dp', 'ctx'))
- grad_char_table: float32 [2, 1000, 768], P('section', None, ('dp', 'ctx'))
- grad_w_gru: float32 [2, 768, 1536], P('section', ('dp', 'ctx'))
- grad_b_gru: float32 [2, 1536], P('section', ('dp', 'ctx'))
- grad_w_conv: float32 [2, 3, 1536, 768], P('section', None, ('dp', 'ctx'))
The draws below stay inside these ranges and needn't reach their ends.
Inputs may be any that keep to these rules, and one draw needn't show every extreme that they name: `groups`: slots 512 * k to 512 * (k + 1) - 1 of a sequence hold, in order, the chars of its tokens 256 * k to 256 * (k + 1) - 1, each token 1 to 2 slots and some token of each such block 2, followed by empty slots (-1). `lengths`: in each aligned block of 2 sequences one has length 1024.
All inputs are finite; a program needn't handle non-finite values.
Results may differ from the reference program's by a relative error of at most 0.015.
Values may be sent and summed in bfloat16 or wider, within the bound.
A program may use at most 384 MiB of HBM per device.

```python
import math
import jax
import jax.numpy as jnp
from jax import lax

D = 768
HEADS = 12
FF = 3072
GRU = 384
CHAR_VOCAB = 1000
KERNEL = 3
CHAR_MOST = 2
LENGTH = 1024
TOK_CTX = 256
CH_CTX = 512
CH = 2048
SEQ_DEV = 2
SEQS = 8
N_DP = 4
N_CTX = 4


def draw_groups(key, part):
    key = jax.random.fold_in(key, 11)
    first, second = jax.random.split(key)
    counts = jax.random.randint(first, (SEQS, N_CTX, TOK_CTX), 1, CHAR_MOST + 1)
    chosen = jax.random.randint(second, (SEQS, N_CTX, 1), 0, TOK_CTX)
    counts = jnp.where(jnp.arange(TOK_CTX)[None, None, :] == chosen, CHAR_MOST, counts)
    starts = jnp.cumsum(counts, axis=-1) - counts
    filled = jnp.sum(counts, axis=-1, keepdims=True)
    slots = jnp.arange(CH_CTX)
    begun = (starts[:, :, None, :] <= slots[None, None, :, None]).astype(jnp.int32)
    local = jnp.sum(begun, axis=-1) - 1
    token = local + jnp.arange(N_CTX)[None, :, None] * TOK_CTX
    token = jnp.where(slots[None, None, :] < filled, token, -1)
    return token.reshape(SEQS, N_CTX * CH_CTX).astype(jnp.int32)


def draw_lengths(key, part):
    key = jax.random.fold_in(key, 23)
    first, second = jax.random.split(key)
    drawn = jax.random.randint(first, (N_DP, SEQ_DEV), LENGTH // 2, LENGTH + 1)
    chosen = jax.random.randint(second, (N_DP, 1), 0, SEQ_DEV)
    drawn = jnp.where(jnp.arange(SEQ_DEV)[None, :] == chosen, LENGTH, drawn)
    return drawn.reshape(SEQS).astype(jnp.int32)


def draw_b_gru(key, part):
    key = jax.random.fold_in(key, 37)
    keys = jax.random.split(key, 4)
    share = 0.5
    fast = jax.random.uniform(keys[0], (2, 2, GRU)) < share
    fast_rate = jnp.exp(jax.random.uniform(keys[1], (2, 2, GRU), minval=jnp.log(1.0 / 50.0), maxval=jnp.log(1.0 / 20.0)))
    slow_rate = jnp.exp(jax.random.uniform(keys[2], (2, 2, GRU), minval=jnp.log(0.25 / CH), maxval=jnp.log(2.0 / CH)))
    rate = jnp.where(fast, fast_rate, slow_rate)
    rate_bias = jnp.log(rate) - jnp.log1p(-rate)
    target = jnp.clip(jax.random.normal(keys[3], (2, 2, GRU)), -3.0, 3.0)
    return jnp.stack([rate_bias, target], axis=2).reshape(2, 4 * GRU).astype(jnp.float32)


def place_ends(result, key, low, top_value):
    longest = result.shape.index(max(result.shape))
    spots = []
    for shift in (0, 1):
        where = [jax.random.randint(jax.random.fold_in(key, axis), (), 0, length) for axis, length in enumerate(result.shape)]
        where[longest] = (where[longest] + shift) % result.shape[longest]
        spots.append(tuple(where))
    return result.at[spots[0]].set(low).at[spots[1]].set(top_value)


def block_levels(key, extent, cuts, least, top_value):
    loudness, own = 1.0, jax.random.fold_in(key, 6)
    for axis_at, blocks in cuts:
        steps = jnp.exp(jax.random.uniform(jax.random.fold_in(own, axis_at), (blocks,), jnp.float32, least / len(cuts), top_value / len(cuts)))
        loudness = loudness * jnp.repeat(steps, extent[axis_at] // blocks).reshape([-1 if axis == axis_at else 1 for axis in range(len(extent))])
    return loudness


def noise(rng, extent, scale, bound, cuts=(), kind=jnp.bfloat16):
    values = jax.random.normal(rng, extent, jnp.float32) * scale
    if len(cuts) > 0:
        values = block_levels(rng, extent, cuts, -0.22, 0.18) * values
    return jnp.clip(values, min=-bound, max=bound).astype(kind)


def setup_inputs(seed: int = 0) -> dict:
    splits = jax.random.split(jax.random.key(seed), 18)
    ends = noise(splits[0], (2, SEQS, LENGTH, D), 1.0, 6.0, ((0, 2), (1, 4), (2, 4)))
    char_ends = noise(splits[1], (2, SEQS, CH, D), 1.0, 6.0, ((0, 2), (1, 4), (2, 4)))
    char_ids = place_ends(jax.random.randint(splits[2], (SEQS, CH), 0, CHAR_VOCAB), jax.random.fold_in(splits[2], 1), 0, CHAR_VOCAB - 1).astype(jnp.int32)
    groups = draw_groups(jax.random.fold_in(splits[17], 71), 0)
    lengths = draw_lengths(jax.random.fold_in(splits[17], 71), 0)
    w_qkv = noise(splits[5], (2, D, 3 * D), D ** -0.5, 0.21875, ((0, 2),))
    biases = noise(splits[6], (2, 5, D), 0.3, 2.0, ((0, 2),), jnp.float32)
    w_out = noise(splits[7], (2, D, D), (D // 64) ** -0.5, 1.75, ((0, 2),))
    w_up = noise(splits[8], (2, D, FF), D ** -0.5, 0.21875, ((0, 2),))
    b_up = noise(splits[9], (2, FF), 0.3, 2.0, ((0, 2),), jnp.float32)
    w_down = noise(splits[10], (2, FF, D), FF ** -0.5, 0.109375, ((0, 2),))
    ln_gain = jnp.clip(1.0 + 0.1 * jax.random.normal(splits[11], (2, 4, D), jnp.float32), 0.5, 1.5)
    ln_shift = noise(splits[12], (2, 4, D), 0.2, 1.2, ((0, 2),), jnp.float32)
    char_table = noise(splits[13], (2, CHAR_VOCAB, D), 0.5, 3.0, ((0, 2),))
    w_gru = noise(splits[14], (2, D, 4 * GRU), D ** -0.5, 0.21875, ((0, 2),))
    b_gru = draw_b_gru(jax.random.fold_in(splits[17], 71), 0)
    w_conv = noise(splits[16], (2, KERNEL, 2 * D, D), (KERNEL * 2 * D) ** -0.5, 0.09375, ((0, 2),))
    return {"ends": ends, "char_ends": char_ends, "char_ids": char_ids, "groups": groups, "lengths": lengths, "w_qkv": w_qkv, "biases": biases, "w_out": w_out, "w_up": w_up, "b_up": b_up, "w_down": w_down, "ln_gain": ln_gain, "ln_shift": ln_shift, "char_table": char_table, "w_gru": w_gru, "b_gru": b_gru, "w_conv": w_conv}


HIGHEST = lax.Precision.HIGHEST
NORM_EPS = 1e-06
MASKED = -1000000000.0

@jax.custom_vjp
def low(v):
    return lax.optimization_barrier(v.astype(jnp.bfloat16)).astype(jnp.float32)

@jax.custom_vjp
def low_back(v):
    return v

def low_keep(v):
    return (low(v), None)

def low_pass(kept, grad):
    return (grad,)

def back_keep(v):
    return (v, None)

def back_low(kept, grad):
    return (low(grad),)
low.defvjp(low_keep, low_pass)
low_back.defvjp(back_keep, back_low)

def matmul(left, right):
    return jnp.dot(left, right, precision=HIGHEST)

def layer_norm(values, gain, shift):
    centred = values - lax.optimization_barrier(jnp.mean(values, axis=-1, keepdims=True))
    spread = lax.optimization_barrier(jnp.mean(centred * centred, axis=-1, keepdims=True))
    return centred * lax.rsqrt(spread + NORM_EPS) * gain + shift

def gelu_exact(values):
    return jax.nn.gelu(values, approximate=False)

def affine_join(earlier, later):
    return (earlier[0] * later[0], later[0] * earlier[1] + later[1])

def direction_terms(projected, present, offset, width):
    rates = projected[..., offset:offset + width]
    targets = projected[..., offset + width:offset + 2 * width]
    live = present[..., None]
    retain = jnp.where(live, jax.nn.sigmoid(-rates), 1.0)
    inflow = jnp.where(live, jax.nn.sigmoid(rates) * targets, 0.0)
    return (retain, inflow)

def both_directions(projected, present):
    width = projected.shape[-1] // 4
    retain_f, inflow_f = direction_terms(projected, present, 0, width)
    retain_b, inflow_b = direction_terms(projected, present, 2 * width, width)
    decay_low, state_low = lax.associative_scan(affine_join, (retain_f, inflow_f), axis=1)
    decay_high, state_high = lax.associative_scan(affine_join, (retain_b, inflow_b), axis=1, reverse=True)
    return (decay_low, state_low, decay_high, state_high)

def attend_block(query_block, keys, values, visible):
    scale = query_block.shape[-1] ** (-0.5)
    scores = jnp.einsum('qhe,khe->hqk', query_block, keys, precision=HIGHEST) * scale
    scores = low_back(jnp.where(visible[None, None, :], scores, MASKED))
    top = lax.optimization_barrier(jnp.max(scores, axis=-1, keepdims=True))
    total = top + jnp.log(lax.optimization_barrier(jnp.sum(jnp.exp(scores - top), axis=-1, keepdims=True)))
    probs = low(jnp.exp(scores - total))
    return low(low_back(jnp.einsum('hqk,khe->qhe', probs, values, precision=HIGHEST)))

def layer(params, tokens, chars, ids, groups, length):
    w_qkv, biases, w_out, w_up, b_up, w_down, gains, shifts, table, w_gru, b_gru, w_conv = params
    tokens = low_back(tokens)
    chars = low_back(chars)
    rows, width = tokens.shape
    head_size = width // HEADS
    qkv_bias = jnp.concatenate([biases[0], jnp.zeros_like(biases[0]), biases[1]])
    projected = low(low_back(matmul(tokens, w_qkv) + qkv_bias))
    query = projected[:, :width].reshape(rows, HEADS, head_size)
    keys = projected[:, width:2 * width].reshape(rows, HEADS, head_size)
    values = projected[:, 2 * width:].reshape(rows, HEADS, head_size)
    visible = jnp.arange(rows) < length
    block = math.gcd(rows, 512)
    pieces = query.reshape(rows // block, block, HEADS, head_size)
    attend = jax.checkpoint(attend_block)
    attended = lax.map(lambda piece: attend(piece, keys, values, visible), pieces).reshape(rows, width)
    branch = low_back(matmul(attended, w_out) + biases[2])
    normed = layer_norm(tokens + branch, gains[0], shifts[0])
    hidden = low_back(matmul(low(normed), w_up) + b_up)
    ffn = low_back(matmul(low(gelu_exact(hidden)), w_down) + biases[3])
    features = layer_norm(normed + ffn, gains[1], shifts[1])
    chars = chars + table[ids]
    char_proj = low_back(matmul(low(chars), w_gru) + b_gru)
    present = groups >= 0
    decay_low, state_low, decay_high, state_high = both_directions(char_proj[None], present[None])
    states = jnp.concatenate([state_low[0], state_high[0]], axis=-1)
    segment = jnp.where(present, groups, rows)
    sums = jax.ops.segment_sum(states, segment, num_segments=rows + 1)[:rows]
    counts = jax.ops.segment_sum(jnp.ones(groups.shape, states.dtype), segment, num_segments=rows + 1)[:rows]
    pooled = sums / counts[:, None]
    joined = low(jnp.concatenate([features, pooled], axis=-1))
    padded = jnp.pad(joined, ((1, 1), (0, 0)))
    mixed = biases[4] + matmul(padded[0:rows], w_conv[0])
    for offset in range(1, w_conv.shape[0]):
        mixed = mixed + matmul(padded[offset:offset + rows], w_conv[offset])
    mixed = low_back(mixed)
    active = gelu_exact(mixed)
    tok_out = low(layer_norm(features + active, gains[2], shifts[2]))
    spread = jnp.concatenate([active, jnp.zeros((1, width), active.dtype)], axis=0)[segment]
    chr_out = low(layer_norm(chars + states + spread, gains[3], shifts[3]))
    return (tok_out, chr_out)

def model(params, tokens, chars, ids, groups, length):
    first = tuple((piece[0] for piece in params))
    second = tuple((piece[1] for piece in params))
    tokens, chars = layer(first, tokens, chars, ids, groups, length)
    return layer(second, tokens, chars, ids, groups, length)

def reference(ends, char_ends, char_ids, groups, lengths, w_qkv, biases, w_out, w_up, b_up, w_down, ln_gain, ln_shift, char_table, w_gru, b_gru, w_conv):
    params = tuple((piece.astype(jnp.float32) for piece in (w_qkv, biases, w_out, w_up, b_up, w_down, ln_gain, ln_shift, char_table, w_gru, b_gru, w_conv)))

    def one_sequence(totals, item):
        tokens, chars, tok_cot, chr_cot, ids, grp, length = item

        def forward(weights, tok_values, chr_values):
            return model(weights, tok_values, chr_values, ids, grp, length)
        outputs, pull = jax.vjp(forward, params, tokens, chars)
        grad_params, grad_tokens, grad_chars = pull((tok_cot, chr_cot))
        totals = jax.tree.map(jnp.add, totals, grad_params)
        return (totals, (outputs[0], outputs[1], grad_tokens, grad_chars))
    zeros = jax.tree.map(jnp.zeros_like, params)
    items = (ends[0].astype(jnp.float32), char_ends[0].astype(jnp.float32), ends[1].astype(jnp.float32), char_ends[1].astype(jnp.float32), char_ids, groups, lengths)
    totals, (tok_out, chr_out, grad_tokens, grad_chars) = lax.scan(one_sequence, zeros, items)
    ends_out = jnp.stack([grad_tokens, tok_out]).astype(jnp.bfloat16)
    char_ends_out = jnp.stack([grad_chars, chr_out]).astype(jnp.bfloat16)
    return (ends_out, char_ends_out, totals[0], totals[1], totals[2], totals[3], totals[4], totals[5], totals[6], totals[7], totals[8], totals[9], totals[10], totals[11])
```

```python
import functools

import jax
import jax.numpy as jnp
from jax import lax
from jax.experimental import pallas as pl
from jax.experimental.pallas import tpu as pltpu
from jax.sharding import PartitionSpec as P

HEADS = 12
CHUNKS = 8
NORM_EPS = 1e-06
MASKED = -1000000000.0
SEC, DP, CTX = "section", "dp", "ctx"
F32, BF16 = jnp.float32, jnp.bfloat16
MIB = 2**20


def contract(left, right, dims):
    return lax.dot_general(left, right, (dims, ((), ())), preferred_element_type=F32)


def mm(left, right):
    return contract(left, right, ((1,), (0,)))


def mt(left, right):
    return contract(left, right, ((1,), (1,)))


def tm(left, right):
    return contract(left, right, ((0,), (0,)))


def flip(value, axis, bit):
    return lax.ppermute(value, axis, [(i, i ^ (1 << bit)) for i in range(lax.axis_size(axis))])


def swap(value):
    return flip(value, SEC, 0)


def turned(value, by):
    count = lax.axis_size(CTX)
    return lax.ppermute(value, CTX, [(i, (i + by) % count) for i in range(count)])


def handed(value, by):
    count = lax.axis_size(CTX)
    return lax.ppermute(value, CTX, [(i, i + by) for i in range(count) if 0 <= i + by < count])


def pick(value, index, axis=0):
    return lax.dynamic_index_in_dim(value, index, axis, keepdims=False)


def interleave(value):
    rows = value.shape[0]
    return jnp.swapaxes(
        value.reshape((CHUNKS, rows // CHUNKS) + value.shape[1:]), 0, 1
    ).reshape(value.shape)


def restore(value):
    rows = value.shape[0]
    return jnp.swapaxes(
        value.reshape((rows // CHUNKS, CHUNKS) + value.shape[1:]), 0, 1
    ).reshape(value.shape)


def norm_parts(values):
    centred = values - jnp.mean(values, axis=-1, keepdims=True)
    scale = lax.rsqrt(jnp.mean(centred * centred, axis=-1, keepdims=True) + NORM_EPS)
    return centred * scale, scale


def layer_norm(values, gain, shift):
    return norm_parts(values)[0] * gain + shift


def norm_back(values, gain, grad):
    unit, scale = norm_parts(values)
    inner = grad * gain
    mean = jnp.mean(inner, axis=-1, keepdims=True)
    along = jnp.mean(inner * unit, axis=-1, keepdims=True)
    return scale * (inner - mean - unit * along), jnp.sum(grad * unit, axis=0), jnp.sum(grad, axis=0)


def gelu(values):
    return jax.nn.gelu(values, approximate=False)


def gelu_slope(values):
    cdf = 0.5 * (1.0 + lax.erf(values * (0.5**0.5)))
    return cdf + values * jnp.exp(-0.5 * values * values) * 0.3989422804014327


def column_sums(values):
    return jnp.sum(values.astype(F32), axis=0)


def params(mib):
    return pltpu.CompilerParams(vmem_limit_bytes=mib * MIB)


def attend_kernel(size, q_ref, k_ref, v_ref, seen_ref, out_ref, lse_ref):
    seen = seen_ref[...] > 0.0
    for head in range(q_ref.shape[1] // size):
        at = slice(head * size, (head + 1) * size)
        scores = mt(k_ref[:, at], q_ref[:, at]) * (size**-0.5)
        scores = jnp.where(seen, scores, MASKED)
        top = jnp.max(scores, axis=0, keepdims=True)
        weights = jnp.exp(scores - top)
        total = jnp.sum(weights, axis=0, keepdims=True)
        probs = (weights * (1.0 / total)).astype(BF16)
        out_ref[:, at] = tm(probs, v_ref[:, at]).astype(BF16)
        lse_ref[0, head : head + 1, :] = top + jnp.log(total)


def attend(query, keys, values, seen):
    rows, width = query.shape
    count = keys.shape[0]
    size = width // HEADS
    block = 2 * size
    steps = width // block
    return pl.pallas_call(
        functools.partial(attend_kernel, size),
        grid=(steps,),
        in_specs=[
            pl.BlockSpec((rows, block), lambda i: (0, i)),
            pl.BlockSpec((count, block), lambda i: (0, i)),
            pl.BlockSpec((count, block), lambda i: (0, i)),
            pl.BlockSpec((count, 1), lambda i: (0, 0)),
        ],
        out_specs=[
            pl.BlockSpec((rows, block), lambda i: (0, i)),
            pl.BlockSpec((1, 8, rows), lambda i: (i, 0, 0)),
        ],
        out_shape=[
            jax.ShapeDtypeStruct((rows, width), BF16),
            jax.ShapeDtypeStruct((steps, 8, rows), F32),
        ],
        compiler_params=params(40),
        cost_estimate=pl.CostEstimate(
            flops=4 * rows * count * width * 2, bytes_accessed=6 * count * width, transcendentals=0
        ),
    )(query, keys, values, seen)


def attend_back_kernel(
    size, q_ref, k_ref, v_ref, seen_ref, lse_ref, do_ref, dq_ref, dk_ref, dv_ref
):
    seen = seen_ref[...] > 0.0
    scale = size**-0.5
    for head in range(q_ref.shape[1] // size):
        at = slice(head * size, (head + 1) * size)
        query, keys, grad = q_ref[:, at], k_ref[:, at], do_ref[:, at]
        scores = jnp.where(seen, mt(keys, query) * scale, MASKED)
        probs = jnp.exp(scores - lse_ref[0, head : head + 1, :])
        g_probs = mt(v_ref[:, at], grad)
        row = jnp.sum(g_probs * probs, axis=0, keepdims=True)
        g_scores = (probs * (g_probs - row)).astype(BF16)
        dv_ref[:, at] = mm(probs.astype(BF16), grad).astype(BF16)
        dk_ref[:, at] = (mm(g_scores, query) * scale).astype(BF16)
        dq_ref[:, at] = (tm(g_scores, keys) * scale).astype(BF16)


def attend_back(query, keys, values, seen, lse, grad):
    rows, width = query.shape
    count = keys.shape[0]
    size = width // HEADS
    block = 2 * size
    steps = width // block
    by_rows = pl.BlockSpec((rows, block), lambda i: (0, i))
    by_keys = pl.BlockSpec((count, block), lambda i: (0, i))
    return pl.pallas_call(
        functools.partial(attend_back_kernel, size),
        grid=(steps,),
        in_specs=[
            by_rows,
            by_keys,
            by_keys,
            pl.BlockSpec((count, 1), lambda i: (0, 0)),
            pl.BlockSpec((1, 8, rows), lambda i: (i, 0, 0)),
            by_rows,
        ],
        out_specs=[by_rows, by_keys, by_keys],
        out_shape=[
            jax.ShapeDtypeStruct((rows, width), BF16),
            jax.ShapeDtypeStruct((count, width), BF16),
            jax.ShapeDtypeStruct((count, width), BF16),
        ],
        compiler_params=params(40),
        cost_estimate=pl.CostEstimate(
            flops=10 * rows * count * width * 2, bytes_accessed=12 * count * width, transcendentals=0
        ),
    )(query, keys, values, seen, lse, grad)


def gate_at(proj_ref, live_ref, at, rate, width):
    live = live_ref[at, :] > 0.0
    opened = jax.nn.sigmoid(proj_ref[at, rate : rate + width])
    return jnp.where(live, 1.0 - opened, 1.0), live, opened


def scan_kernel(proj_ref, live_ref, state_ref, decay_ref, carry_ref, total_ref):
    rows = proj_ref.shape[0]
    width = proj_ref.shape[1] // 4
    steps = rows // CHUNKS
    unroll = 8

    def step(i, carry):
        state_f, decay_f, state_b, decay_b = carry
        for u in range(unroll):
            at = pl.ds(pl.multiple_of((i * unroll + u) * CHUNKS, CHUNKS), CHUNKS)
            keep, live, opened = gate_at(proj_ref, live_ref, at, 0, width)
            inflow = jnp.where(live, opened * proj_ref[at, width : 2 * width], 0.0)
            state_f = keep * state_f + inflow
            decay_f = keep * decay_f
            state_ref[at, 0:width] = state_f
            decay_ref[at, 0:width] = decay_f
            at = pl.ds(pl.multiple_of((steps - 1 - i * unroll - u) * CHUNKS, CHUNKS), CHUNKS)
            keep, live, opened = gate_at(proj_ref, live_ref, at, 2 * width, width)
            inflow = jnp.where(live, opened * proj_ref[at, 3 * width : 4 * width], 0.0)
            state_b = keep * state_b + inflow
            decay_b = keep * decay_b
            state_ref[at, width : 2 * width] = state_b
            decay_ref[at, width : 2 * width] = decay_b
        return state_f, decay_f, state_b, decay_b

    zero = jnp.zeros((CHUNKS, width), F32)
    one = jnp.ones((CHUNKS, width), F32)
    state_f, decay_f, state_b, decay_b = lax.fori_loop(
        0, steps // unroll, step, (zero, one, zero, one)
    )
    join_chunks(carry_ref, total_ref, 0, state_f, decay_f, range(CHUNKS))
    join_chunks(carry_ref, total_ref, 2, state_b, decay_b, range(CHUNKS - 1, -1, -1))


def join_chunks(carry_ref, total_ref, slot, state, decay, order):
    width = state.shape[1]
    before = jnp.zeros((1, width), F32)
    faded = jnp.ones((1, width), F32)
    for chunk in order:
        carry_ref[slot, chunk : chunk + 1, :] = before
        carry_ref[slot + 1, chunk : chunk + 1, :] = faded
        own = decay[chunk : chunk + 1, :]
        before = own * before + state[chunk : chunk + 1, :]
        faded = own * faded
    total_ref[slot : slot + 1, :] = before
    total_ref[slot + 1 : slot + 2, :] = faded
    if slot:
        total_ref[4:8, :] = jnp.zeros((4, width), F32)


def scan_back_kernel(grad_ref, proj_ref, live_ref, state_ref, decay_ref, carry_ref, total_ref):
    rows = proj_ref.shape[0]
    width = proj_ref.shape[1] // 4
    steps = rows // CHUNKS
    unroll = 8

    def step(i, carry):
        state_f, decay_f, state_b, decay_b = carry
        for u in range(unroll):
            at = pl.ds(pl.multiple_of((steps - 1 - i * unroll - u) * CHUNKS, CHUNKS), CHUNKS)
            keep = gate_at(proj_ref, live_ref, at, 0, width)[0]
            whole = grad_ref[at, 0:width] + state_f
            state_ref[at, 0:width] = whole
            decay_ref[at, 0:width] = decay_f
            state_f = keep * whole
            decay_f = keep * decay_f
            at = pl.ds(pl.multiple_of((i * unroll + u) * CHUNKS, CHUNKS), CHUNKS)
            keep = gate_at(proj_ref, live_ref, at, 2 * width, width)[0]
            whole = grad_ref[at, width : 2 * width] + state_b
            state_ref[at, width : 2 * width] = whole
            decay_ref[at, width : 2 * width] = decay_b
            state_b = keep * whole
            decay_b = keep * decay_b
        return state_f, decay_f, state_b, decay_b

    zero = jnp.zeros((CHUNKS, width), F32)
    one = jnp.ones((CHUNKS, width), F32)
    state_f, decay_f, state_b, decay_b = lax.fori_loop(
        0, steps // unroll, step, (zero, one, zero, one)
    )
    join_chunks(carry_ref, total_ref, 0, state_f, decay_f, range(CHUNKS - 1, -1, -1))
    join_chunks(carry_ref, total_ref, 2, state_b, decay_b, range(CHUNKS))


def scan_call(kernel, width, *arrays):
    rows = arrays[0].shape[0]
    return pl.pallas_call(
        kernel,
        out_shape=[
            jax.ShapeDtypeStruct((rows, 2 * width), F32),
            jax.ShapeDtypeStruct((rows, 2 * width), F32),
            jax.ShapeDtypeStruct((4, CHUNKS, width), F32),
            jax.ShapeDtypeStruct((8, width), F32),
        ],
        compiler_params=params(40),
        cost_estimate=pl.CostEstimate(
            flops=rows * width * 200, bytes_accessed=rows * width * 32, transcendentals=0
        ),
    )(*arrays)


def joined_scan(kernel, width, place, arrays, reverse):
    state, decay, carry, total = scan_call(kernel, width, *arrays)
    count = lax.axis_size(CTX)
    others = {j: turned(total, j) for j in range(1, count)}
    zero = jnp.zeros((1, width), F32)
    entering = []
    for slot in (0, 2):
        so_far = zero
        rising = (slot == 0) != reverse
        for hop in range(count - 1, 0, -1):
            there = others[hop] if rising else others[count - hop]
            valid = (place >= hop) if rising else (place + hop < count)
            so_far = jnp.where(
                valid, there[slot + 1 : slot + 2] * so_far + there[slot : slot + 1], so_far
            )
        entering.append(carry[slot] + carry[slot + 1] * so_far)
    entering = jnp.concatenate(entering, axis=1)
    shape = (state.shape[0] // CHUNKS, CHUNKS, 2 * width)
    whole = state.reshape(shape) + decay.reshape(shape) * entering[None]
    return whole.reshape(state.shape), entering


def layer_forward(w, x, chars_in, ids, live, onehot, counts, seen, place):
    rows, width = x.shape
    n_ctx = lax.axis_size(CTX)
    x_all = jnp.concatenate([x] + [turned(x, j) for j in range(1, n_ctx)], axis=0)
    named = (ids[:, None] == jnp.arange(w["table"].shape[0])[None, :]).astype(BF16)
    chars = chars_in.astype(F32) + mm(named, w["table"])
    chars_low = chars.astype(BF16)
    proj = mm(chars_low, w["gru"]) + w["b_gru"]
    half = proj.shape[1] // 4
    states, entering = joined_scan(scan_kernel, half, place, (proj, live), False)
    pooled = mm(onehot, states.astype(BF16)) / counts
    biases, gains, shifts = w["biases"], w["gains"], w["shifts"]
    query = (mm(x, w["qkv"][:, :width]) + biases[0]).astype(BF16)
    keys = mm(x_all, w["qkv"][:, width : 2 * width]).astype(BF16)
    values = (mm(x_all, w["qkv"][:, 2 * width :]) + biases[1]).astype(BF16)
    attended, lse = attend(query, keys, values, seen)
    first = x.astype(F32) + mm(attended, w["out"]) + biases[2]
    normed = layer_norm(first, gains[0], shifts[0])
    normed_low = normed.astype(BF16)
    hidden = mm(normed_low, w["up"]) + w["b_up"]
    active = gelu(hidden).astype(BF16)
    second = normed + mm(active, w["down"]) + biases[3]
    features = layer_norm(second, gains[1], shifts[1])
    joined = jnp.concatenate([features, pooled], axis=1).astype(BF16)
    three = three_taps(joined, 1)
    conv = w["conv"]
    mixed = mm(three, conv.reshape(-1, width)) + biases[4]
    lifted = gelu(mixed)
    tok_sum = features + lifted
    chr_sum = chars + states + tm(onehot, lifted.astype(BF16))
    tok_out = layer_norm(tok_sum, gains[2], shifts[2]).astype(BF16)
    chr_out = layer_norm(chr_sum, gains[3], shifts[3]).astype(BF16)
    saved = dict(
        x=x, x_all=x_all, query=query, keys=keys, values=values, lse=lse, attended=attended,
        first=first, normed_low=normed_low, hidden=hidden, active=active, second=second,
        chars_low=chars_low, proj=proj, states=states, entering=entering, three=three,
        mixed=mixed, tok_sum=tok_sum, chr_sum=chr_sum,
    )
    return tok_out, chr_out, saved


def three_taps(values, step):
    before = handed(values[-1:], 1)
    after = handed(values[:1], -1)
    lower = jnp.concatenate([before, values[:-1]], axis=0)
    upper = jnp.concatenate([values[1:], after], axis=0)
    return jnp.concatenate([lower, values, upper][::step], axis=1)


class Halves:
    def __init__(self, section):
        self.section = section

    def inputs(self, values):
        return jnp.concatenate([values, swap(values)], axis=0)

    def grads(self, values):
        half = values.shape[1] // 2
        sent = lax.dynamic_slice_in_dim(values, (1 - self.section) * half, half, 1)
        kept = lax.dynamic_slice_in_dim(values, self.section * half, half, 1)
        return jnp.concatenate([kept, swap(sent)], axis=0)


def bits_of(axis):
    return [(axis, bit) for bit in range(lax.axis_size(axis).bit_length() - 1)]


def reduce_scattered(pairs, lead, order):
    layout = bits_of(DP)[::-1] + bits_of(CTX)[::-1]
    rows = pairs[0][0].shape[1]

    def split(value, key, axis):
        place = layout.index(key)
        shape = value.shape
        outer = lead * 2**place
        view = value.reshape(shape[:axis] + (outer, 2, shape[axis] // (2 * outer)) + shape[axis + 1 :])
        mine = (lax.axis_index(key[0]) >> key[1]) & 1
        less = shape[:axis] + (shape[axis] // 2,) + shape[axis + 1 :]
        return [pick(view, side, axis + 1).reshape(less) for side in (mine, 1 - mine)]

    total = None
    for count, key in enumerate(order):
        if count == 0:
            kept, sent = [], []
            for left, right in pairs:
                mine, other = split(left, key, 1)
                kept.append(tm(mine, right))
                sent.append(tm(other, right))
            kept, sent = (v[0] if len(v) == 1 else jnp.concatenate(v, axis=1) for v in (kept, sent))
        else:
            kept, sent = split(total, key, 0)
        layout_next = [k for k in layout if k != key]
        total = kept.astype(F32) + flip(sent.astype(BF16), *key).astype(F32)
        if count < len(order) - 1:
            total = total.astype(BF16)
        layout = layout_next
    return total


def layer_backward(w, saved, g_tok, g_chr, ids, ids_other, live, onehot, counts, seen, place, halves):
    g_tok, g_chr = g_tok.astype(F32), g_chr.astype(F32)
    rows, width = g_tok.shape
    gains = w["gains"]
    n_ctx = lax.axis_size(CTX)
    x_first = bits_of(DP) + bits_of(CTX)
    y_first = bits_of(DP)[::-1] + bits_of(CTX)
    made = {}
    d_tok, gain3, shift3 = norm_back(saved["tok_sum"], gains[2], g_tok)
    d_chr, gain4, shift4 = norm_back(saved["chr_sum"], gains[3], g_chr)
    d_lifted = d_tok + mm(onehot, d_chr.astype(BF16))
    d_mixed = (d_lifted * gelu_slope(saved["mixed"])).astype(BF16)
    made["conv"] = reduce_scattered(
        [(halves.inputs(saved["three"]), halves.grads(d_mixed))], w["conv"].shape[0], x_first
    )
    around = three_taps(d_mixed, -1)
    conv = w["conv"]
    d_joined = mt(around[:, :width], conv[0])
    for tap in range(1, conv.shape[0]):
        d_joined = d_joined + mt(around[:, tap * width : (tap + 1) * width], conv[tap])
    d_feat = d_tok + d_joined[:, :width]
    d_second, gain2, shift2 = norm_back(saved["second"], gains[1], d_feat)
    d_ffn = d_second.astype(BF16)
    made["down"] = reduce_scattered([(halves.inputs(saved["active"]), halves.grads(d_ffn))], 1, y_first)
    d_hidden = (mt(d_ffn, w["down"]) * gelu_slope(saved["hidden"])).astype(BF16)
    made["up"] = reduce_scattered(
        [(halves.inputs(saved["normed_low"]), halves.grads(d_hidden))], 1, x_first
    )
    d_normed = d_second + mt(d_hidden, w["up"])
    d_first, gain1, shift1 = norm_back(saved["first"], gains[0], d_normed)
    d_branch = d_first.astype(BF16)
    made["out"] = reduce_scattered(
        [(halves.inputs(saved["attended"]), halves.grads(d_branch))], 1, y_first
    )
    d_attended = mt(d_branch, w["out"]).astype(BF16)
    dq, dk, dv = attend_back(
        saved["query"], saved["keys"], saved["values"], seen, saved["lse"], d_attended
    )
    wide = halves.inputs(saved["x_all"])
    made["qkv"] = reduce_scattered(
        [
            (halves.inputs(saved["x"]), halves.grads(dq)),
            (wide, halves.grads(dk)),
            (wide, halves.grads(dv)),
        ],
        1,
        y_first,
    )
    qkv = w["qkv"]
    parts = mt(dk, qkv[:, width : 2 * width]) + mt(dv, qkv[:, 2 * width :])
    d_x = d_first + mt(dq, qkv[:, :width]) + parts[:rows]
    for j in range(1, n_ctx):
        d_x = d_x + turned(parts[j * rows : (j + 1) * rows].astype(BF16), n_ctx - j).astype(F32)
    d_pool = (d_joined[:, width:] / counts).astype(BF16)
    d_states = d_chr + tm(onehot, d_pool)
    proj, states, entering = saved["proj"], saved["states"], saved["entering"]
    half = proj.shape[1] // 4
    whole, _ = joined_scan(scan_back_kernel, half, place, (d_states, proj, live), True)
    pieces = []
    for side in (0, 1):
        at = slice(side * half, (side + 1) * half)
        if side == 0:
            before = jnp.concatenate([entering[:, at], states[:-CHUNKS, at]], axis=0)
        else:
            before = jnp.concatenate([states[CHUNKS:, at], entering[:, at]], axis=0)
        opened = jax.nn.sigmoid(proj[:, 2 * side * half : (2 * side + 1) * half])
        target = proj[:, (2 * side + 1) * half : (2 * side + 2) * half]
        flow = jnp.where(live > 0.0, whole[:, at] * opened, 0.0)
        pieces += [flow * (1.0 - opened) * (target - before), flow]
    d_proj = jnp.concatenate(pieces, axis=1).astype(BF16)
    made["gru"] = reduce_scattered(
        [(halves.inputs(saved["chars_low"]), halves.grads(d_proj))], 1, y_first
    )
    d_c = (d_chr + mt(d_proj, w["gru"])).astype(BF16)
    vocab = -(-w["table"].shape[0] // 256) * 256
    names = jnp.concatenate([ids, ids_other])[:, None] - halves.section * (vocab // 2)
    named = (names == jnp.arange(vocab // 2)[None, :]).astype(BF16)
    made["table"] = reduce_scattered([(halves.inputs(d_c), named)], 1, x_first)
    small = (
        jnp.stack(
            [column_sums(dq), column_sums(dv), column_sums(d_branch), column_sums(d_ffn), column_sums(d_mixed)]
        ),
        column_sums(d_hidden)[None],
        jnp.stack([gain1, gain2, gain3, gain4]),
        jnp.stack([shift1, shift2, shift3, shift4]),
        column_sums(d_proj)[None],
    )
    return d_x.astype(BF16), d_c, made, small


def on_device(
    ends, char_ends, char_ids, groups, lengths, w_qkv, biases, w_out, w_up, b_up, w_down,
    ln_gain, ln_shift, char_table, w_gru, b_gru, w_conv,
):
    section, place = lax.axis_index(SEC), lax.axis_index(CTX)
    n_dp, n_ctx = lax.axis_size(DP), lax.axis_size(CTX)
    is_first = section == 0
    names = ("gru", "table", "qkv", "out", "up", "down", "conv", "biases", "b_up", "gains", "shifts", "b_gru")
    local = (w_gru, char_table, w_qkv, w_out, w_up, w_down, w_conv, biases, b_up, ln_gain, ln_shift, b_gru)
    chars_here = jax.vmap(interleave)(char_ends[0])

    def dealt(pair):
        kept = pick(pair, section)
        got = swap(pick(pair, 1 - section))
        return jnp.where(is_first, kept, got), jnp.where(is_first, got, kept)

    x, cot_tok = dealt(ends[0])
    c, cot_chr = dealt(chars_here)
    layers = ({}, {})
    for name, value in zip(names, local):
        own = value[0]
        other = swap(own)
        layers[0][name] = jnp.where(is_first, own, other)
        layers[1][name] = jnp.where(is_first, other, own)
    rows = x.shape[0]
    ids = interleave(pick(char_ids, section))
    ids_other = interleave(pick(char_ids, 1 - section))
    group = interleave(pick(groups, section))
    live = (group >= 0).astype(F32)[:, None]
    onehot = jnp.arange(rows)[:, None] == (group - place * rows)[None, :]
    counts = jnp.sum(onehot.astype(F32), axis=1, keepdims=True)
    onehot = onehot.astype(BF16)
    shard = jnp.mod(place - jnp.arange(n_ctx), n_ctx)
    spots = (shard[:, None] * rows + jnp.arange(rows)[None, :]).reshape(-1, 1)
    seen = (spots < pick(lengths, section)).astype(F32)

    kept = []
    for layer in (0, 1):
        x, c, saved = layer_forward(layers[layer], x, c, ids, live, onehot, counts, seen, place)
        kept.append(saved)
    g_x, g_c = cot_tok, cot_chr
    halves = Halves(section)
    made, small = [None, None], [None, None]
    for layer in (1, 0):
        g_x, g_c, made[layer], small[layer] = layer_backward(
            layers[layer], kept[layer], g_x, g_c, ids, ids_other, live, onehot, counts, seen, place, halves
        )

    def gathered(grad, value):
        got = swap(jnp.where(is_first, value, grad))
        return jnp.where(is_first, jnp.stack([grad, got]), jnp.stack([got, value]))[None]

    ends_out = gathered(g_x, x)
    char_ends_out = gathered(restore(g_c), restore(c))

    whole = {}
    for name in made[0]:
        mine = jnp.where(is_first, made[0][name], made[1][name])
        got = swap(jnp.where(is_first, made[1][name], made[0][name]))
        whole[name] = (jnp.where(is_first, mine, got), jnp.where(is_first, got, mine))

    def sided(name):
        return jnp.concatenate(whole[name], axis=1)

    d_qkv = jnp.concatenate(
        [
            half[:, part * half.shape[1] // 3 : (part + 1) * half.shape[1] // 3]
            for part in range(3)
            for half in whole["qkv"]
        ],
        axis=1,
    )
    d_conv = sided("conv")
    d_conv = d_conv.reshape(w_conv.shape[1], -1, d_conv.shape[1])
    d_table = sided("table")[:, : char_table.shape[1]].T

    devices = n_dp * n_ctx

    def by_device(parts):
        return jnp.concatenate(
            [jnp.swapaxes(p.reshape(p.shape[0], devices, -1), 0, 1).reshape(devices, -1) for p in parts],
            axis=1,
        )

    packed = [by_device(parts) for parts in small]
    total = jnp.where(is_first, packed[0], packed[1]) + swap(jnp.where(is_first, packed[1], packed[0]))
    for key in bits_of(DP)[::-1] + bits_of(CTX)[::-1]:
        view = total.reshape(2, -1, total.shape[1])
        mine = (lax.axis_index(key[0]) >> key[1]) & 1
        total = pick(view, mine) + flip(pick(view, 1 - mine), *key)
    sums, at = [], 0
    for parts in small[0]:
        size = parts.size // devices
        sums.append(total[0, at : at + size].reshape(parts.shape[0], -1))
        at += size
    return (
        ends_out,
        char_ends_out,
        d_qkv[None],
        sums[0][None],
        sided("out")[None],
        sided("up")[None],
        sums[1],
        sided("down")[None],
        sums[2][None],
        sums[3][None],
        d_table[None],
        sided("gru")[None],
        sums[4],
        d_conv[None],
    )


def solution(mesh):
    both = (DP, CTX)
    held, rows, columns = P(SEC, DP, CTX), P(SEC, both), P(SEC, None, both)
    layer = P(SEC)
    in_specs = (held, held, P(DP, CTX), P(DP, CTX), P(DP)) + (layer,) * 12
    out_specs = (
        held, held, rows, columns, rows, rows, rows, rows, columns, columns, columns, rows, rows, columns,
    )
    return jax.shard_map(
        on_device, mesh=mesh, in_specs=in_specs, out_specs=out_specs, check_vma=False
    )
```

```python
import functools

import jax
import jax.numpy as jnp
from jax import lax
from jax.experimental import pallas as pl
from jax.experimental.pallas import tpu as pltpu
from jax.sharding import PartitionSpec as P

HEADS = 12
CHUNKS = 8
NORM_EPS = 1e-06
MASKED = -1000000000.0
SEC, DP, CTX = "section", "dp", "ctx"
F32, BF16 = jnp.float32, jnp.bfloat16
MIB = 2**20


def contract(left, right, dims):
    return lax.dot_general(left, right, (dims, ((), ())), preferred_element_type=F32)


def mm(left, right):
    return contract(left, right, ((1,), (0,)))


def mt(left, right):
    return contract(left, right, ((1,), (1,)))


def tm(left, right):
    return contract(left, right, ((0,), (0,)))


def flip(value, axis, bit):
    return lax.ppermute(value, axis, [(i, i ^ (1 << bit)) for i in range(lax.axis_size(axis))])


def swap(value):
    return flip(value, SEC, 0)


def turned(value, by):
    count = lax.axis_size(CTX)
    return lax.ppermute(value, CTX, [(i, (i + by) % count) for i in range(count)])


def handed(value, by):
    count = lax.axis_size(CTX)
    return lax.ppermute(value, CTX, [(i, i + by) for i in range(count) if 0 <= i + by < count])


def pick(value, index, axis=0):
    return lax.dynamic_index_in_dim(value, index, axis, keepdims=False)


def interleave(value):
    rows = value.shape[0]
    return jnp.swapaxes(
        value.reshape((CHUNKS, rows // CHUNKS) + value.shape[1:]), 0, 1
    ).reshape(value.shape)


def restore(value):
    rows = value.shape[0]
    return jnp.swapaxes(
        value.reshape((rows // CHUNKS, CHUNKS) + value.shape[1:]), 0, 1
    ).reshape(value.shape)


def norm_parts(values):
    centred = values - jnp.mean(values, axis=-1, keepdims=True)
    scale = lax.rsqrt(jnp.mean(centred * centred, axis=-1, keepdims=True) + NORM_EPS)
    return centred * scale, scale


def layer_norm(values, gain, shift):
    return norm_parts(values)[0] * gain + shift


def norm_back(values, gain, grad):
    unit, scale = norm_parts(values)
    inner = grad * gain
    mean = jnp.mean(inner, axis=-1, keepdims=True)
    along = jnp.mean(inner * unit, axis=-1, keepdims=True)
    return scale * (inner - mean - unit * along), jnp.sum(grad * unit, axis=0), jnp.sum(grad, axis=0)


def gelu(values):
    return jax.nn.gelu(values, approximate=False)


def gelu_slope(values):
    cdf = 0.5 * (1.0 + lax.erf(values * (0.5**0.5)))
    return cdf + values * jnp.exp(-0.5 * values * values) * 0.3989422804014327


def column_sums(values):
    return jnp.sum(values.astype(F32), axis=0)


def params(mib):
    return pltpu.CompilerParams(vmem_limit_bytes=mib * MIB)


def attend_kernel(size, q_ref, k_ref, v_ref, seen_ref, out_ref, lse_ref):
    seen = seen_ref[...] > 0.0
    for head in range(q_ref.shape[1] // size):
        at = slice(head * size, (head + 1) * size)
        scores = mt(k_ref[:, at], q_ref[:, at]) * (size**-0.5)
        scores = jnp.where(seen, scores, MASKED)
        top = jnp.max(scores, axis=0, keepdims=True)
        weights = jnp.exp(scores - top)
        total = jnp.sum(weights, axis=0, keepdims=True)
        probs = (weights * (1.0 / total)).astype(BF16)
        out_ref[:, at] = tm(probs, v_ref[:, at]).astype(BF16)
        lse_ref[0, head : head + 1, :] = top + jnp.log(total)


def attend(query, keys, values, seen):
    rows, width = query.shape
    count = keys.shape[0]
    size = width // HEADS
    block = 2 * size
    steps = width // block
    return pl.pallas_call(
        functools.partial(attend_kernel, size),
        grid=(steps,),
        in_specs=[
            pl.BlockSpec((rows, block), lambda i: (0, i)),
            pl.BlockSpec((count, block), lambda i: (0, i)),
            pl.BlockSpec((count, block), lambda i: (0, i)),
            pl.BlockSpec((count, 1), lambda i: (0, 0)),
        ],
        out_specs=[
            pl.BlockSpec((rows, block), lambda i: (0, i)),
            pl.BlockSpec((1, 8, rows), lambda i: (i, 0, 0)),
        ],
        out_shape=[
            jax.ShapeDtypeStruct((rows, width), BF16),
            jax.ShapeDtypeStruct((steps, 8, rows), F32),
        ],
        compiler_params=params(40),
        cost_estimate=pl.CostEstimate(
            flops=4 * rows * count * width * 2, bytes_accessed=6 * count * width, transcendentals=0
        ),
    )(query, keys, values, seen)


def attend_back_kernel(
    size, q_ref, k_ref, v_ref, seen_ref, lse_ref, do_ref, dq_ref, dk_ref, dv_ref
):
    seen = seen_ref[...] > 0.0
    scale = size**-0.5
    for head in range(q_ref.shape[1] // size):
        at = slice(head * size, (head + 1) * size)
        query, keys, grad = q_ref[:, at], k_ref[:, at], do_ref[:, at]
        scores = jnp.where(seen, mt(keys, query) * scale, MASKED)
        probs = jnp.exp(scores - lse_ref[0, head : head + 1, :])
        g_probs = mt(v_ref[:, at], grad)
        row = jnp.sum(g_probs * probs, axis=0, keepdims=True)
        g_scores = (probs * (g_probs - row)).astype(BF16)
        dv_ref[:, at] = mm(probs.astype(BF16), grad).astype(BF16)
        dk_ref[:, at] = (mm(g_scores, query) * scale).astype(BF16)
        dq_ref[:, at] = (tm(g_scores, keys) * scale).astype(BF16)


def attend_back(query, keys, values, seen, lse, grad):
    rows, width = query.shape
    count = keys.shape[0]
    size = width // HEADS
    block = 2 * size
    steps = width // block
    by_rows = pl.BlockSpec((rows, block), lambda i: (0, i))
    by_keys = pl.BlockSpec((count, block), lambda i: (0, i))
    return pl.pallas_call(
        functools.partial(attend_back_kernel, size),
        grid=(steps,),
        in_specs=[
            by_rows,
            by_keys,
            by_keys,
            pl.BlockSpec((count, 1), lambda i: (0, 0)),
            pl.BlockSpec((1, 8, rows), lambda i: (i, 0, 0)),
            by_rows,
        ],
        out_specs=[by_rows, by_keys, by_keys],
        out_shape=[
            jax.ShapeDtypeStruct((rows, width), BF16),
            jax.ShapeDtypeStruct((count, width), BF16),
            jax.ShapeDtypeStruct((count, width), BF16),
        ],
        compiler_params=params(40),
        cost_estimate=pl.CostEstimate(
            flops=10 * rows * count * width * 2, bytes_accessed=12 * count * width, transcendentals=0
        ),
    )(query, keys, values, seen, lse, grad)


def gate_at(proj_ref, live_ref, at, rate, width):
    live = live_ref[at, :] > 0.0
    opened = jax.nn.sigmoid(proj_ref[at, rate : rate + width])
    return jnp.where(live, 1.0 - opened, 1.0), live, opened


def scan_kernel(proj_ref, live_ref, state_ref, decay_ref, carry_ref, total_ref):
    rows = proj_ref.shape[0]
    width = proj_ref.shape[1] // 4
    steps = rows // CHUNKS
    unroll = 8

    def step(i, carry):
        state_f, decay_f, state_b, decay_b = carry
        for u in range(unroll):
            at = pl.ds(pl.multiple_of((i * unroll + u) * CHUNKS, CHUNKS), CHUNKS)
            keep, live, opened = gate_at(proj_ref, live_ref, at, 0, width)
            inflow = jnp.where(live, opened * proj_ref[at, width : 2 * width], 0.0)
            state_f = keep * state_f + inflow
            decay_f = keep * decay_f
            state_ref[at, 0:width] = state_f
            decay_ref[at, 0:width] = decay_f
            at = pl.ds(pl.multiple_of((steps - 1 - i * unroll - u) * CHUNKS, CHUNKS), CHUNKS)
            keep, live, opened = gate_at(proj_ref, live_ref, at, 2 * width, width)
            inflow = jnp.where(live, opened * proj_ref[at, 3 * width : 4 * width], 0.0)
            state_b = keep * state_b + inflow
            decay_b = keep * decay_b
            state_ref[at, width : 2 * width] = state_b
            decay_ref[at, width : 2 * width] = decay_b
        return state_f, decay_f, state_b, decay_b

    zero = jnp.zeros((CHUNKS, width), F32)
    one = jnp.ones((CHUNKS, width), F32)
    state_f, decay_f, state_b, decay_b = lax.fori_loop(
        0, steps // unroll, step, (zero, one, zero, one)
    )
    join_chunks(carry_ref, total_ref, 0, state_f, decay_f, range(CHUNKS))
    join_chunks(carry_ref, total_ref, 2, state_b, decay_b, range(CHUNKS - 1, -1, -1))


def join_chunks(carry_ref, total_ref, slot, state, decay, order):
    width = state.shape[1]
    before = jnp.zeros((1, width), F32)
    faded = jnp.ones((1, width), F32)
    for chunk in order:
        carry_ref[slot, chunk : chunk + 1, :] = before
        carry_ref[slot + 1, chunk : chunk + 1, :] = faded
        own = decay[chunk : chunk + 1, :]
        before = own * before + state[chunk : chunk + 1, :]
        faded = own * faded
    total_ref[slot : slot + 1, :] = before
    total_ref[slot + 1 : slot + 2, :] = faded
    if slot:
        total_ref[4:8, :] = jnp.zeros((4, width), F32)


def scan_back_kernel(grad_ref, proj_ref, live_ref, state_ref, decay_ref, carry_ref, total_ref):
    rows = proj_ref.shape[0]
    width = proj_ref.shape[1] // 4
    steps = rows // CHUNKS
    unroll = 8

    def step(i, carry):
        state_f, decay_f, state_b, decay_b = carry
        for u in range(unroll):
            at = pl.ds(pl.multiple_of((steps - 1 - i * unroll - u) * CHUNKS, CHUNKS), CHUNKS)
            keep = gate_at(proj_ref, live_ref, at, 0, width)[0]
            whole = grad_ref[at, 0:width] + state_f
            state_ref[at, 0:width] = whole
            decay_ref[at, 0:width] = decay_f
            state_f = keep * whole
            decay_f = keep * decay_f
            at = pl.ds(pl.multiple_of((i * unroll + u) * CHUNKS, CHUNKS), CHUNKS)
            keep = gate_at(proj_ref, live_ref, at, 2 * width, width)[0]
            whole = grad_ref[at, width : 2 * width] + state_b
            state_ref[at, width : 2 * width] = whole
            decay_ref[at, width : 2 * width] = decay_b
            state_b = keep * whole
            decay_b = keep * decay_b
        return state_f, decay_f, state_b, decay_b

    zero = jnp.zeros((CHUNKS, width), F32)
    one = jnp.ones((CHUNKS, width), F32)
    state_f, decay_f, state_b, decay_b = lax.fori_loop(
        0, steps // unroll, step, (zero, one, zero, one)
    )
    join_chunks(carry_ref, total_ref, 0, state_f, decay_f, range(CHUNKS - 1, -1, -1))
    join_chunks(carry_ref, total_ref, 2, state_b, decay_b, range(CHUNKS))


def scan_call(kernel, width, *arrays):
    rows = arrays[0].shape[0]
    return pl.pallas_call(
        kernel,
        out_shape=[
            jax.ShapeDtypeStruct((rows, 2 * width), F32),
            jax.ShapeDtypeStruct((rows, 2 * width), F32),
            jax.ShapeDtypeStruct((4, CHUNKS, width), F32),
            jax.ShapeDtypeStruct((8, width), F32),
        ],
        compiler_params=params(40),
        cost_estimate=pl.CostEstimate(
            flops=rows * width * 200, bytes_accessed=rows * width * 32, transcendentals=0
        ),
    )(*arrays)


def joined_scan(kernel, width, place, arrays, reverse):
    state, decay, carry, total = scan_call(kernel, width, *arrays)
    count = lax.axis_size(CTX)
    others = {j: turned(total, j) for j in range(1, count)}
    zero = jnp.zeros((1, width), F32)
    entering = []
    for slot in (0, 2):
        so_far = zero
        rising = (slot == 0) != reverse
        for hop in range(count - 1, 0, -1):
            there = others[hop] if rising else others[count - hop]
            valid = (place >= hop) if rising else (place + hop < count)
            so_far = jnp.where(
                valid, there[slot + 1 : slot + 2] * so_far + there[slot : slot + 1], so_far
            )
        entering.append(carry[slot] + carry[slot + 1] * so_far)
    entering = jnp.concatenate(entering, axis=1)
    shape = (state.shape[0] // CHUNKS, CHUNKS, 2 * width)
    whole = state.reshape(shape) + decay.reshape(shape) * entering[None]
    return whole.reshape(state.shape), entering


def layer_forward(w, x, chars_in, ids, live, onehot, counts, seen, place):
    rows, width = x.shape
    n_ctx = lax.axis_size(CTX)
    x_all = jnp.concatenate([x] + [turned(x, j) for j in range(1, n_ctx)], axis=0)
    named = (ids[:, None] == jnp.arange(w["table"].shape[0])[None, :]).astype(BF16)
    chars = chars_in.astype(F32) + mm(named, w["table"])
    chars_low = chars.astype(BF16)
    proj = mm(chars_low, w["gru"]) + w["b_gru"]
    half = proj.shape[1] // 4
    states, entering = joined_scan(scan_kernel, half, place, (proj, live), False)
    pooled = mm(onehot, states.astype(BF16)) / counts
    biases, gains, shifts = w["biases"], w["gains"], w["shifts"]
    query = (mm(x, w["qkv"][:, :width]) + biases[0]).astype(BF16)
    keys = mm(x_all, w["qkv"][:, width : 2 * width]).astype(BF16)
    values = (mm(x_all, w["qkv"][:, 2 * width :]) + biases[1]).astype(BF16)
    attended, lse = attend(query, keys, values, seen)
    first = x.astype(F32) + mm(attended, w["out"]) + biases[2]
    normed = layer_norm(first, gains[0], shifts[0])
    normed_low = normed.astype(BF16)
    hidden = mm(normed_low, w["up"]) + w["b_up"]
    active = gelu(hidden).astype(BF16)
    second = normed + mm(active, w["down"]) + biases[3]
    features = layer_norm(second, gains[1], shifts[1])
    joined = jnp.concatenate([features, pooled], axis=1).astype(BF16)
    three = three_taps(joined, 1)
    mixed = mm(three, w["conv"]) + biases[4]
    lifted = gelu(mixed)
    tok_sum = features + lifted
    chr_sum = chars + states + tm(onehot, lifted.astype(BF16))
    tok_out = layer_norm(tok_sum, gains[2], shifts[2]).astype(BF16)
    chr_out = layer_norm(chr_sum, gains[3], shifts[3]).astype(BF16)
    saved = dict(
        x=x, x_all=x_all, query=query, keys=keys, values=values, lse=lse, attended=attended,
        first=first, normed_low=normed_low, hidden=hidden, active=active, second=second,
        chars_low=chars_low, proj=proj, states=states, entering=entering, joined=joined,
        mixed=mixed, tok_sum=tok_sum, chr_sum=chr_sum,
    )
    return tok_out, chr_out, saved


def three_taps(values, step):
    before = handed(values[-1:], 1)
    after = handed(values[:1], -1)
    lower = jnp.concatenate([before, values[:-1]], axis=0)
    upper = jnp.concatenate([values[1:], after], axis=0)
    return jnp.concatenate([lower, values, upper][::step], axis=1)


def bits_of(axis):
    return [(axis, bit) for bit in range(lax.axis_size(axis).bit_length() - 1)]


def exchange_order(x_first):
    dp = bits_of(DP)
    return (dp if x_first else dp[::-1]) + bits_of(CTX)


def shard_at(place, order, n_ctx):
    index = {DP: lax.axis_index(DP), CTX: lax.axis_index(CTX)}
    shard = index[DP] * n_ctx + index[CTX]
    for nth, (axis, bit) in enumerate(order):
        if (place >> (len(order) - 1 - nth)) & 1:
            mine = (index[axis] // (1 << bit)) % 2
            shard = shard + (1 - 2 * mine) * ((1 << bit) * (n_ctx if axis == DP else 1))
    return shard


class Packing:
    def __init__(self, section, unit, x_first):
        self.section, self.unit, self.x_first = section, unit, x_first
        self.arrays, self.moves, self.jobs, self.rows = [], [], [], 0

    def operand(self, value, pieces=None):
        width = value.shape[1]
        self.arrays.append(value)
        self.moves.append([(0, 0, width)] if pieces is None else [(b, h, h) for b, h in pieces])
        return len(self.arrays) - 1

    def local(self, *values):
        self.arrays.extend(values)
        self.moves.extend([None] * len(values))
        return len(self.arrays) - len(values)

    def product(self, left, right, begin, half, there, size):
        self.jobs.append(
            dict(left=left, right=right, begin=begin, half=half, there=there, rows=size, row=self.rows)
        )
        self.rows += size

    def plain(self, value, size):
        self.jobs.append(dict(left=None, plain=self.local(value), rows=size, row=self.rows))
        self.rows += size

    def run(self, collective_id):
        order = exchange_order(self.x_first)
        n_ctx = lax.axis_size(CTX)
        count = lax.axis_size(DP) * n_ctx
        unit, section = self.unit, self.section
        if any(job["rows"] % 16 for job in self.jobs):
            return self.run_plainly(order, n_ctx, count)
        vmem = pl.BlockSpec(memory_space=pltpu.VMEM)
        half = jax.ShapeDtypeStruct((count // 2, self.rows, unit), BF16)
        most = max(job["rows"] for job in self.jobs) * count
        coming = [
            pltpu.VMEM((a.shape[0], sum(piece[2] for piece in move)), a.dtype)
            for a, move in zip(self.arrays, self.moves)
            if move
        ]
        copies = sum(len(move) for move in self.moves if move)
        semaphores = [pltpu.SemaphoreType.DMA((copies,))] * 2
        return pl.pallas_call(
            functools.partial(pack_kernel, self.jobs, self.moves, count, order, n_ctx),
            in_specs=[vmem] * len(self.arrays),
            out_specs=[vmem, vmem],
            out_shape=[half, half],
            scratch_shapes=[pltpu.VMEM((2, most, unit), BF16), coming, semaphores],
            compiler_params=pltpu.CompilerParams(
                vmem_limit_bytes=56 * MIB, collective_id=collective_id, has_side_effects=True
            ),
            cost_estimate=pl.CostEstimate(
                flops=count * self.rows * unit * 1024,
                bytes_accessed=count * self.rows * unit * 4,
                transcendentals=0,
            ),
        )(*self.arrays)

    def run_plainly(self, order, n_ctx, count):
        blocks = []
        for job in self.jobs:
            if job["left"] is None:
                value = self.arrays[job["plain"]]
            else:
                left, right = job["left"], job["right"]
                pairs = []
                for core in (0, 1):
                    owner = jnp.where(core == 0, self.section, 1 - self.section)
                    one = self.other(left, owner) if core else self.arrays[left]
                    if self.moves[right] is None:
                        two = lax.slice_in_dim(
                            self.arrays[right + core], job["begin"], job["begin"] + self.unit, axis=1
                        )
                    else:
                        two = self.other(right, owner) if core else self.arrays[right]
                        column = job["begin"] + self.section * job["half"]
                        two = lax.dynamic_slice_in_dim(two, column, self.unit, 1)
                    pairs.append(tm(one, two))
                value = (pairs[0] + pairs[1]).astype(BF16)
            blocks.append(value.reshape(count, job["rows"], self.unit))
        shards = jnp.stack([shard_at(place, order, n_ctx) for place in range(count)])
        whole = jnp.take(jnp.concatenate(blocks, axis=1), shards, axis=0)
        return whole[count // 2 :], whole[: count // 2]

    def other(self, index, owner):
        return swap(self.arrays[index])


def pack_kernel(jobs, moves, count, order, n_ctx, *refs):
    arrays, (sent_ref, kept_ref, scratch, coming, semaphores) = refs[: len(moves)], refs[len(moves) :]
    send_sems, recv_sems = semaphores
    section = lax.axis_index(SEC)
    unit = kept_ref.shape[2]
    barrier = pltpu.get_barrier_semaphore()
    pl.semaphore_signal(
        barrier, inc=1, device_id={SEC: 1 - section}, device_id_type=pl.DeviceIdType.MESH
    )
    pl.semaphore_wait(barrier, 1)
    places, copies, pending, nth, slot = {}, [], {}, 0, 0
    for index, move in enumerate(moves):
        if not move:
            continue
        target, at = coming[slot], 0
        places[index] = target
        pending[index] = []
        slot += 1
        for begin, half, width in move:
            if half:
                source = arrays[index].at[:, pl.ds(pl.multiple_of(begin + (1 - section) * half, 128), width)]
            else:
                source = arrays[index]
            copy = pltpu.make_async_remote_copy(
                src_ref=source,
                dst_ref=target.at[:, at : at + width] if half else target,
                send_sem=send_sems.at[nth],
                recv_sem=recv_sems.at[nth],
                device_id={SEC: 1 - section},
                device_id_type=pl.DeviceIdType.MESH,
            )
            copy.start()
            copies.append(copy)
            pending[index].append(copy)
            at += width
            nth += 1
    for turn, job in enumerate(jobs):
        at, size = job["row"], job["rows"]
        held = scratch.at[turn % 2]
        if job["left"] is None:
            held[0 : count * size, :] = arrays[job["plain"]][...]
        else:
            left, right = job["left"], job["right"]
            for index in (left, right):
                for copy in pending.pop(index, ()):
                    copy.wait_recv()
            if moves[right]:
                column = pl.multiple_of(job["begin"] + section * job["half"], 128)
                mine = arrays[right].at[:, pl.ds(column, unit)]
                theirs = places[right].at[:, job["there"] : job["there"] + unit]
            else:
                mine, theirs = (
                    arrays[right + core].at[:, job["begin"] : job["begin"] + unit] for core in (0, 1)
                )
            for begin in range(0, count * size, 768):
                span = slice(begin, begin + 768)
                value = tm(arrays[left][:, span], mine[...]) + tm(places[left][:, span], theirs[...])
                held[span, :] = value.astype(BF16)
        for place in range(count):
            begin = pl.multiple_of(shard_at(place, order, n_ctx) * size, 16)
            target = kept_ref if place < count // 2 else sent_ref
            target[place % (count // 2), at : at + size, :] = held[pl.ds(begin, size), :]
    for copy in copies:
        copy.wait_send()


class Halving:
    def __init__(self, packed, x_first):
        self.sent, self.kept = packed
        self.order = exchange_order(x_first)
        self.total = None

    def step(self, after):
        key, self.order = self.order[0], self.order[1:]
        got = flip(self.sent, *key)
        got, kept, after = lax.optimization_barrier((got, self.kept, after))
        if not self.order:
            self.total = kept[0].astype(F32) + got[0].astype(F32)
            self.total, after = lax.optimization_barrier((self.total, after))
            return after
        cut = kept.shape[0] // 2
        sent = (kept[cut:].astype(F32) + got[cut:].astype(F32)).astype(BF16)
        kept = (kept[:cut].astype(F32) + got[:cut].astype(F32)).astype(BF16)
        self.sent, self.kept, after = lax.optimization_barrier((sent, kept, after))
        return after


def finish(steps):
    after = jnp.zeros((), F32)
    for chain in steps:
        if chain.order:
            after = chain.step(after)


def layer_backward(w, saved, g_tok, g_chr, ids, ids_other, live, onehot, counts, seen, place, section, earlier):
    g_tok, g_chr = g_tok.astype(F32), g_chr.astype(F32)
    rows, width = g_tok.shape
    gains = w["gains"]
    n_ctx = lax.axis_size(CTX)
    count = lax.axis_size(DP) * n_ctx
    unit = width // 2
    block = width // count
    d_tok, gain3, shift3 = norm_back(saved["tok_sum"], gains[2], g_tok)
    d_chr, gain4, shift4 = norm_back(saved["chr_sum"], gains[3], g_chr)
    d_lifted = d_tok + mm(onehot, d_chr.astype(BF16))
    d_mixed = (d_lifted * gelu_slope(saved["mixed"])).astype(BF16)
    around = three_taps(d_mixed, -1)
    conv = w["conv"].reshape(-1, 2 * width, width)
    d_joined = mt(around[:, :width], conv[0])
    for tap in range(1, conv.shape[0]):
        d_joined = d_joined + mt(around[:, tap * width : (tap + 1) * width], conv[tap])
    d_feat = d_tok + d_joined[:, :width]
    d_second, gain2, shift2 = norm_back(saved["second"], gains[1], d_feat)
    d_ffn = d_second.astype(BF16)
    d_hidden = (mt(d_ffn, w["down"]) * gelu_slope(saved["hidden"])).astype(BF16)
    if earlier:
        d_hidden = earlier[0].step(d_hidden)
    d_normed = d_second + mt(d_hidden, w["up"])
    d_first, gain1, shift1 = norm_back(saved["first"], gains[0], d_normed)
    d_branch = d_first.astype(BF16)
    group = Packing(section, unit, True)
    taps = conv.shape[0]
    left, right = group.operand(saved["joined"]), group.operand(around, [(t * width, unit) for t in range(taps)])
    for tap in range(taps):
        group.product(left, right, tap * width, unit, tap * unit, 2 * block)
    ups = d_hidden.shape[1] // 2
    left, right = group.operand(saved["normed_low"]), group.operand(d_hidden, [(0, ups)])
    for begin in range(0, ups, unit):
        group.product(left, right, begin, ups, begin, block)
    left, right = group.operand(saved["attended"]), group.operand(d_branch, [(0, unit)])
    group.product(left, right, 0, unit, 0, block)
    first_pack = group.run(0)
    *first_pack, d_branch = lax.optimization_barrier((*first_pack, d_branch))
    d_attended = mt(d_branch, w["out"]).astype(BF16)
    dq, dk, dv = attend_back(
        saved["query"], saved["keys"], saved["values"], seen, saved["lse"], d_attended
    )
    if earlier:
        dq = earlier[1].step(dq)
    qkv = w["qkv"]
    parts = mt(dk, qkv[:, width : 2 * width]) + mt(dv, qkv[:, 2 * width :])
    d_x = d_first + mt(dq, qkv[:, :width]) + parts[:rows]
    for j in range(1, n_ctx):
        d_x = d_x + turned(parts[j * rows : (j + 1) * rows].astype(BF16), n_ctx - j).astype(F32)
    d_pool = (d_joined[:, width:] / counts).astype(BF16)
    d_states = d_chr + tm(onehot, d_pool)
    proj, states, entering = saved["proj"], saved["states"], saved["entering"]
    half = proj.shape[1] // 4
    whole, _ = joined_scan(scan_back_kernel, half, place, (d_states, proj, live), True)
    pieces = []
    for side in (0, 1):
        cols = slice(side * half, (side + 1) * half)
        if side == 0:
            before = jnp.concatenate([entering[:, cols], states[:-CHUNKS, cols]], axis=0)
        else:
            before = jnp.concatenate([states[CHUNKS:, cols], entering[:, cols]], axis=0)
        opened = jax.nn.sigmoid(proj[:, 2 * side * half : (2 * side + 1) * half])
        target = proj[:, (2 * side + 1) * half : (2 * side + 2) * half]
        flow = jnp.where(live > 0.0, whole[:, cols] * opened, 0.0)
        pieces += [flow * (1.0 - opened) * (target - before), flow]
    d_proj = jnp.concatenate(pieces, axis=1).astype(BF16)
    d_c = (d_chr + mt(d_proj, w["gru"])).astype(BF16)
    if earlier:
        d_c = earlier[0].step(d_c)
    small = (
        jnp.stack(
            [column_sums(dq), column_sums(dv), column_sums(d_branch), column_sums(d_ffn), column_sums(d_mixed)]
        ),
        column_sums(d_hidden)[None],
        jnp.stack([gain1, gain2, gain3, gain4]),
        jnp.stack([shift1, shift2, shift3, shift4]),
        column_sums(d_proj)[None],
    )
    packed = jnp.concatenate(
        [jnp.swapaxes(p.reshape(p.shape[0], count, -1), 0, 1).reshape(count, -1) for p in small], axis=1
    )
    packed = jnp.pad(packed, ((0, 0), (0, 16 * unit - packed.shape[1])))
    group = Packing(section, unit, False)
    left, right = group.operand(saved["active"]), group.operand(d_ffn, [(0, unit)])
    group.product(left, right, 0, unit, 0, 4 * block)
    left, right = group.operand(saved["x"]), group.operand(dq, [(0, unit)])
    group.product(left, right, 0, unit, 0, block)
    left = group.operand(saved["x_all"])
    for grad in (dk, dv):
        group.product(left, group.operand(grad, [(0, unit)]), 0, unit, 0, block)
    left, right = group.operand(saved["chars_low"]), group.operand(d_proj, [(0, width)])
    for begin in range(0, width, unit):
        group.product(left, right, begin, width, begin, block)
    left = group.operand(d_c)
    split = table_split(w["table"].shape[0])
    named = []
    for names in (ids, ids_other):
        names = names[:, None] - section * split
        named.append((names == jnp.arange(2 * unit)[None, :]).astype(BF16))
    right = group.local(*named)
    for begin in (0, unit):
        group.product(left, right, begin, 0, 0, block)
    group.plain(packed.astype(BF16).reshape(-1, unit), 16)
    second_pack = group.run(1)
    sizes = [(p.shape[0], p.size // count // p.shape[0]) for p in small]
    return d_x.astype(BF16), d_c, first_pack, second_pack, sizes


def table_split(vocab):
    return -(-vocab // 256) * 128


def on_device(
    ends, char_ends, char_ids, groups, lengths, w_qkv, biases, w_out, w_up, b_up, w_down,
    ln_gain, ln_shift, char_table, w_gru, b_gru, w_conv,
):
    section, place = lax.axis_index(SEC), lax.axis_index(CTX)
    n_dp, n_ctx = lax.axis_size(DP), lax.axis_size(CTX)
    is_first = section == 0
    names = ("gru", "table", "qkv", "out", "up", "down", "conv")
    local = (w_gru, char_table, w_qkv, w_out, w_up, w_down, w_conv)
    chars_here = jax.vmap(interleave)(char_ends[0])

    def dealt(pair):
        kept = pick(pair, section)
        got = swap(pick(pair, 1 - section))
        return jnp.where(is_first, kept, got), jnp.where(is_first, got, kept)

    x, cot_tok = dealt(ends[0])
    c, cot_chr = dealt(chars_here)
    layers = ({}, {})

    def spread(own):
        other = swap(own)
        return jnp.where(is_first, own, other), jnp.where(is_first, other, own)

    for name, value in zip(names, local):
        for layer, own in zip(layers, spread(value[0].reshape(-1, value.shape[-1]))):
            layer[name] = own
    vectors = (biases, b_up, ln_gain, ln_shift, b_gru)
    for layer, own in zip(layers, spread(jnp.concatenate([v[0].reshape(-1) for v in vectors]))):
        at = 0
        for name, value in zip(("biases", "b_up", "gains", "shifts", "b_gru"), vectors):
            layer[name] = own[at : at + value[0].size].reshape(value.shape[1:])
            at += value[0].size
    rows, width = x.shape
    ids = interleave(pick(char_ids, section))
    ids_other = interleave(pick(char_ids, 1 - section))
    group = interleave(pick(groups, section))
    live = (group >= 0).astype(F32)[:, None]
    onehot = jnp.arange(rows)[:, None] == (group - place * rows)[None, :]
    counts = jnp.sum(onehot.astype(F32), axis=1, keepdims=True)
    onehot = onehot.astype(BF16)
    shard = jnp.mod(place - jnp.arange(n_ctx), n_ctx)
    spots = (shard[:, None] * rows + jnp.arange(rows)[None, :]).reshape(-1, 1)
    seen = (spots < pick(lengths, section)).astype(F32)

    kept = []
    for layer in (0, 1):
        x, c, saved = layer_forward(layers[layer], x, c, ids, live, onehot, counts, seen, place)
        kept.append(saved)
    g_x, g_c = cot_tok, cot_chr
    chains = [None, None]
    for layer in (1, 0):
        g_x, g_c, first_pack, second_pack, sizes = layer_backward(
            layers[layer], kept[layer], g_x, g_c, ids, ids_other, live, onehot, counts, seen, place, section,
            chains[1],
        )
        chains[layer] = (Halving(first_pack, True), Halving(second_pack, False))
        if layer:
            g_x, g_c, chains[1][1].sent = lax.optimization_barrier((g_x, g_c, chains[1][1].sent))
    (x0, y0), (x1, y1) = chains
    finish([y1, x1, x0, y1, y0, x1, x0, y1, y0, x0, y0, x0, y0] + [x1, y1, x0, y0] * n_dp * n_ctx)
    packs = [[chain.total for chain in pair] for pair in chains]

    def gathered(grad, value):
        got = swap(jnp.where(is_first, value, grad))
        return jnp.where(is_first, jnp.stack([grad, got]), jnp.stack([got, value]))[None]

    ends_out = gathered(g_x, x)
    char_ends_out = gathered(restore(g_c), restore(c))

    both = []
    for one, two in zip(*packs):
        mine = jnp.where(is_first, one, two)
        got = swap(jnp.where(is_first, two, one))
        both.append((jnp.where(is_first, mine, got), jnp.where(is_first, got, mine)))
    block = width // (n_dp * n_ctx)

    def columns(which, at, size, parts, crossed=False):
        cut = [[half[at + i * size : at + (i + 1) * size] for i in range(parts)] for half in both[which]]
        if crossed:
            return jnp.concatenate([half[i] for i in range(parts) for half in cut], axis=1)
        return jnp.concatenate(cut[0] + cut[1], axis=1)

    d_conv = jnp.stack([columns(0, tap * 2 * block, 2 * block, 1) for tap in range(w_conv.shape[1])])
    at = w_conv.shape[1] * 2 * block
    ups = w_up.shape[2] // width
    d_up = columns(0, at, block, ups)
    d_out = columns(0, at + ups * block, block, 1)
    d_down = columns(1, 0, ups * block, 1)
    at = ups * block
    d_qkv = columns(1, at, block, 3, True)
    d_gru = columns(1, at + 3 * block, block, 2)
    at += 5 * block
    split = table_split(char_table.shape[1])
    d_table = jnp.concatenate(
        [
            jnp.concatenate([half[at : at + block], half[at + block : at + 2 * block]], axis=1)[:, :take]
            for half, take in zip(both[1], (split, char_table.shape[1] - split))
        ],
        axis=1,
    ).T
    vectors = (both[1][0][at + 2 * block :] + both[1][1][at + 2 * block :]).reshape(-1)
    sums, at = [], 0
    for parts, size in sizes:
        sums.append(vectors[at : at + parts * size].reshape(parts, size))
        at += parts * size
    return (
        ends_out,
        char_ends_out,
        d_qkv[None],
        sums[0][None],
        d_out[None],
        d_up[None],
        sums[1],
        d_down[None],
        sums[2][None],
        sums[3][None],
        d_table[None],
        d_gru[None],
        sums[4],
        d_conv[None],
    )


def solution(mesh):
    both = (DP, CTX)
    held, rows, columns = P(SEC, DP, CTX), P(SEC, both), P(SEC, None, both)
    layer = P(SEC)
    in_specs = (held, held, P(DP, CTX), P(DP, CTX), P(DP)) + (layer,) * 12
    out_specs = (
        held, held, rows, columns, rows, rows, rows, rows, columns, columns, columns, rows, rows, columns,
    )
    return jax.shard_map(
        on_device, mesh=mesh, in_specs=in_specs, out_specs=out_specs, check_vma=False
    )
```

```python
import functools

import jax
import jax.numpy as jnp
from jax import lax
from jax.experimental import pallas as pl
from jax.experimental.pallas import tpu as pltpu
from jax.sharding import PartitionSpec as P

HEADS = 12
CHUNKS = 8
NORM_EPS = 1e-06
MASKED = -1000000000.0
SEC, DP, CTX = "section", "dp", "ctx"
F32, BF16 = jnp.float32, jnp.bfloat16
MIB = 2**20


def contract(left, right, dims):
    return lax.dot_general(left, right, (dims, ((), ())), preferred_element_type=F32)


def mm(left, right):
    return contract(left, right, ((1,), (0,)))


def mt(left, right):
    return contract(left, right, ((1,), (1,)))


def tm(left, right):
    return contract(left, right, ((0,), (0,)))


def flip(value, axis, bit):
    return lax.ppermute(value, axis, [(i, i ^ (1 << bit)) for i in range(lax.axis_size(axis))])


def swap(value):
    return flip(value, SEC, 0)


def turned(value, by):
    count = lax.axis_size(CTX)
    return lax.ppermute(value, CTX, [(i, (i + by) % count) for i in range(count)])


def pick(value, index, axis=0):
    return lax.dynamic_index_in_dim(value, index, axis, keepdims=False)


def interleave(value):
    rows = value.shape[0]
    return jnp.swapaxes(
        value.reshape((CHUNKS, rows // CHUNKS) + value.shape[1:]), 0, 1
    ).reshape(value.shape)


def restore(value):
    rows = value.shape[0]
    return jnp.swapaxes(
        value.reshape((rows // CHUNKS, CHUNKS) + value.shape[1:]), 0, 1
    ).reshape(value.shape)


def params(mib):
    return pltpu.CompilerParams(vmem_limit_bytes=mib * MIB)


def attend_back_kernel(
    size, q_ref, k_ref, v_ref, seen_ref, lse_ref, do_ref, dq_ref, dk_ref, dv_ref
):
    seen = seen_ref[...] > 0.0
    scale = size**-0.5
    for head in range(q_ref.shape[1] // size):
        at = slice(head * size, (head + 1) * size)
        query, keys, grad = q_ref[:, at], k_ref[:, at], do_ref[:, at]
        scores = jnp.where(seen, mt(keys, query), MASKED)
        probs = jnp.exp(scores - lse_ref[0, head : head + 1, :])
        g_probs = mt(v_ref[:, at], grad)
        row = jnp.sum(g_probs * probs, axis=0, keepdims=True)
        g_scores = (probs * (g_probs - row)).astype(BF16)
        dv_ref[:, at] = mm(probs.astype(BF16), grad).astype(BF16)
        dk_ref[:, at] = mm(g_scores, query).astype(BF16)
        dq_ref[:, at] = (tm(g_scores, keys) * scale).astype(BF16)


def attend_back(query, keys, values, seen, lse, grad):
    rows, width = query.shape
    count = keys.shape[0]
    size = width // HEADS
    block = 2 * size
    steps = width // block
    by_rows = pl.BlockSpec((rows, block), lambda i: (0, i))
    by_keys = pl.BlockSpec((count, block), lambda i: (0, i))
    return pl.pallas_call(
        functools.partial(attend_back_kernel, size),
        grid=(steps,),
        in_specs=[
            by_rows,
            by_keys,
            by_keys,
            pl.BlockSpec((count, 1), lambda i: (0, 0)),
            pl.BlockSpec((1, 8, rows), lambda i: (i, 0, 0)),
            by_rows,
        ],
        out_specs=[by_rows, by_keys, by_keys],
        out_shape=[
            jax.ShapeDtypeStruct((rows, width), BF16),
            jax.ShapeDtypeStruct((count, width), BF16),
            jax.ShapeDtypeStruct((count, width), BF16),
        ],
        compiler_params=params(40),
        cost_estimate=pl.CostEstimate(flops=1, bytes_accessed=1, transcendentals=0),
    )(query, keys, values, seen, lse, grad)


MESH = pl.DeviceIdType.MESH


def fetch(layer, own, other, target, semaphore):
    section = lax.axis_index(SEC)
    copies = [pltpu.make_async_copy(source, target, semaphore) for source in (own, other)]

    @pl.when(section == layer)
    def _():
        copies[0].start()

    @pl.when(section != layer)
    def _():
        copies[1].start()

    return copies[0]


def greet(hops):
    barrier = pltpu.get_barrier_semaphore()
    count = lax.axis_size(CTX)
    for hop in hops:
        to = lax.rem(lax.axis_index(CTX) + hop, count)
        pl.semaphore_signal(barrier, inc=1, device_id={CTX: to}, device_id_type=MESH)
    pl.semaphore_wait(barrier, len(hops))


def send(source, target, hop, send_sem, recv_sem):
    to = lax.rem(lax.axis_index(CTX) + hop, lax.axis_size(CTX))
    copy = pltpu.make_async_remote_copy(
        src_ref=source, dst_ref=target, send_sem=send_sem, recv_sem=recv_sem,
        device_id={CTX: to}, device_id_type=MESH,
    )
    copy.start()
    return copy


class Relay:
    def __init__(self, source, slots, sems):
        self.source, self.slots, self.sems = source, slots, sems
        self.rows, self.count, self.place = source.shape[0], lax.axis_size(CTX), lax.axis_index(CTX)

    def slot(self, j):
        return self.slots.at[j * self.rows : (j + 1) * self.rows, :]

    def copies(self, step):
        n, me = self.count, self.place
        right = (me < n - 1) & (me >= step - 1)
        left = (me > 0) & (me <= n - step)
        for nth, (there, going, to, slot, held) in enumerate(
            ((1, right, step, step, step - 1), (n - 1, left, n - step, n - step, n - step + 1))
        ):
            source = self.source if step == 1 else self.slot(held)
            copy = pltpu.make_async_remote_copy(
                src_ref=source, dst_ref=self.slot(slot),
                send_sem=self.sems[0].at[2 * step - 2 + nth], recv_sem=self.sems[1].at[slot - 1],
                device_id={CTX: lax.rem(me + there, n)}, device_id_type=MESH,
            )
            yield going, held, copy

    def wait(self, slot):
        pltpu.make_async_remote_copy(
            src_ref=self.source, dst_ref=self.slot(slot),
            send_sem=self.sems[0].at[0], recv_sem=self.sems[1].at[slot - 1],
            device_id={CTX: lax.rem(self.place + 1, self.count)}, device_id_type=MESH,
        ).wait_recv()

    def start(self, step):
        for nth, (going, held, copy) in enumerate(self.copies(step)):
            if step > 1:
                came = (self.place >= step - 1) if nth == 0 else (self.place <= self.count - step)
                pl.when(came)(functools.partial(self.wait, held))
            pl.when(going)(copy.start)

    def finish(self):
        n, me = self.count, self.place
        pl.when(me == n - 1)(functools.partial(self.wait, n - 1))
        pl.when(me == 0)(functools.partial(self.wait, 1))
        for step in range(1, n):
            for going, _, copy in self.copies(step):
                pl.when(going)(copy.wait_send)


def unit_of(values):
    centred = values - jnp.mean(values, axis=1, keepdims=True)
    scale = lax.rsqrt(jnp.mean(centred * centred, axis=1, keepdims=True) + NORM_EPS)
    return centred * scale, scale


def unit_back(unit, scale, inner):
    mean = jnp.mean(inner, axis=1, keepdims=True)
    along = jnp.mean(inner * unit, axis=1, keepdims=True)
    return scale * (inner - mean - unit * along)


def gelu_pair(values):
    size = jnp.abs(values)
    bell = jnp.exp(-0.5 * values * values)
    t = 1.0 / (1.0 + (0.3275911 * 0.7071067811865476) * size)
    poly = t * (
        0.254829592 + t * (-0.284496736 + t * (1.421413741 + t * (-1.453152027 + t * 1.061405429)))
    )
    tail = 0.5 * poly * bell
    cdf = jnp.where(values >= 0.0, 1.0 - tail, tail)
    return values * cdf, cdf + values * (bell * 0.3989422804014327)


def gates(proj_ref, live_ref, at, rate, width):
    live = live_ref[at, :] > 0.0
    opened = jax.nn.sigmoid(proj_ref[at, rate : rate + width])
    return jnp.where(live, 1.0 - opened, 1.0), live, opened


def step_rows(step):
    return pl.ds(pl.multiple_of(step * CHUNKS, CHUNKS), CHUNKS)


def join_chunks(carry_ref, total_ref, slot, state, decay, order):
    width = state.shape[1]
    before = jnp.zeros((1, width), F32)
    faded = jnp.ones((1, width), F32)
    for chunk in order:
        carry_ref[slot, chunk : chunk + 1, :] = before
        carry_ref[slot + 1, chunk : chunk + 1, :] = faded
        own = decay[chunk : chunk + 1, :]
        before = own * before + state[chunk : chunk + 1, :]
        faded = own * faded
    total_ref[slot : slot + 1, :] = before
    total_ref[slot + 1 : slot + 2, :] = faded
    if slot:
        total_ref[4:8, :] = jnp.zeros((4, width), F32)


def entering_chunks(carry_ref, total_ref, inbox_ref, sems, reverse):
    count, place = lax.axis_size(CTX), lax.axis_index(CTX)
    width = total_ref.shape[1]
    copies = [
        send(total_ref, inbox_ref.at[j - 1], j, sems[0].at[j - 1], sems[1].at[j - 1])
        for j in range(1, count)
    ]
    for copy in copies:
        copy.wait()
    entering = []
    for slot in (0, 2):
        so_far = jnp.zeros((1, width), F32)
        rising = (slot == 0) != reverse
        for hop in range(count - 1, 0, -1):
            there = inbox_ref.at[(hop if rising else count - hop) - 1]
            valid = (place >= hop) if rising else (place + hop < count)
            longer = there[slot + 1 : slot + 2, :] * so_far + there[slot : slot + 1, :]
            so_far = jnp.where(valid, longer, so_far)
        entering.append(carry_ref[slot] + carry_ref[slot + 1] * so_far)
    return entering


def by_step(values):
    return values.reshape(values.shape[0] // CHUNKS, CHUNKS, values.shape[1])


def chars_kernel(
    layer, x_ref, c_ref, ids_ref, live_ref, group_ref, bias_ref, table_a, table_b, gru_a, gru_b,
    all_ref, chars_ref, low_ref, proj_ref, state_ref, entering_ref, pooled_ref,
    table_v, gru_v, decay_ref, carry_ref, total_ref, inbox_ref, fetch_sems, x_sems, total_sems,
):
    count = lax.axis_size(CTX)
    rows = x_ref.shape[0]
    width = proj_ref.shape[1] // 4
    steps = proj_ref.shape[0] // CHUNKS
    table = fetch(layer, table_a, table_b, table_v, fetch_sems.at[0])
    gru = fetch(layer, gru_a, gru_b, gru_v, fetch_sems.at[1])
    greet(range(1, count))
    relay = Relay(x_ref, all_ref, x_sems)
    relay.start(1)
    all_ref[0:rows, :] = x_ref[...]
    table.wait()
    names = lax.broadcasted_iota(jnp.int32, (c_ref.shape[0], table_v.shape[0]), 1)
    named = jnp.where(names == ids_ref[...], 1.0, 0.0).astype(BF16)
    chars = c_ref[...].astype(F32) + mm(named, table_v[...])
    chars_ref[...] = chars
    low_ref[...] = chars.astype(BF16)
    gru.wait()
    proj_ref[...] = mm(low_ref[...], gru_v[...]) + bias_ref[...]
    relay.start(2)
    unroll = 8

    def step(i, carry):
        state_f, decay_f, state_b, decay_b = carry
        for u in range(unroll):
            at = step_rows(i * unroll + u)
            keep, live, opened = gates(proj_ref, live_ref, at, 0, width)
            inflow = jnp.where(live, opened * proj_ref[at, width : 2 * width], 0.0)
            state_f = keep * state_f + inflow
            decay_f = keep * decay_f
            state_ref[at, 0:width] = state_f
            decay_ref[at, 0:width] = decay_f
            at = step_rows(steps - 1 - i * unroll - u)
            keep, live, opened = gates(proj_ref, live_ref, at, 2 * width, width)
            inflow = jnp.where(live, opened * proj_ref[at, 3 * width : 4 * width], 0.0)
            state_b = keep * state_b + inflow
            decay_b = keep * decay_b
            state_ref[at, width : 2 * width] = state_b
            decay_ref[at, width : 2 * width] = decay_b
        return state_f, decay_f, state_b, decay_b

    zero = jnp.zeros((CHUNKS, width), F32)
    one = jnp.ones((CHUNKS, width), F32)
    state_f, decay_f, state_b, decay_b = lax.fori_loop(
        0, steps // unroll, step, (zero, one, zero, one)
    )
    join_chunks(carry_ref, total_ref, 0, state_f, decay_f, range(CHUNKS))
    join_chunks(carry_ref, total_ref, 2, state_b, decay_b, range(CHUNKS - 1, -1, -1))
    entering = entering_chunks(carry_ref, total_ref, inbox_ref, total_sems, False)
    for side, carried in enumerate(entering):
        at = slice(side * width, (side + 1) * width)
        entering_ref[:, at] = carried
        whole = by_step(state_ref[:, at]) + by_step(decay_ref[:, at]) * carried[None]
        state_ref[:, at] = whole.reshape(steps * CHUNKS, width)
    tokens = lax.broadcasted_iota(jnp.int32, (rows, group_ref.shape[1]), 0)
    onehot = jnp.where(tokens == group_ref[...], 1.0, 0.0)
    counts = jnp.sum(onehot, axis=1, keepdims=True)
    pooled_ref[...] = (mm(onehot.astype(BF16), state_ref[...].astype(BF16)) / counts).astype(BF16)
    for step in range(3, count):
        relay.start(step)
    relay.finish()


VMEM_SPEC = pl.BlockSpec(memory_space=pltpu.VMEM)
ANY_SPEC = pl.BlockSpec(memory_space=pl.ANY)
DMA = pltpu.SemaphoreType.DMA


def call(kernel, plain, weights, outs, scratch, collective_id=None):
    options = {} if collective_id is None else dict(collective_id=collective_id, has_side_effects=True)
    return pl.pallas_call(
        kernel,
        in_specs=[VMEM_SPEC] * len(plain) + [ANY_SPEC] * len(weights),
        out_specs=[VMEM_SPEC] * len(outs),
        out_shape=[jax.ShapeDtypeStruct(*o) for o in outs],
        scratch_shapes=scratch,
        compiler_params=pltpu.CompilerParams(vmem_limit_bytes=58 * MIB, **options),
        cost_estimate=pl.CostEstimate(flops=1, bytes_accessed=1, transcendentals=0),
    )(*plain, *weights)


def room(weight):
    return pltpu.VMEM(weight.shape, weight.dtype)


def deal_kernel(
    lengths_ref, e_ref, ce_ref, rows_ref, columns_ref, vec_ref, inner_ref, gru_ref, table_ref,
    x_ref, cot_ref, c_ref, ccot_ref, vec0_ref, vec1_ref, inner0_ref, inner1_ref,
    ids_ref, other_ref, live_ref, row_ref, column_ref, seen_ref, gru_out, table_out,
    e_in, ce_in, vec_in, inner_in, sems,
):
    section, place = lax.axis_index(SEC), lax.axis_index(CTX)
    rows = x_ref.shape[0]
    barrier = pltpu.get_barrier_semaphore()
    pl.semaphore_signal(barrier, inc=1, device_id={SEC: 1 - section}, device_id_type=MESH)
    pl.semaphore_wait(barrier, 1)
    copies = []
    for nth, (source, target) in enumerate(
        (
            (e_ref.at[1 - section], e_in), (ce_ref.at[1 - section], ce_in), (vec_ref, vec_in),
            (inner_ref, inner_in), (table_ref, table_out), (gru_ref, gru_out),
        )
    ):
        copy = pltpu.make_async_remote_copy(
            src_ref=source, dst_ref=target, send_sem=sems[0].at[nth], recv_sem=sems[1].at[nth],
            device_id={SEC: 1 - section}, device_id_type=MESH,
        )
        copy.start()
        copies.append(copy)
    first = section == 0
    ids_ref[...] = jnp.where(first, columns_ref[:, 0:1], columns_ref[:, 1:2])
    other_ref[...] = jnp.where(first, columns_ref[:, 1:2], columns_ref[:, 0:1])
    group = jnp.where(first, columns_ref[:, 2:3], columns_ref[:, 3:4])
    live_ref[...] = jnp.where(group >= 0, 1.0, 0.0)
    column_ref[...] = group - place * rows
    row_ref[...] = jnp.where(first, rows_ref[2:3, :], rows_ref[3:4, :]) - place * rows
    length = jnp.where(first, lengths_ref[0], lengths_ref[1])
    count = lax.axis_size(CTX)
    for j in range(count):
        spots = lax.broadcasted_iota(jnp.int32, (rows, 1), 0) + lax.rem(place - j + count, count) * rows
        seen_ref[j * rows : (j + 1) * rows, :] = jnp.where(spots < length, 1.0, 0.0)
    for copy in copies:
        copy.wait()
    x_ref[...] = jnp.where(first, e_ref[0], e_in[...])
    cot_ref[...] = jnp.where(first, e_in[...], e_ref[1])
    c_ref[...] = jnp.where(first, ce_ref[0], ce_in[...])
    ccot_ref[...] = jnp.where(first, ce_in[...], ce_ref[1])
    vec0_ref[...] = jnp.where(first, vec_ref[...], vec_in[...])
    vec1_ref[...] = jnp.where(first, vec_in[...], vec_ref[...])
    inner0_ref[...] = jnp.where(first, inner_ref[...], inner_in[...])
    inner1_ref[...] = jnp.where(first, inner_in[...], inner_ref[...])


def deal(lengths, e, ce, indices, vec, inner, gru, table):
    _, rows, width = e.shape
    slots, keys = ce.shape[1], rows * lax.axis_size(CTX)
    tok, char = ((rows, width), BF16), ((slots, width), BF16)
    thin = ((slots, 1), jnp.int32)
    outs = [
        tok, tok, char, char, (vec.shape, F32), (vec.shape, F32), (inner.shape, F32), (inner.shape, F32),
        thin, thin, ((slots, 1), F32), ((1, slots), jnp.int32), thin, ((keys, 1), F32),
        (gru.shape, BF16), (table.shape, BF16),
    ]
    plain = [e, ce, indices, indices.T, vec, inner]
    return pl.pallas_call(
        deal_kernel,
        in_specs=[pl.BlockSpec(memory_space=pltpu.SMEM)] + [VMEM_SPEC] * len(plain) + [ANY_SPEC] * 2,
        out_specs=[VMEM_SPEC] * 14 + [ANY_SPEC] * 2,
        out_shape=[jax.ShapeDtypeStruct(*o) for o in outs],
        scratch_shapes=[
            pltpu.VMEM(*tok), pltpu.VMEM(*char), pltpu.VMEM(vec.shape, F32), pltpu.VMEM(inner.shape, F32),
            [DMA((6,))] * 2,
        ],
        compiler_params=pltpu.CompilerParams(
            vmem_limit_bytes=58 * MIB, collective_id=10, has_side_effects=True
        ),
        cost_estimate=pl.CostEstimate(flops=1, bytes_accessed=1, transcendentals=0),
    )(lengths, *plain, gru, table)


def chars_forward(layer, w, x, c, ids, live, group):
    rows, width = x.shape
    slots = c.shape[0]
    count = lax.axis_size(CTX)
    half = width // 2
    outs = [
        ((count * rows, width), BF16), ((slots, width), F32), ((slots, width), BF16),
        ((slots, 4 * half), F32), ((slots, width), F32), ((CHUNKS, width), F32), ((rows, width), BF16),
    ]
    pair = [DMA((count - 1,))] * 2
    scratch = [
        room(w["table"][0]), room(w["gru"][0]), pltpu.VMEM((slots, width), F32),
        pltpu.VMEM((4, CHUNKS, half), F32), pltpu.VMEM((8, half), F32),
        pltpu.VMEM((count - 1, 8, half), F32), DMA((2,)), [DMA((2 * count - 2,)), DMA((count - 1,))], pair,
    ]
    return call(
        functools.partial(chars_kernel, layer), [x, c, ids, live, group, w["b_gru"]],
        [*w["table"], *w["gru"]], outs, scratch, 2 + layer,
    )


def heads_of(block, size, head):
    lanes = lax.broadcasted_iota(jnp.int32, block.shape, 1)
    return jnp.where(lanes // size == head, block, jnp.zeros_like(block))


def tokens_kernel(
    layer, size, x_ref, seen_ref, vec_ref, bias_ref,
    qkv_a, qkv_b, out_a, out_b, up_a, up_b, down_a, down_b,
    q_ref, k_ref, v_ref, lse_ref, att_ref, unit1_ref, scale1_ref, low_ref, active_ref, slope_ref,
    unit2_ref, scale2_ref, features_ref,
    qkv_v, out_v, up_v, down_v, scores_ref, sems,
):
    rows, width = q_ref.shape
    keys = x_ref.shape[0]
    waits = [
        fetch(layer, a, b, v, sems.at[i])
        for i, (a, b, v) in enumerate(
            [(qkv_a, qkv_b, qkv_v), (out_a, out_b, out_v), (up_a, up_b, up_v), (down_a, down_b, down_v)]
        )
    ]
    waits[0].wait()
    query = (mm(x_ref[0:rows, :], qkv_v[:, 0:width]) + vec_ref[0:1, :]).astype(BF16)
    q_ref[...] = query * jnp.asarray(size**-0.5, BF16)
    for begin in range(0, keys, 256):
        at = slice(begin, begin + 256)
        k_ref[at, :] = mm(x_ref[at, :], qkv_v[:, width : 2 * width]).astype(BF16)
        v_ref[at, :] = (mm(x_ref[at, :], qkv_v[:, 2 * width : 3 * width]) + vec_ref[1:2, :]).astype(BF16)
    block = 128
    heads = block // size

    def pair(i, carry):
        at = pl.ds(pl.multiple_of(i * block, block), block)
        query = q_ref[:, at]
        lanes = lax.broadcasted_iota(jnp.int32, (rows, block), 1)
        result = None
        for head in range(heads):
            mine = heads_of(query, size, head)
            top = jnp.full((1, rows), MASKED, F32)
            for begin in range(0, keys, 256):
                span = slice(begin, begin + 256)
                scores = mt(k_ref[span, at], mine)
                scores = jnp.where(seen_ref[span, :] > 0.0, scores, MASKED)
                scores_ref[span, :] = scores
                top = jnp.maximum(top, jnp.max(scores, axis=0, keepdims=True))
            total = jnp.zeros((1, rows), F32)
            for begin in range(0, keys, 256):
                span = slice(begin, begin + 256)
                weights = jnp.exp(scores_ref[span, :] - top)
                scores_ref[span, :] = weights
                total = total + jnp.sum(weights, axis=0, keepdims=True)
            lse_ref[i, head : head + 1, :] = top + jnp.log(total)
            share = 1.0 / total
            mixed = jnp.zeros((rows, block), F32)
            for begin in range(0, keys, 256):
                span = slice(begin, begin + 256)
                probs = (scores_ref[span, :] * share).astype(BF16)
                mixed = mixed + tm(probs, v_ref[span, at])
            result = mixed if head == 0 else jnp.where(lanes // size == head, mixed, result)
        att_ref[:, at] = result.astype(BF16)
        return carry

    lax.fori_loop(0, width // block, pair, 0)
    waits[1].wait()
    first = x_ref[0:rows, :].astype(F32) + mm(att_ref[...], out_v[...]) + vec_ref[2:3, :]
    unit, scale = unit_of(first)
    unit1_ref[...] = unit
    scale1_ref[...] = scale
    normed = unit * vec_ref[5:6, :] + vec_ref[9:10, :]
    low_ref[...] = normed.astype(BF16)
    waits[2].wait()
    waits[3].wait()
    second = normed + vec_ref[3:4, :]
    for begin in range(0, active_ref.shape[1], width):
        at = slice(begin, begin + width)
        hidden = mm(low_ref[...], up_v[:, at]) + bias_ref[:, at]
        active, slope = gelu_pair(hidden)
        active_ref[:, at] = active.astype(BF16)
        slope_ref[:, at] = slope.astype(BF16)
        second = second + mm(active_ref[:, at], down_v[at, :])
    unit, scale = unit_of(second)
    unit2_ref[...] = unit
    scale2_ref[...] = scale
    features_ref[...] = unit * vec_ref[6:7, :] + vec_ref[10:11, :]


def tokens_forward(layer, w, x_all, seen, rows):
    keys, width = x_all.shape
    inner = w["up"][0].shape[1]
    size = width // HEADS
    outs = [
        ((rows, width), BF16), ((keys, width), BF16), ((keys, width), BF16), ((width // 128, 8, rows), F32),
        ((rows, width), BF16), ((rows, width), F32), ((rows, 1), F32), ((rows, width), BF16),
        ((rows, inner), BF16), ((rows, inner), BF16), ((rows, width), F32), ((rows, 1), F32),
        ((rows, width), F32),
    ]
    names = ("qkv", "out", "up", "down")
    scratch = [room(w[name][0]) for name in names] + [pltpu.VMEM((keys, rows), F32), DMA((4,))]
    return call(
        functools.partial(tokens_kernel, layer, size), [x_all, seen, w["vec"], w["b_up"]],
        [a for name in names for a in w[name]], outs, scratch,
    )


def edges(values_ref, before_ref, after_ref, sems):
    rows, count = values_ref.shape[0], lax.axis_size(CTX)
    return [
        send(values_ref.at[rows - 16 : rows, :], before_ref, 1, sems[0].at[0], sems[1].at[0]),
        send(values_ref.at[0:16, :], after_ref, count - 1, sems[0].at[1], sems[1].at[1]),
    ]


def moved(values, edge, by):
    rows = values.shape[0]
    at = lax.broadcasted_iota(jnp.int32, values.shape, 0)
    rolled = pltpu.roll(values, by % rows, 0)
    return jnp.where(at == (0 if by > 0 else rows - 1), edge, rolled)


def edge_masks():
    place = lax.axis_index(CTX)
    before = jnp.where(place > 0, 1.0, 0.0)
    after = jnp.where(place < lax.axis_size(CTX) - 1, 1.0, 0.0)
    return before, after


def uniting_kernel(
    layer, features_ref, pooled_ref, chars_ref, state_ref, column_ref, vec_ref, conv_a, conv_b,
    tok_ref, chr_ref, joined_ref, slope_ref, unit3_ref, scale3_ref, unit4_ref, scale4_ref,
    conv_v, before_ref, after_ref, fetch_sem, sems,
):
    rows, width = features_ref.shape
    conv = fetch(layer, conv_a, conv_b, conv_v, fetch_sem.at[0])
    joined_ref[:, 0:width] = features_ref[...].astype(BF16)
    joined_ref[:, width : 2 * width] = pooled_ref[...]
    greet((1, lax.axis_size(CTX) - 1))
    copies = edges(joined_ref, before_ref, after_ref, sems)
    conv.wait()
    deep = 2 * width
    taps = [conv_v.at[tap * deep : (tap + 1) * deep, :] for tap in range(3)]
    joined = joined_ref[...]
    mixed = mm(joined, taps[1][...]) + vec_ref[4:5, :]
    lower = mm(joined, taps[0][...])
    upper = mm(joined, taps[2][...])
    for copy in copies:
        copy.wait()
    has_before, has_after = edge_masks()
    edge = mm(before_ref[...], taps[0][...])[15:16, :] * has_before
    mixed = mixed + moved(lower, edge, 1)
    edge = mm(after_ref[...], taps[2][...])[0:1, :] * has_after
    mixed = mixed + moved(upper, edge, -1)
    lifted, slope = gelu_pair(mixed)
    slope_ref[...] = slope
    unit, scale = unit_of(features_ref[...] + lifted)
    unit3_ref[...] = unit
    scale3_ref[...] = scale
    tok_ref[...] = (unit * vec_ref[7:8, :] + vec_ref[11:12, :]).astype(BF16)
    slots = column_ref.shape[0]
    tokens = lax.broadcasted_iota(jnp.int32, (slots, rows), 1)
    onehot = jnp.where(tokens == column_ref[...], 1.0, 0.0).astype(BF16)
    unit, scale = unit_of(chars_ref[...] + state_ref[...] + mm(onehot, lifted.astype(BF16)))
    unit4_ref[...] = unit
    scale4_ref[...] = scale
    chr_ref[...] = (unit * vec_ref[8:9, :] + vec_ref[12:13, :]).astype(BF16)


def uniting_forward(layer, w, features, pooled, chars, states, column):
    rows, width = features.shape
    slots = chars.shape[0]
    outs = [
        ((rows, width), BF16), ((slots, width), BF16), ((rows, 2 * width), BF16), ((rows, width), F32),
        ((rows, width), F32), ((rows, 1), F32), ((slots, width), F32), ((slots, 1), F32),
    ]
    edge = pltpu.VMEM((16, 2 * width), BF16)
    scratch = [room(w["conv"][0]), edge, edge, DMA((1,)), [DMA((2,))] * 2]
    return call(
        functools.partial(uniting_kernel, layer), [features, pooled, chars, states, column, w["vec"]],
        [*w["conv"]], outs, scratch, 4 + layer,
    )


def uniting_back_kernel(
    layer, gt_ref, gc_ref, unit3_ref, scale3_ref, unit4_ref, scale4_ref, slope_ref, column_ref, group_ref,
    vec_ref, conv_a, conv_b,
    feat_ref, chr_ref, states_ref, around_ref, sums_ref,
    conv_v, mixed_ref, before_ref, after_ref, fetch_sem, sems,
):
    rows, width = gt_ref.shape
    slots = gc_ref.shape[0]
    conv = fetch(layer, conv_a, conv_b, conv_v, fetch_sem.at[0])
    grad = gt_ref[...].astype(F32)
    unit = unit3_ref[...]
    sums_ref[1:2, :] = jnp.sum(grad * unit, axis=0, keepdims=True)
    sums_ref[2:3, :] = jnp.sum(grad, axis=0, keepdims=True)
    d_tok = unit_back(unit, scale3_ref[...], grad * vec_ref[7:8, :])
    grad = gc_ref[...].astype(F32)
    unit = unit4_ref[...]
    sums_ref[3:4, :] = jnp.sum(grad * unit, axis=0, keepdims=True)
    sums_ref[4:5, :] = jnp.sum(grad, axis=0, keepdims=True)
    d_chr = unit_back(unit, scale4_ref[...], grad * vec_ref[8:9, :])
    chr_ref[...] = d_chr
    tokens = lax.broadcasted_iota(jnp.int32, (rows, slots), 0)
    onehot = jnp.where(tokens == group_ref[...], 1.0, 0.0)
    counts = jnp.sum(onehot, axis=1, keepdims=True)
    d_lifted = d_tok + mm(onehot.astype(BF16), d_chr.astype(BF16))
    low = (d_lifted * slope_ref[...]).astype(BF16)
    mixed_ref[...] = low
    greet((1, lax.axis_size(CTX) - 1))
    copies = edges(mixed_ref, before_ref, after_ref, sems)
    d_mixed = low.astype(F32)
    sums_ref[0:1, :] = jnp.sum(d_mixed, axis=0, keepdims=True)
    sums_ref[5:8, :] = jnp.zeros((3, width), F32)
    conv.wait()
    deep = 2 * width
    taps = [conv_v.at[tap * deep : (tap + 1) * deep, :] for tap in range(3)]
    joined = mt(low, taps[1][...])
    earlier = mt(low, taps[0][...])
    later = mt(low, taps[2][...])
    for copy in copies:
        copy.wait()
    has_before, has_after = edge_masks()
    before = before_ref[...].astype(F32)[15:16, :] * has_before
    after = after_ref[...].astype(F32)[0:1, :] * has_after
    around_ref[:, 0:width] = moved(d_mixed, after, -1).astype(BF16)
    around_ref[:, width : 2 * width] = low
    around_ref[:, 2 * width : 3 * width] = moved(d_mixed, before, 1).astype(BF16)
    edge = mt(after_ref[...], taps[0][...])[0:1, :] * has_after
    joined = joined + moved(earlier, edge, -1)
    edge = mt(before_ref[...], taps[2][...])[15:16, :] * has_before
    joined = joined + moved(later, edge, 1)
    feat_ref[...] = d_tok + joined[:, 0:width]
    pool = (joined[:, width : 2 * width] / counts).astype(BF16)
    tokens = lax.broadcasted_iota(jnp.int32, (slots, rows), 1)
    across = jnp.where(tokens == column_ref[...], 1.0, 0.0).astype(BF16)
    states_ref[...] = chr_ref[...] + mm(across, pool)


def uniting_back(layer, w, g_tok, g_chr, saved, column, group):
    rows, width = g_tok.shape
    slots = g_chr.shape[0]
    outs = [
        ((rows, width), F32), ((slots, width), F32), ((slots, width), F32), ((rows, 3 * width), BF16),
        ((8, width), F32),
    ]
    edge = pltpu.VMEM((16, width), BF16)
    scratch = [
        room(w["conv"][0]), pltpu.VMEM((rows, width), BF16), edge, edge, DMA((1,)), [DMA((2,))] * 2,
    ]
    plain = [g_tok, g_chr, *(saved[k] for k in ("unit3", "scale3", "unit4", "scale4", "mixed_slope"))]
    return call(
        functools.partial(uniting_back_kernel, layer), plain + [column, group, w["vec"]],
        [*w["conv"]], outs, scratch, 6 + layer,
    )


def feed_back_kernel(
    layer, feat_ref, unit2_ref, scale2_ref, slope_ref, unit1_ref, scale1_ref, vec_ref,
    out_a, out_b, up_a, up_b, down_a, down_b,
    ffn_ref, hidden_ref, first_ref, branch_ref, att_ref, sums_ref, inner_ref,
    out_v, up_v, down_v, sems,
):
    rows, width = feat_ref.shape
    waits = [
        fetch(layer, a, b, v, sems.at[i])
        for i, (a, b, v) in enumerate([(out_a, out_b, out_v), (up_a, up_b, up_v), (down_a, down_b, down_v)])
    ]
    grad = feat_ref[...]
    unit = unit2_ref[...]
    sums_ref[0:1, :] = jnp.sum(grad * unit, axis=0, keepdims=True)
    sums_ref[1:2, :] = jnp.sum(grad, axis=0, keepdims=True)
    d_second = unit_back(unit, scale2_ref[...], grad * vec_ref[6:7, :])
    low = d_second.astype(BF16)
    ffn_ref[...] = low
    sums_ref[2:3, :] = jnp.sum(low.astype(F32), axis=0, keepdims=True)
    waits[2].wait()
    waits[1].wait()
    d_normed = d_second
    for begin in range(0, hidden_ref.shape[1], width):
        at = slice(begin, begin + width)
        hidden = (mt(low, down_v[at, :]) * slope_ref[:, at].astype(F32)).astype(BF16)
        hidden_ref[:, at] = hidden
        inner_ref[:, at] = jnp.sum(hidden.astype(F32), axis=0, keepdims=True)
        d_normed = d_normed + mt(hidden, up_v[:, at])
    unit = unit1_ref[...]
    sums_ref[3:4, :] = jnp.sum(d_normed * unit, axis=0, keepdims=True)
    sums_ref[4:5, :] = jnp.sum(d_normed, axis=0, keepdims=True)
    d_first = unit_back(unit, scale1_ref[...], d_normed * vec_ref[5:6, :])
    first_ref[...] = d_first
    low = d_first.astype(BF16)
    branch_ref[...] = low
    sums_ref[5:6, :] = jnp.sum(low.astype(F32), axis=0, keepdims=True)
    sums_ref[6:8, :] = jnp.zeros((2, width), F32)
    waits[0].wait()
    att_ref[...] = mt(low, out_v[...]).astype(BF16)


def feed_back(layer, w, d_feat, saved):
    rows, width = d_feat.shape
    inner = w["up"][0].shape[1]
    outs = [
        ((rows, width), BF16), ((rows, inner), BF16), ((rows, width), F32), ((rows, width), BF16),
        ((rows, width), BF16), ((8, width), F32), ((1, inner), F32),
    ]
    names = ("out", "up", "down")
    plain = [d_feat, *(saved[k] for k in ("unit2", "scale2", "slope", "unit1", "scale1"))]
    return call(
        functools.partial(feed_back_kernel, layer), plain + [w["vec"]],
        [a for name in names for a in w[name]], outs, [room(w[name][0]) for name in names] + [DMA((3,))],
    )


def project_back_kernel(
    layer, first_ref, dq_ref, dk_ref, dv_ref, qkv_a, qkv_b, own_ref, parts_ref, sums_ref, qkv_v, sems
):
    rows, width = dq_ref.shape
    qkv = fetch(layer, qkv_a, qkv_b, qkv_v, sems.at[0])
    sums_ref[...] = jnp.zeros_like(sums_ref)
    sums_ref[0:1, :] = jnp.sum(dq_ref[...].astype(F32), axis=0, keepdims=True)
    sums_ref[1:2, :] = jnp.sum(dv_ref[...].astype(F32), axis=0, keepdims=True)
    qkv.wait()
    for begin in range(0, dk_ref.shape[0], rows):
        at = slice(begin, begin + rows)
        value = mt(dk_ref[at, :], qkv_v[:, width : 2 * width]) + mt(dv_ref[at, :], qkv_v[:, 2 * width :])
        if begin == 0:
            own_ref[...] = first_ref[...] + value + mt(dq_ref[...], qkv_v[:, 0:width])
        else:
            parts_ref[begin - rows : begin, :] = value.astype(BF16)


def project_back(layer, w, d_first, dq, dk, dv):
    rows, width = dq.shape
    outs = [((rows, width), F32), ((dk.shape[0] - rows, width), BF16), ((8, width), F32)]
    return call(
        functools.partial(project_back_kernel, layer), [d_first, dq, dk, dv], [*w["qkv"]], outs,
        [room(w["qkv"][0]), DMA((1,))],
    )


def chars_back_kernel(
    layer, grad_ref, chr_ref, proj_ref, live_ref, before_ref, entering_ref, gru_a, gru_b,
    dproj_ref, dc_ref, sums_ref,
    gru_v, state_ref, decay_ref, carry_ref, total_ref, inbox_ref, fetch_sem, total_sems,
):
    count = lax.axis_size(CTX)
    width = proj_ref.shape[1] // 4
    slots = proj_ref.shape[0]
    steps = slots // CHUNKS
    gru = fetch(layer, gru_a, gru_b, gru_v, fetch_sem.at[0])
    greet(range(1, count))
    unroll = 8

    def step(i, carry):
        state_f, decay_f, state_b, decay_b = carry
        for u in range(unroll):
            at = step_rows(steps - 1 - i * unroll - u)
            keep = gates(proj_ref, live_ref, at, 0, width)[0]
            whole = grad_ref[at, 0:width] + state_f
            state_ref[at, 0:width] = whole
            decay_ref[at, 0:width] = decay_f
            state_f = keep * whole
            decay_f = keep * decay_f
            at = step_rows(i * unroll + u)
            keep = gates(proj_ref, live_ref, at, 2 * width, width)[0]
            whole = grad_ref[at, width : 2 * width] + state_b
            state_ref[at, width : 2 * width] = whole
            decay_ref[at, width : 2 * width] = decay_b
            state_b = keep * whole
            decay_b = keep * decay_b
        return state_f, decay_f, state_b, decay_b

    zero = jnp.zeros((CHUNKS, width), F32)
    one = jnp.ones((CHUNKS, width), F32)
    state_f, decay_f, state_b, decay_b = lax.fori_loop(
        0, steps // unroll, step, (zero, one, zero, one)
    )
    join_chunks(carry_ref, total_ref, 0, state_f, decay_f, range(CHUNKS - 1, -1, -1))
    join_chunks(carry_ref, total_ref, 2, state_b, decay_b, range(CHUNKS))
    entering = entering_chunks(carry_ref, total_ref, inbox_ref, total_sems, True)
    live = live_ref[...] > 0.0
    for side, carried in enumerate(entering):
        at = slice(side * width, (side + 1) * width)
        whole = by_step(state_ref[:, at]) + by_step(decay_ref[:, at]) * carried[None]
        whole = whole.reshape(slots, width)
        edge = entering_ref[:, at]
        if side == 0:
            before = jnp.concatenate([edge, before_ref[0 : slots - CHUNKS, at]], axis=0)
        else:
            before = jnp.concatenate([before_ref[CHUNKS:slots, at], edge], axis=0)
        opened = jax.nn.sigmoid(proj_ref[:, 2 * side * width : (2 * side + 1) * width])
        target = proj_ref[:, (2 * side + 1) * width : (2 * side + 2) * width]
        flow = jnp.where(live, whole * opened, 0.0)
        for part, value in enumerate((flow * (1.0 - opened) * (target - before), flow)):
            column = slice((2 * side + part) * width, (2 * side + part + 1) * width)
            low = value.astype(BF16)
            dproj_ref[:, column] = low
            sums_ref[:, column] = jnp.sum(low.astype(F32), axis=0, keepdims=True)
    gru.wait()
    dc_ref[...] = (chr_ref[...] + mt(dproj_ref[...], gru_v[...])).astype(BF16)


def chars_back(layer, w, d_states, d_chr, saved, live):
    slots, width = d_states.shape
    count = lax.axis_size(CTX)
    half = width // 2
    outs = [((slots, 4 * half), BF16), ((slots, width), BF16), ((1, 4 * half), F32)]
    scratch = [
        room(w["gru"][0]), pltpu.VMEM((slots, width), F32), pltpu.VMEM((slots, width), F32),
        pltpu.VMEM((4, CHUNKS, half), F32), pltpu.VMEM((8, half), F32),
        pltpu.VMEM((count - 1, 8, half), F32), DMA((1,)), [DMA((count - 1,))] * 2,
    ]
    plain = [d_states, d_chr, saved["proj"], live, saved["states"], saved["entering"]]
    return call(
        functools.partial(chars_back_kernel, layer), plain, [*w["gru"]], outs, scratch, 8 + layer,
    )


def layer_forward(layer, w, x, c, ids, live, group, column, seen):
    x_all, chars, chars_low, proj, states, entering, pooled = chars_forward(layer, w, x, c, ids, live, group)
    (
        query, keys, values, lse, attended, unit1, scale1, normed_low, active, slope, unit2, scale2, features,
    ) = tokens_forward(layer, w, x_all, seen, x.shape[0])
    tok_out, chr_out, joined, mixed_slope, unit3, scale3, unit4, scale4 = uniting_forward(
        layer, w, features, pooled, chars, states, column
    )
    saved = dict(
        x=x, x_all=x_all, chars_low=chars_low, proj=proj, states=states, entering=entering, query=query,
        keys=keys, values=values, lse=lse, attended=attended, unit1=unit1, scale1=scale1,
        normed_low=normed_low, active=active, slope=slope, unit2=unit2, scale2=scale2, joined=joined,
        mixed_slope=mixed_slope, unit3=unit3, scale3=scale3, unit4=unit4, scale4=scale4,
    )
    return tok_out, chr_out, saved


def bits_of(axis):
    return [(axis, bit) for bit in range(lax.axis_size(axis).bit_length() - 1)]


def exchange_order(x_first):
    dp = bits_of(DP)
    return (dp if x_first else dp[::-1]) + bits_of(CTX)


def shard_at(place, order, n_ctx):
    index = {DP: lax.axis_index(DP), CTX: lax.axis_index(CTX)}
    shard = index[DP] * n_ctx + index[CTX]
    for nth, (axis, bit) in enumerate(order):
        if (place >> (len(order) - 1 - nth)) & 1:
            mine = (index[axis] // (1 << bit)) % 2
            shard = shard + (1 - 2 * mine) * ((1 << bit) * (n_ctx if axis == DP else 1))
    return shard


class Packing:
    def __init__(self, section, unit, groups):
        self.section, self.unit, self.groups = section, unit, groups
        self.arrays, self.moves, self.jobs, self.rows = [], [], [], [0] * len(groups)

    def operand(self, value, pieces=None):
        width = value.shape[1]
        self.arrays.append(value)
        self.moves.append([(0, 0, width)] if pieces is None else [(b, h, h) for b, h in pieces])
        return len(self.arrays) - 1

    def local(self, *values):
        self.arrays.extend(values)
        self.moves.extend([None] * len(values))
        return len(self.arrays) - len(values)

    def product(self, group, left, chunks, size):
        self.jobs.append(dict(group=group, left=left, chunks=chunks, rows=size, row=self.rows[group]))
        self.rows[group] += size * len(chunks)

    def plain(self, group, value, size):
        self.jobs.append(
            dict(group=group, left=None, plain=self.local(value), rows=size, row=self.rows[group])
        )
        self.rows[group] += size

    def run(self, collective_id):
        orders = [exchange_order(x_first) for x_first in self.groups]
        n_ctx = lax.axis_size(CTX)
        count = lax.axis_size(DP) * n_ctx
        unit = self.unit
        if any(job["rows"] % 16 for job in self.jobs):
            return self.run_plainly(orders, n_ctx, count)
        outs = [((count // 2, rows, unit), BF16) for rows in self.rows for _ in (0, 1)]
        most = max(job["rows"] * len(job.get("chunks", (0,))) for job in self.jobs) * count
        coming = [
            pltpu.VMEM((a.shape[0], sum(piece[2] for piece in move)), a.dtype)
            for a, move in zip(self.arrays, self.moves)
            if move
        ]
        copies = sum(len(move) for move in self.moves if move)
        scratch = [pltpu.VMEM((most, unit), BF16), coming, [DMA((copies,))] * 2]
        kernel = functools.partial(pack_kernel, self.jobs, self.moves, count, orders, n_ctx)
        results = call(kernel, self.arrays, [], outs, scratch, collective_id)
        return [(results[2 * i], results[2 * i + 1]) for i in range(len(orders))]

    def run_plainly(self, orders, n_ctx, count):
        blocks = [[] for _ in orders]
        for job in self.jobs:
            if job["left"] is None:
                blocks[job["group"]].append(self.arrays[job["plain"]].reshape(count, job["rows"], self.unit))
                continue
            for right, begin, half, _ in job["chunks"]:
                parts = []
                for core in (0, 1):
                    one = self.arrays[job["left"]]
                    if self.moves[right] is None:
                        two = self.arrays[right + core]
                    else:
                        two = swap(self.arrays[right]) if core else self.arrays[right]
                    two = lax.dynamic_slice_in_dim(two, begin + self.section * half, self.unit, 1)
                    parts.append(tm(swap(one) if core else one, two))
                value = (parts[0] + parts[1]).astype(BF16)
                blocks[job["group"]].append(value.reshape(count, job["rows"], self.unit))
        results = []
        for order, parts in zip(orders, blocks):
            shards = jnp.stack([shard_at(place, order, n_ctx) for place in range(count)])
            whole = jnp.take(jnp.concatenate(parts, axis=1), shards, axis=0)
            results.append((whole[count // 2 :], whole[: count // 2]))
        return results


def pack_kernel(jobs, moves, count, orders, n_ctx, *refs):
    arrays, rest = refs[: len(moves)], refs[len(moves) :]
    outs, (held, coming, semaphores) = rest[: 2 * len(orders)], rest[2 * len(orders) :]
    send_sems, recv_sems = semaphores
    section = lax.axis_index(SEC)
    unit = held.shape[1]
    barrier = pltpu.get_barrier_semaphore()
    pl.semaphore_signal(barrier, inc=1, device_id={SEC: 1 - section}, device_id_type=MESH)
    pl.semaphore_wait(barrier, 1)
    places, copies, pending, nth, slot = {}, [], {}, 0, 0
    for index, move in enumerate(moves):
        if not move:
            continue
        target, at = coming[slot], 0
        places[index] = target
        pending[index] = []
        slot += 1
        for begin, half, width in move:
            source = arrays[index]
            if half:
                source = source.at[:, pl.ds(pl.multiple_of(begin + (1 - section) * half, 128), width)]
            copy = pltpu.make_async_remote_copy(
                src_ref=source,
                dst_ref=target.at[:, at : at + width] if half else target,
                send_sem=send_sems.at[nth],
                recv_sem=recv_sems.at[nth],
                device_id={SEC: 1 - section},
                device_id_type=MESH,
            )
            copy.start()
            copies.append(copy)
            pending[index].append(copy)
            at += width
            nth += 1
    for job in jobs:
        at, size = job["row"], job["rows"]
        total = count * size
        if job["left"] is None:
            held[0:total, :] = arrays[job["plain"]][...]
            chunks = [None]
        else:
            left, chunks = job["left"], job["chunks"]
            mine, theirs = [], []
            for index in [left] + [chunk[0] for chunk in chunks]:
                for copy in pending.pop(index, ()):
                    copy.wait_recv()
            for right, begin, half, there in chunks:
                if moves[right]:
                    column = pl.multiple_of(begin + section * half, 128)
                    mine.append(arrays[right][:, pl.ds(column, unit)])
                    theirs.append(places[right][:, there : there + unit])
                else:
                    mine.append(arrays[right][:, begin : begin + unit])
                    theirs.append(arrays[right + 1][:, begin : begin + unit])
            mine = jnp.concatenate(mine, axis=1)
            theirs = jnp.concatenate(theirs, axis=1)
            for begin in range(0, total, 768):
                span = slice(begin, begin + 768)
                value = tm(arrays[left][:, span], mine) + tm(places[left][:, span], theirs)
                for nth in range(len(chunks)):
                    held[nth * total + begin : nth * total + begin + 768, :] = value[
                        :, nth * unit : (nth + 1) * unit
                    ].astype(BF16)
        sent_ref, kept_ref = outs[2 * job["group"] : 2 * job["group"] + 2]
        for place in range(count):
            shard = shard_at(place, orders[job["group"]], n_ctx) * size
            target = kept_ref if place < count // 2 else sent_ref
            for nth in range(len(chunks)):
                begin = pl.multiple_of(shard + nth * total, 16)
                row = at + nth * size
                target[place % (count // 2), row : row + size, :] = held[pl.ds(begin, size), :]
    for copy in copies:
        copy.wait_send()


class Halving:
    def __init__(self, packed, x_first):
        self.sent, self.kept = packed
        self.order = exchange_order(x_first)
        self.total = None

    def step(self, after):
        key, self.order = self.order[0], self.order[1:]
        got = flip(self.sent, *key)
        got, kept, after = lax.optimization_barrier((got, self.kept, after))
        if not self.order:
            self.total = kept[0].astype(F32) + got[0].astype(F32)
            self.total, after = lax.optimization_barrier((self.total, after))
            return after
        cut = kept.shape[0] // 2
        sent = (kept[cut:].astype(F32) + got[cut:].astype(F32)).astype(BF16)
        kept = (kept[:cut].astype(F32) + got[:cut].astype(F32)).astype(BF16)
        self.sent, self.kept, after = lax.optimization_barrier((sent, kept, after))
        return after


class Queue:
    def __init__(self):
        self.chains = []

    def add(self, chains):
        self.chains.extend(chains)

    def advance(self, value, layer, part):
        for chain in PLAN.get((layer, part), ()):
            if self.chains[chain].order:
                value = self.chains[chain].step(value)
        return value

    def finish(self):
        after = jnp.zeros((), F32)
        while any(chain.order for chain in self.chains):
            for chain in TAIL:
                if self.chains[chain].order:
                    after = self.chains[chain].step(after)


PLAN = {
    (1, 1): (0, 1),
    (0, 3): (0, 1),
    (0, 4): (0, 1),
    (0, 0): (2, 3),
    (0, 1): (0, 1),
}
TAIL = (0, 1, 4, 5, 2, 3, 6, 7)


def returned(d_x, parts):
    rows, n_ctx = d_x.shape[0], lax.axis_size(CTX)
    for j in range(1, n_ctx):
        d_x = d_x + turned(parts[(j - 1) * rows : j * rows], n_ctx - j).astype(F32)
    return d_x


def layer_backward(layer, w, saved, g_tok, g_chr, ids_both, live, group_row, column, seen, section, queue):
    rows, width = g_tok.shape
    count = lax.axis_size(DP) * lax.axis_size(CTX)
    unit = width // 2
    block = width // count
    d_feat, d_chr, d_states, around, sums_a = uniting_back(layer, w, g_tok, g_chr, saved, column, group_row)
    d_feat = queue.advance(d_feat, layer, 3)
    d_ffn, d_hidden, d_first, d_branch, d_attended, sums_b, inner_sums = feed_back(layer, w, d_feat, saved)
    d_attended = queue.advance(d_attended, layer, 4)
    early = Packing(section, unit, (True, False))
    taps = around.shape[1] // width
    right = early.operand(around, [(t * width, unit) for t in range(taps)])
    chunks = [(right, t * width, unit, t * unit) for t in range(taps)]
    early.product(0, early.operand(saved["joined"]), chunks, 2 * block)
    ups = d_hidden.shape[1] // 2
    right = early.operand(d_hidden, [(0, ups)])
    chunks = [(right, begin, ups, begin) for begin in range(0, ups, unit)]
    early.product(1, early.operand(saved["normed_low"]), chunks, block)
    right = early.operand(d_branch, [(0, unit)])
    early.product(1, early.operand(saved["attended"]), [(right, 0, unit, 0)], block)
    packs = early.run(0)
    packs, d_attended = lax.optimization_barrier((packs, d_attended))
    chains = [Halving(pack, x_first) for pack, x_first in zip(packs, early.groups)]
    queue.add(chains)
    dq, dk, dv = attend_back(
        saved["query"], saved["keys"], saved["values"], seen, saved["lse"], d_attended
    )
    dq = queue.advance(dq, layer, 0)
    d_x, parts, sums_c = project_back(layer, w, d_first, dq, dk, dv)
    if layer:
        d_x = returned(d_x, parts)
    d_proj, d_c, proj_sums = chars_back(layer, w, d_states, d_chr, saved, live)
    d_proj = queue.advance(d_proj, layer, 1)
    small = (
        jnp.stack([sums_c[0], sums_c[1], sums_b[5], sums_b[2], sums_a[0]]),
        inner_sums,
        jnp.stack([sums_b[3], sums_b[0], sums_a[1], sums_a[3]]),
        jnp.stack([sums_b[4], sums_b[1], sums_a[2], sums_a[4]]),
        proj_sums,
    )
    packed = jnp.concatenate(
        [jnp.swapaxes(p.reshape(p.shape[0], count, -1), 0, 1).reshape(count, -1) for p in small], axis=1
    )
    packed = jnp.pad(packed, ((0, 0), (0, 16 * unit - packed.shape[1])))
    late = Packing(section, unit, (True, False))
    right = late.operand(d_ffn, [(0, unit)])
    late.product(0, late.operand(saved["active"]), [(right, 0, unit, 0)], 4 * block)
    left = late.operand(d_c)
    split = w["table"][0].shape[0] // 2
    named = []
    for names in ids_both:
        names = names - section * split
        named.append((names == jnp.arange(2 * unit)[None, :]).astype(BF16))
    right = late.local(*named)
    late.product(0, left, [(right, 0, 0, 0), (right, unit, 0, 0)], block)
    right = late.operand(dq, [(0, unit)])
    late.product(1, late.operand(saved["x"]), [(right, 0, unit, 0)], block)
    rights = [late.operand(grad, [(0, unit)]) for grad in (dk, dv)]
    late.product(1, late.operand(saved["x_all"]), [(right, 0, unit, 0) for right in rights], block)
    right = late.operand(d_proj, [(0, width)])
    chunks = [(right, begin, width, begin) for begin in range(0, width, unit)]
    late.product(1, late.operand(saved["chars_low"]), chunks, block)
    late.plain(1, packed.astype(BF16).reshape(-1, unit), 16)
    packs = late.run(1)
    packs, d_c, parts = lax.optimization_barrier((packs, d_c, parts))
    if not layer:
        d_x = returned(d_x, parts)
    more = [Halving(pack, x_first) for pack, x_first in zip(packs, late.groups)]
    queue.add(more)
    d_c = queue.advance(d_c, layer, 2)
    sizes = [(p.shape[0], p.size // count // p.shape[0]) for p in small]
    return d_x.astype(BF16), d_c, chains + more, sizes


def on_device(
    ends, char_ends, char_ids, groups, lengths, w_qkv, biases, w_out, w_up, b_up, w_down,
    ln_gain, ln_shift, char_table, w_gru, b_gru, w_conv,
):
    section = lax.axis_index(SEC)
    n_dp, n_ctx = lax.axis_size(DP), lax.axis_size(CTX)
    is_first = section == 0
    def turned_rows(value):
        shape = value.shape
        return jnp.swapaxes(value.reshape((shape[0], CHUNKS, -1) + shape[2:]), 1, 2).reshape(shape)

    padded = jnp.pad(char_table[0], ((0, -char_table.shape[1] % 256), (0, 0)))
    rows_16 = jnp.concatenate([biases[0], ln_gain[0], ln_shift[0], jnp.zeros_like(biases[0, :3])])
    inner_own = jnp.concatenate([b_up, b_gru], axis=1)
    indices = turned_rows(jnp.concatenate([char_ids, groups]))
    (
        x, cot_tok, c, cot_chr, vec0, vec1, inner0, inner1, ids, ids_other, live, group_row, column, seen,
        gru_other, table_other,
    ) = deal(lengths, ends[0], turned_rows(char_ends[0]), indices, rows_16, inner_own, w_gru[0], padded)
    ids_both = (ids, ids_other)
    weights = {"gru": (w_gru[0], gru_other), "table": (padded, table_other)}
    for name, own in (
        ("qkv", w_qkv[0]), ("out", w_out[0]), ("up", w_up[0]), ("down", w_down[0]),
        ("conv", w_conv[0].reshape(-1, w_conv.shape[3])),
    ):
        tied, x = lax.optimization_barrier((own, x))
        weights[name] = (own, swap(tied))
    layers = [
        dict(weights, vec=vec, b_up=inner[:, : b_up.shape[1]], b_gru=inner[:, b_up.shape[1] :])
        for vec, inner in ((vec0, inner0), (vec1, inner1))
    ]
    rows, width = x.shape

    kept = []
    for layer in (0, 1):
        x, c, saved = layer_forward(
            layer, layers[layer], x, c, ids, live, group_row, column, seen
        )
        kept.append(saved)
    g_x, g_c = cot_tok, cot_chr
    queue = Queue()
    chains = [None, None]
    for layer in (1, 0):
        g_x, g_c, chains[layer], sizes = layer_backward(
            layer, layers[layer], kept[layer], g_x, g_c, ids_both, live, group_row, column, seen, section, queue
        )
    queue.finish()
    packs = [[chain.total for chain in four] for four in chains]

    def gathered(grad, value):
        got = swap(jnp.where(is_first, value, grad))
        return jnp.where(is_first, jnp.stack([grad, got]), jnp.stack([got, value]))[None]

    ends_out = gathered(g_x, x)
    char_ends_out = gathered(restore(g_c), restore(c))

    both = []
    for one, two in zip(*packs):
        mine = jnp.where(is_first, one, two)
        got = swap(jnp.where(is_first, two, one))
        both.append((jnp.where(is_first, mine, got), jnp.where(is_first, got, mine)))
    block = width // (n_dp * n_ctx)

    def columns(which, at, size, parts, crossed=False):
        cut = [[half[at + i * size : at + (i + 1) * size] for i in range(parts)] for half in both[which]]
        if crossed:
            return jnp.concatenate([half[i] for i in range(parts) for half in cut], axis=1)
        return jnp.concatenate(cut[0] + cut[1], axis=1)

    d_conv = jnp.stack([columns(0, tap * 2 * block, 2 * block, 1) for tap in range(w_conv.shape[1])])
    ups = w_up.shape[2] // width
    d_up = columns(1, 0, block, ups)
    d_out = columns(1, ups * block, block, 1)
    d_down = columns(2, 0, ups * block, 1)
    at = ups * block
    split = padded.shape[0] // 2
    d_table = jnp.concatenate(
        [
            jnp.concatenate([half[at : at + block], half[at + block : at + 2 * block]], axis=1)[:, :take]
            for half, take in zip(both[2], (split, char_table.shape[1] - split))
        ],
        axis=1,
    ).T
    d_qkv = columns(3, 0, block, 3, True)
    d_gru = columns(3, 3 * block, block, 2)
    vectors = (both[3][0][5 * block :] + both[3][1][5 * block :]).reshape(-1)
    sums, at = [], 0
    for parts, size in sizes:
        sums.append(vectors[at : at + parts * size].reshape(parts, size))
        at += parts * size
    return (
        ends_out,
        char_ends_out,
        d_qkv[None],
        sums[0][None],
        d_out[None],
        d_up[None],
        sums[1],
        d_down[None],
        sums[2][None],
        sums[3][None],
        d_table[None],
        d_gru[None],
        sums[4],
        d_conv[None],
    )


def solution(mesh):
    both = (DP, CTX)
    held, rows, columns = P(SEC, DP, CTX), P(SEC, both), P(SEC, None, both)
    layer = P(SEC)
    in_specs = (held, held, P(DP, CTX), P(DP, CTX), P(DP)) + (layer,) * 12
    out_specs = (
        held, held, rows, columns, rows, rows, rows, rows, columns, columns, columns, rows, rows, columns,
    )
    return jax.shard_map(
        on_device, mesh=mesh, in_specs=in_specs, out_specs=out_specs, check_vma=False
    )
```

```python
import functools

import jax
import jax.numpy as jnp
from jax import lax
from jax.experimental import pallas as pl
from jax.experimental.pallas import tpu as pltpu
from jax.sharding import PartitionSpec as P

HEADS = 12
CHUNKS = 8
NORM_EPS = 1e-06
MASKED = -1000000000.0
SEC, DP, CTX = "section", "dp", "ctx"
F32, BF16 = jnp.float32, jnp.bfloat16
MIB = 2**20


def contract(left, right, dims):
    return lax.dot_general(left, right, (dims, ((), ())), preferred_element_type=F32)


def mm(left, right):
    return contract(left, right, ((1,), (0,)))


def mt(left, right):
    return contract(left, right, ((1,), (1,)))


def tm(left, right):
    return contract(left, right, ((0,), (0,)))


def flip(value, axis, bit):
    return lax.ppermute(value, axis, [(i, i ^ (1 << bit)) for i in range(lax.axis_size(axis))])


def swap(value):
    return flip(value, SEC, 0)


def turned(value, by):
    count = lax.axis_size(CTX)
    return lax.ppermute(value, CTX, [(i, (i + by) % count) for i in range(count)])


def pick(value, index, axis=0):
    return lax.dynamic_index_in_dim(value, index, axis, keepdims=False)


def interleave(value):
    rows = value.shape[0]
    return jnp.swapaxes(
        value.reshape((CHUNKS, rows // CHUNKS) + value.shape[1:]), 0, 1
    ).reshape(value.shape)


def restore(value):
    rows = value.shape[0]
    return jnp.swapaxes(
        value.reshape((rows // CHUNKS, CHUNKS) + value.shape[1:]), 0, 1
    ).reshape(value.shape)


def params(mib):
    return pltpu.CompilerParams(vmem_limit_bytes=mib * MIB)


def attend_back_kernel(
    size, q_ref, k_ref, v_ref, seen_ref, lse_ref, do_ref, dq_ref, dk_ref, dv_ref
):
    seen = seen_ref[...] > 0.0
    scale = size**-0.5
    for head in range(q_ref.shape[1] // size):
        at = slice(head * size, (head + 1) * size)
        query, keys, grad = q_ref[:, at], k_ref[:, at], do_ref[:, at]
        scores = jnp.where(seen, mt(keys, query), MASKED)
        probs = jnp.exp(scores - lse_ref[0, head : head + 1, :])
        g_probs = mt(v_ref[:, at], grad)
        row = jnp.sum(g_probs * probs, axis=0, keepdims=True)
        g_scores = (probs * (g_probs - row)).astype(BF16)
        dv_ref[:, at] = mm(probs.astype(BF16), grad).astype(BF16)
        dk_ref[:, at] = mm(g_scores, query).astype(BF16)
        dq_ref[:, at] = (tm(g_scores, keys) * scale).astype(BF16)


def attend_back(query, keys, values, seen, lse, grad):
    rows, width = query.shape
    count = keys.shape[0]
    size = width // HEADS
    block = 2 * size
    steps = width // block
    by_rows = pl.BlockSpec((rows, block), lambda i: (0, i))
    by_keys = pl.BlockSpec((count, block), lambda i: (0, i))
    return pl.pallas_call(
        functools.partial(attend_back_kernel, size),
        grid=(steps,),
        in_specs=[
            by_rows,
            by_keys,
            by_keys,
            pl.BlockSpec((count, 1), lambda i: (0, 0)),
            pl.BlockSpec((1, 8, rows), lambda i: (i, 0, 0)),
            by_rows,
        ],
        out_specs=[by_rows, by_keys, by_keys],
        out_shape=[
            jax.ShapeDtypeStruct((rows, width), BF16),
            jax.ShapeDtypeStruct((count, width), BF16),
            jax.ShapeDtypeStruct((count, width), BF16),
        ],
        compiler_params=params(40),
        cost_estimate=pl.CostEstimate(flops=1, bytes_accessed=1, transcendentals=0),
    )(query, keys, values, seen, lse, grad)


MESH = pl.DeviceIdType.MESH


def fetch(layer, own, other, target, semaphore):
    section = lax.axis_index(SEC)
    copies = [pltpu.make_async_copy(source, target, semaphore) for source in (own, other)]

    @pl.when(section == layer)
    def _():
        copies[0].start()

    @pl.when(section != layer)
    def _():
        copies[1].start()

    return copies[0]


def greet(hops):
    barrier = pltpu.get_barrier_semaphore()
    count = lax.axis_size(CTX)
    for hop in hops:
        to = lax.rem(lax.axis_index(CTX) + hop, count)
        pl.semaphore_signal(barrier, inc=1, device_id={CTX: to}, device_id_type=MESH)
    pl.semaphore_wait(barrier, len(hops))


def send(source, target, hop, send_sem, recv_sem):
    to = lax.rem(lax.axis_index(CTX) + hop, lax.axis_size(CTX))
    copy = pltpu.make_async_remote_copy(
        src_ref=source, dst_ref=target, send_sem=send_sem, recv_sem=recv_sem,
        device_id={CTX: to}, device_id_type=MESH,
    )
    copy.start()
    return copy


class Relay:
    def __init__(self, source, slots, sems):
        self.source, self.slots, self.sems = source, slots, sems
        self.rows, self.count, self.place = source.shape[0], lax.axis_size(CTX), lax.axis_index(CTX)

    def slot(self, j):
        return self.slots.at[j * self.rows : (j + 1) * self.rows, :]

    def copies(self, step):
        n, me = self.count, self.place
        right = (me < n - 1) & (me >= step - 1)
        left = (me > 0) & (me <= n - step)
        for nth, (there, going, to, slot, held) in enumerate(
            ((1, right, step, step, step - 1), (n - 1, left, n - step, n - step, n - step + 1))
        ):
            source = self.source if step == 1 else self.slot(held)
            copy = pltpu.make_async_remote_copy(
                src_ref=source, dst_ref=self.slot(slot),
                send_sem=self.sems[0].at[2 * step - 2 + nth], recv_sem=self.sems[1].at[slot - 1],
                device_id={CTX: lax.rem(me + there, n)}, device_id_type=MESH,
            )
            yield going, held, copy

    def wait(self, slot):
        pltpu.make_async_remote_copy(
            src_ref=self.source, dst_ref=self.slot(slot),
            send_sem=self.sems[0].at[0], recv_sem=self.sems[1].at[slot - 1],
            device_id={CTX: lax.rem(self.place + 1, self.count)}, device_id_type=MESH,
        ).wait_recv()

    def start(self, step):
        for nth, (going, held, copy) in enumerate(self.copies(step)):
            if step > 1:
                came = (self.place >= step - 1) if nth == 0 else (self.place <= self.count - step)
                pl.when(came)(functools.partial(self.wait, held))
            pl.when(going)(copy.start)

    def finish(self):
        n, me = self.count, self.place
        pl.when(me == n - 1)(functools.partial(self.wait, n - 1))
        pl.when(me == 0)(functools.partial(self.wait, 1))
        for step in range(1, n):
            for going, _, copy in self.copies(step):
                pl.when(going)(copy.wait_send)


def unit_of(values):
    centred = values - jnp.mean(values, axis=1, keepdims=True)
    scale = lax.rsqrt(jnp.mean(centred * centred, axis=1, keepdims=True) + NORM_EPS)
    return centred * scale, scale


def unit_back(unit, scale, inner):
    mean = jnp.mean(inner, axis=1, keepdims=True)
    along = jnp.mean(inner * unit, axis=1, keepdims=True)
    return scale * (inner - mean - unit * along)


def gelu_pair(values):
    size = jnp.abs(values)
    bell = jnp.exp(-0.5 * values * values)
    t = 1.0 / (1.0 + (0.3275911 * 0.7071067811865476) * size)
    poly = t * (
        0.254829592 + t * (-0.284496736 + t * (1.421413741 + t * (-1.453152027 + t * 1.061405429)))
    )
    tail = 0.5 * poly * bell
    cdf = jnp.where(values >= 0.0, 1.0 - tail, tail)
    return values * cdf, cdf + values * (bell * 0.3989422804014327)


def gates(proj_ref, live_ref, at, rate, width):
    live = live_ref[at, :] > 0.0
    opened = jax.nn.sigmoid(proj_ref[at, rate : rate + width])
    return jnp.where(live, 1.0 - opened, 1.0), live, opened


def step_rows(step):
    return pl.ds(pl.multiple_of(step * CHUNKS, CHUNKS), CHUNKS)


def join_chunks(carry_ref, total_ref, slot, state, decay, order):
    width = state.shape[1]
    before = jnp.zeros((1, width), F32)
    faded = jnp.ones((1, width), F32)
    for chunk in order:
        carry_ref[slot, chunk : chunk + 1, :] = before
        carry_ref[slot + 1, chunk : chunk + 1, :] = faded
        own = decay[chunk : chunk + 1, :]
        before = own * before + state[chunk : chunk + 1, :]
        faded = own * faded
    total_ref[slot : slot + 1, :] = before
    total_ref[slot + 1 : slot + 2, :] = faded
    if slot:
        total_ref[4:8, :] = jnp.zeros((4, width), F32)


def entering_chunks(carry_ref, total_ref, inbox_ref, sems, reverse):
    count, place = lax.axis_size(CTX), lax.axis_index(CTX)
    width = total_ref.shape[1]
    copies = [
        send(total_ref, inbox_ref.at[j - 1], j, sems[0].at[j - 1], sems[1].at[j - 1])
        for j in range(1, count)
    ]
    for copy in copies:
        copy.wait()
    entering = []
    for slot in (0, 2):
        so_far = jnp.zeros((1, width), F32)
        rising = (slot == 0) != reverse
        for hop in range(count - 1, 0, -1):
            there = inbox_ref.at[(hop if rising else count - hop) - 1]
            valid = (place >= hop) if rising else (place + hop < count)
            longer = there[slot + 1 : slot + 2, :] * so_far + there[slot : slot + 1, :]
            so_far = jnp.where(valid, longer, so_far)
        entering.append(carry_ref[slot] + carry_ref[slot + 1] * so_far)
    return entering


def by_step(values):
    return values.reshape(values.shape[0] // CHUNKS, CHUNKS, values.shape[1])


def chars_kernel(
    layer, x_ref, c_ref, ids_ref, live_ref, group_ref, bias_ref, table_a, table_b, gru_a, gru_b,
    all_ref, chars_ref, low_ref, proj_ref, state_ref, entering_ref, pooled_ref,
    table_v, gru_v, decay_ref, carry_ref, total_ref, inbox_ref, fetch_sems, x_sems, total_sems,
):
    count = lax.axis_size(CTX)
    rows = x_ref.shape[0]
    width = proj_ref.shape[1] // 4
    steps = proj_ref.shape[0] // CHUNKS
    table = fetch(layer, table_a, table_b, table_v, fetch_sems.at[0])
    gru = fetch(layer, gru_a, gru_b, gru_v, fetch_sems.at[1])
    greet(range(1, count))
    relay = Relay(x_ref, all_ref, x_sems)
    relay.start(1)
    all_ref[0:rows, :] = x_ref[...]
    table.wait()
    names = lax.broadcasted_iota(jnp.int32, (c_ref.shape[0], table_v.shape[0]), 1)
    named = jnp.where(names == ids_ref[...], 1.0, 0.0).astype(BF16)
    chars = c_ref[...].astype(F32) + mm(named, table_v[...])
    chars_ref[...] = chars
    low_ref[...] = chars.astype(BF16)
    gru.wait()
    proj_ref[...] = mm(low_ref[...], gru_v[...]) + bias_ref[...]
    relay.start(2)
    unroll = 8

    def step(i, carry):
        state_f, decay_f, state_b, decay_b = carry
        for u in range(unroll):
            at = step_rows(i * unroll + u)
            keep, live, opened = gates(proj_ref, live_ref, at, 0, width)
            inflow = jnp.where(live, opened * proj_ref[at, width : 2 * width], 0.0)
            state_f = keep * state_f + inflow
            decay_f = keep * decay_f
            state_ref[at, 0:width] = state_f
            decay_ref[at, 0:width] = decay_f
            at = step_rows(steps - 1 - i * unroll - u)
            keep, live, opened = gates(proj_ref, live_ref, at, 2 * width, width)
            inflow = jnp.where(live, opened * proj_ref[at, 3 * width : 4 * width], 0.0)
            state_b = keep * state_b + inflow
            decay_b = keep * decay_b
            state_ref[at, width : 2 * width] = state_b
            decay_ref[at, width : 2 * width] = decay_b
        return state_f, decay_f, state_b, decay_b

    zero = jnp.zeros((CHUNKS, width), F32)
    one = jnp.ones((CHUNKS, width), F32)
    state_f, decay_f, state_b, decay_b = lax.fori_loop(
        0, steps // unroll, step, (zero, one, zero, one)
    )
    join_chunks(carry_ref, total_ref, 0, state_f, decay_f, range(CHUNKS))
    join_chunks(carry_ref, total_ref, 2, state_b, decay_b, range(CHUNKS - 1, -1, -1))
    entering = entering_chunks(carry_ref, total_ref, inbox_ref, total_sems, False)
    for side, carried in enumerate(entering):
        at = slice(side * width, (side + 1) * width)
        entering_ref[:, at] = carried
        whole = by_step(state_ref[:, at]) + by_step(decay_ref[:, at]) * carried[None]
        state_ref[:, at] = whole.reshape(steps * CHUNKS, width)
    tokens = lax.broadcasted_iota(jnp.int32, (rows, group_ref.shape[1]), 0)
    onehot = jnp.where(tokens == group_ref[...], 1.0, 0.0)
    counts = jnp.sum(onehot, axis=1, keepdims=True)
    pooled_ref[...] = (mm(onehot.astype(BF16), state_ref[...].astype(BF16)) / counts).astype(BF16)
    for step in range(3, count):
        relay.start(step)
    relay.finish()


VMEM_SPEC = pl.BlockSpec(memory_space=pltpu.VMEM)
ANY_SPEC = pl.BlockSpec(memory_space=pl.ANY)
DMA = pltpu.SemaphoreType.DMA


def call(kernel, plain, weights, outs, scratch, collective_id=None):
    options = {} if collective_id is None else dict(collective_id=collective_id, has_side_effects=True)
    return pl.pallas_call(
        kernel,
        in_specs=[VMEM_SPEC] * len(plain) + [ANY_SPEC] * len(weights),
        out_specs=[VMEM_SPEC] * len(outs),
        out_shape=[jax.ShapeDtypeStruct(*o) for o in outs],
        scratch_shapes=scratch,
        compiler_params=pltpu.CompilerParams(vmem_limit_bytes=58 * MIB, **options),
        cost_estimate=pl.CostEstimate(flops=1, bytes_accessed=1, transcendentals=0),
    )(*plain, *weights)


def room(weight):
    return pltpu.VMEM(weight.shape, weight.dtype)


def deal_kernel(
    lengths_ref, e_ref, ce_ref, rows_ref, columns_ref, vec_ref, inner_ref, gru_ref, table_ref,
    x_ref, cot_ref, c_ref, ccot_ref, vec0_ref, vec1_ref, inner0_ref, inner1_ref,
    ids_ref, other_ref, live_ref, row_ref, column_ref, seen_ref, gru_out, table_out,
    e_in, ce_in, vec_in, inner_in, sems,
):
    section, place = lax.axis_index(SEC), lax.axis_index(CTX)
    rows = x_ref.shape[0]
    barrier = pltpu.get_barrier_semaphore()
    pl.semaphore_signal(barrier, inc=1, device_id={SEC: 1 - section}, device_id_type=MESH)
    pl.semaphore_wait(barrier, 1)
    copies = []
    for nth, (source, target) in enumerate(
        (
            (e_ref.at[1 - section], e_in), (ce_ref.at[1 - section], ce_in), (vec_ref, vec_in),
            (inner_ref, inner_in), (table_ref, table_out), (gru_ref, gru_out),
        )
    ):
        copy = pltpu.make_async_remote_copy(
            src_ref=source, dst_ref=target, send_sem=sems[0].at[nth], recv_sem=sems[1].at[nth],
            device_id={SEC: 1 - section}, device_id_type=MESH,
        )
        copy.start()
        copies.append(copy)
    first = section == 0
    ids_ref[...] = jnp.where(first, columns_ref[:, 0:1], columns_ref[:, 1:2])
    other_ref[...] = jnp.where(first, columns_ref[:, 1:2], columns_ref[:, 0:1])
    group = jnp.where(first, columns_ref[:, 2:3], columns_ref[:, 3:4])
    live_ref[...] = jnp.where(group >= 0, 1.0, 0.0)
    column_ref[...] = group - place * rows
    row_ref[...] = jnp.where(first, rows_ref[2:3, :], rows_ref[3:4, :]) - place * rows
    length = jnp.where(first, lengths_ref[0], lengths_ref[1])
    count = lax.axis_size(CTX)
    for j in range(count):
        spots = lax.broadcasted_iota(jnp.int32, (rows, 1), 0) + lax.rem(place - j + count, count) * rows
        seen_ref[j * rows : (j + 1) * rows, :] = jnp.where(spots < length, 1.0, 0.0)
    for copy in copies:
        copy.wait()
    x_ref[...] = jnp.where(first, e_ref[0], e_in[...])
    cot_ref[...] = jnp.where(first, e_in[...], e_ref[1])
    c_ref[...] = jnp.where(first, ce_ref[0], ce_in[...])
    ccot_ref[...] = jnp.where(first, ce_in[...], ce_ref[1])
    vec0_ref[...] = jnp.where(first, vec_ref[...], vec_in[...])
    vec1_ref[...] = jnp.where(first, vec_in[...], vec_ref[...])
    inner0_ref[...] = jnp.where(first, inner_ref[...], inner_in[...])
    inner1_ref[...] = jnp.where(first, inner_in[...], inner_ref[...])


def deal(lengths, e, ce, indices, vec, inner, gru, table):
    _, rows, width = e.shape
    slots, keys = ce.shape[1], rows * lax.axis_size(CTX)
    tok, char = ((rows, width), BF16), ((slots, width), BF16)
    thin = ((slots, 1), jnp.int32)
    outs = [
        tok, tok, char, char, (vec.shape, F32), (vec.shape, F32), (inner.shape, F32), (inner.shape, F32),
        thin, thin, ((slots, 1), F32), ((1, slots), jnp.int32), thin, ((keys, 1), F32),
        (gru.shape, BF16), (table.shape, BF16),
    ]
    plain = [e, ce, indices, indices.T, vec, inner]
    return pl.pallas_call(
        deal_kernel,
        in_specs=[pl.BlockSpec(memory_space=pltpu.SMEM)] + [VMEM_SPEC] * len(plain) + [ANY_SPEC] * 2,
        out_specs=[VMEM_SPEC] * 14 + [ANY_SPEC] * 2,
        out_shape=[jax.ShapeDtypeStruct(*o) for o in outs],
        scratch_shapes=[
            pltpu.VMEM(*tok), pltpu.VMEM(*char), pltpu.VMEM(vec.shape, F32), pltpu.VMEM(inner.shape, F32),
            [DMA((6,))] * 2,
        ],
        compiler_params=pltpu.CompilerParams(
            vmem_limit_bytes=58 * MIB, collective_id=10, has_side_effects=True
        ),
        cost_estimate=pl.CostEstimate(flops=1, bytes_accessed=1, transcendentals=0),
    )(lengths, *plain, gru, table)


def chars_forward(layer, w, x, c, ids, live, group):
    rows, width = x.shape
    slots = c.shape[0]
    count = lax.axis_size(CTX)
    half = width // 2
    outs = [
        ((count * rows, width), BF16), ((slots, width), F32), ((slots, width), BF16),
        ((slots, 4 * half), F32), ((slots, width), F32), ((CHUNKS, width), F32), ((rows, width), BF16),
    ]
    pair = [DMA((count - 1,))] * 2
    scratch = [
        room(w["table"][0]), room(w["gru"][0]), pltpu.VMEM((slots, width), F32),
        pltpu.VMEM((4, CHUNKS, half), F32), pltpu.VMEM((8, half), F32),
        pltpu.VMEM((count - 1, 8, half), F32), DMA((2,)), [DMA((2 * count - 2,)), DMA((count - 1,))], pair,
    ]
    return call(
        functools.partial(chars_kernel, layer), [x, c, ids, live, group, w["b_gru"]],
        [*w["table"], *w["gru"]], outs, scratch, 2 + layer,
    )


def heads_of(block, size, head):
    lanes = lax.broadcasted_iota(jnp.int32, block.shape, 1)
    return jnp.where(lanes // size == head, block, jnp.zeros_like(block))


def tokens_kernel(
    layer, size, x_ref, seen_ref, vec_ref, bias_ref,
    qkv_a, qkv_b, out_a, out_b, up_a, up_b, down_a, down_b,
    q_ref, k_ref, v_ref, lse_ref, att_ref, unit1_ref, scale1_ref, low_ref, active_ref, slope_ref,
    unit2_ref, scale2_ref, features_ref,
    qkv_v, out_v, up_v, down_v, scores_ref, sems,
):
    rows, width = q_ref.shape
    keys = x_ref.shape[0]
    waits = [
        fetch(layer, a, b, v, sems.at[i])
        for i, (a, b, v) in enumerate(
            [(qkv_a, qkv_b, qkv_v), (out_a, out_b, out_v), (up_a, up_b, up_v), (down_a, down_b, down_v)]
        )
    ]
    waits[0].wait()
    query = (mm(x_ref[0:rows, :], qkv_v[:, 0:width]) + vec_ref[0:1, :]).astype(BF16)
    q_ref[...] = query * jnp.asarray(size**-0.5, BF16)
    for begin in range(0, keys, 256):
        at = slice(begin, begin + 256)
        k_ref[at, :] = mm(x_ref[at, :], qkv_v[:, width : 2 * width]).astype(BF16)
        v_ref[at, :] = (mm(x_ref[at, :], qkv_v[:, 2 * width : 3 * width]) + vec_ref[1:2, :]).astype(BF16)
    block = 128
    heads = block // size

    def pair(i, carry):
        at = pl.ds(pl.multiple_of(i * block, block), block)
        query = q_ref[:, at]
        lanes = lax.broadcasted_iota(jnp.int32, (rows, block), 1)
        result = None
        for head in range(heads):
            mine = heads_of(query, size, head)
            top = jnp.full((1, rows), MASKED, F32)
            for begin in range(0, keys, 256):
                span = slice(begin, begin + 256)
                scores = mt(k_ref[span, at], mine)
                scores = jnp.where(seen_ref[span, :] > 0.0, scores, MASKED)
                scores_ref[span, :] = scores
                top = jnp.maximum(top, jnp.max(scores, axis=0, keepdims=True))
            total = jnp.zeros((1, rows), F32)
            for begin in range(0, keys, 256):
                span = slice(begin, begin + 256)
                weights = jnp.exp(scores_ref[span, :] - top)
                scores_ref[span, :] = weights
                total = total + jnp.sum(weights, axis=0, keepdims=True)
            lse_ref[i, head : head + 1, :] = top + jnp.log(total)
            share = 1.0 / total
            mixed = jnp.zeros((rows, block), F32)
            for begin in range(0, keys, 256):
                span = slice(begin, begin + 256)
                probs = (scores_ref[span, :] * share).astype(BF16)
                mixed = mixed + tm(probs, v_ref[span, at])
            result = mixed if head == 0 else jnp.where(lanes // size == head, mixed, result)
        att_ref[:, at] = result.astype(BF16)
        return carry

    lax.fori_loop(0, width // block, pair, 0)
    waits[1].wait()
    first = x_ref[0:rows, :].astype(F32) + mm(att_ref[...], out_v[...]) + vec_ref[2:3, :]
    unit, scale = unit_of(first)
    unit1_ref[...] = unit
    scale1_ref[...] = scale
    normed = unit * vec_ref[5:6, :] + vec_ref[9:10, :]
    low_ref[...] = normed.astype(BF16)
    waits[2].wait()
    waits[3].wait()
    second = normed + vec_ref[3:4, :]
    for begin in range(0, active_ref.shape[1], width):
        at = slice(begin, begin + width)
        hidden = mm(low_ref[...], up_v[:, at]) + bias_ref[:, at]
        active, slope = gelu_pair(hidden)
        active_ref[:, at] = active.astype(BF16)
        slope_ref[:, at] = slope.astype(BF16)
        second = second + mm(active_ref[:, at], down_v[at, :])
    unit, scale = unit_of(second)
    unit2_ref[...] = unit
    scale2_ref[...] = scale
    features_ref[...] = unit * vec_ref[6:7, :] + vec_ref[10:11, :]


def tokens_forward(layer, w, x_all, seen, rows):
    keys, width = x_all.shape
    inner = w["up"][0].shape[1]
    size = width // HEADS
    outs = [
        ((rows, width), BF16), ((keys, width), BF16), ((keys, width), BF16), ((width // 128, 8, rows), F32),
        ((rows, width), BF16), ((rows, width), F32), ((rows, 1), F32), ((rows, width), BF16),
        ((rows, inner), BF16), ((rows, inner), BF16), ((rows, width), F32), ((rows, 1), F32),
        ((rows, width), F32),
    ]
    names = ("qkv", "out", "up", "down")
    scratch = [room(w[name][0]) for name in names] + [pltpu.VMEM((keys, rows), F32), DMA((4,))]
    return call(
        functools.partial(tokens_kernel, layer, size), [x_all, seen, w["vec"], w["b_up"]],
        [a for name in names for a in w[name]], outs, scratch,
    )


def edges(values_ref, before_ref, after_ref, sems):
    rows, count = values_ref.shape[0], lax.axis_size(CTX)
    return [
        send(values_ref.at[rows - 16 : rows, :], before_ref, 1, sems[0].at[0], sems[1].at[0]),
        send(values_ref.at[0:16, :], after_ref, count - 1, sems[0].at[1], sems[1].at[1]),
    ]


def moved(values, edge, by):
    rows = values.shape[0]
    at = lax.broadcasted_iota(jnp.int32, values.shape, 0)
    rolled = pltpu.roll(values, by % rows, 0)
    return jnp.where(at == (0 if by > 0 else rows - 1), edge, rolled)


def edge_masks():
    place = lax.axis_index(CTX)
    before = jnp.where(place > 0, 1.0, 0.0)
    after = jnp.where(place < lax.axis_size(CTX) - 1, 1.0, 0.0)
    return before, after


def uniting_kernel(
    layer, features_ref, pooled_ref, chars_ref, state_ref, column_ref, vec_ref, conv_a, conv_b,
    tok_ref, chr_ref, joined_ref, slope_ref, unit3_ref, scale3_ref, unit4_ref, scale4_ref,
    conv_v, before_ref, after_ref, fetch_sem, sems,
):
    rows, width = features_ref.shape
    conv = fetch(layer, conv_a, conv_b, conv_v, fetch_sem.at[0])
    joined_ref[:, 0:width] = features_ref[...].astype(BF16)
    joined_ref[:, width : 2 * width] = pooled_ref[...]
    greet((1, lax.axis_size(CTX) - 1))
    copies = edges(joined_ref, before_ref, after_ref, sems)
    conv.wait()
    deep = 2 * width
    taps = [conv_v.at[tap * deep : (tap + 1) * deep, :] for tap in range(3)]
    joined = joined_ref[...]
    mixed = mm(joined, taps[1][...]) + vec_ref[4:5, :]
    lower = mm(joined, taps[0][...])
    upper = mm(joined, taps[2][...])
    for copy in copies:
        copy.wait()
    has_before, has_after = edge_masks()
    edge = mm(before_ref[...], taps[0][...])[15:16, :] * has_before
    mixed = mixed + moved(lower, edge, 1)
    edge = mm(after_ref[...], taps[2][...])[0:1, :] * has_after
    mixed = mixed + moved(upper, edge, -1)
    lifted, slope = gelu_pair(mixed)
    slope_ref[...] = slope
    unit, scale = unit_of(features_ref[...] + lifted)
    unit3_ref[...] = unit
    scale3_ref[...] = scale
    tok_ref[...] = (unit * vec_ref[7:8, :] + vec_ref[11:12, :]).astype(BF16)
    slots = column_ref.shape[0]
    tokens = lax.broadcasted_iota(jnp.int32, (slots, rows), 1)
    onehot = jnp.where(tokens == column_ref[...], 1.0, 0.0).astype(BF16)
    unit, scale = unit_of(chars_ref[...] + state_ref[...] + mm(onehot, lifted.astype(BF16)))
    unit4_ref[...] = unit
    scale4_ref[...] = scale
    chr_ref[...] = (unit * vec_ref[8:9, :] + vec_ref[12:13, :]).astype(BF16)


def uniting_forward(layer, w, features, pooled, chars, states, column):
    rows, width = features.shape
    slots = chars.shape[0]
    outs = [
        ((rows, width), BF16), ((slots, width), BF16), ((rows, 2 * width), BF16), ((rows, width), F32),
        ((rows, width), F32), ((rows, 1), F32), ((slots, width), F32), ((slots, 1), F32),
    ]
    edge = pltpu.VMEM((16, 2 * width), BF16)
    scratch = [room(w["conv"][0]), edge, edge, DMA((1,)), [DMA((2,))] * 2]
    return call(
        functools.partial(uniting_kernel, layer), [features, pooled, chars, states, column, w["vec"]],
        [*w["conv"]], outs, scratch, 4 + layer,
    )


def uniting_back_kernel(
    layer, gt_ref, gc_ref, unit3_ref, scale3_ref, unit4_ref, scale4_ref, slope_ref, column_ref, group_ref,
    vec_ref, conv_a, conv_b,
    feat_ref, chr_ref, states_ref, around_ref, sums_ref,
    conv_v, mixed_ref, before_ref, after_ref, fetch_sem, sems,
):
    rows, width = gt_ref.shape
    slots = gc_ref.shape[0]
    conv = fetch(layer, conv_a, conv_b, conv_v, fetch_sem.at[0])
    grad = gt_ref[...].astype(F32)
    unit = unit3_ref[...]
    sums_ref[1:2, :] = jnp.sum(grad * unit, axis=0, keepdims=True)
    sums_ref[2:3, :] = jnp.sum(grad, axis=0, keepdims=True)
    d_tok = unit_back(unit, scale3_ref[...], grad * vec_ref[7:8, :])
    grad = gc_ref[...].astype(F32)
    unit = unit4_ref[...]
    sums_ref[3:4, :] = jnp.sum(grad * unit, axis=0, keepdims=True)
    sums_ref[4:5, :] = jnp.sum(grad, axis=0, keepdims=True)
    d_chr = unit_back(unit, scale4_ref[...], grad * vec_ref[8:9, :])
    chr_ref[...] = d_chr
    tokens = lax.broadcasted_iota(jnp.int32, (rows, slots), 0)
    onehot = jnp.where(tokens == group_ref[...], 1.0, 0.0)
    counts = jnp.sum(onehot, axis=1, keepdims=True)
    d_lifted = d_tok + mm(onehot.astype(BF16), d_chr.astype(BF16))
    low = (d_lifted * slope_ref[...]).astype(BF16)
    mixed_ref[...] = low
    greet((1, lax.axis_size(CTX) - 1))
    copies = edges(mixed_ref, before_ref, after_ref, sems)
    d_mixed = low.astype(F32)
    sums_ref[0:1, :] = jnp.sum(d_mixed, axis=0, keepdims=True)
    sums_ref[5:8, :] = jnp.zeros((3, width), F32)
    conv.wait()
    deep = 2 * width
    taps = [conv_v.at[tap * deep : (tap + 1) * deep, :] for tap in range(3)]
    joined = mt(low, taps[1][...])
    earlier = mt(low, taps[0][...])
    later = mt(low, taps[2][...])
    for copy in copies:
        copy.wait()
    has_before, has_after = edge_masks()
    before = before_ref[...].astype(F32)[15:16, :] * has_before
    after = after_ref[...].astype(F32)[0:1, :] * has_after
    around_ref[:, 0:width] = moved(d_mixed, after, -1).astype(BF16)
    around_ref[:, width : 2 * width] = low
    around_ref[:, 2 * width : 3 * width] = moved(d_mixed, before, 1).astype(BF16)
    edge = mt(after_ref[...], taps[0][...])[0:1, :] * has_after
    joined = joined + moved(earlier, edge, -1)
    edge = mt(before_ref[...], taps[2][...])[15:16, :] * has_before
    joined = joined + moved(later, edge, 1)
    feat_ref[...] = d_tok + joined[:, 0:width]
    pool = (joined[:, width : 2 * width] / counts).astype(BF16)
    tokens = lax.broadcasted_iota(jnp.int32, (slots, rows), 1)
    across = jnp.where(tokens == column_ref[...], 1.0, 0.0).astype(BF16)
    states_ref[...] = chr_ref[...] + mm(across, pool)


def uniting_back(layer, w, g_tok, g_chr, saved, column, group):
    rows, width = g_tok.shape
    slots = g_chr.shape[0]
    outs = [
        ((rows, width), F32), ((slots, width), F32), ((slots, width), F32), ((rows, 3 * width), BF16),
        ((8, width), F32),
    ]
    edge = pltpu.VMEM((16, width), BF16)
    scratch = [
        room(w["conv"][0]), pltpu.VMEM((rows, width), BF16), edge, edge, DMA((1,)), [DMA((2,))] * 2,
    ]
    plain = [g_tok, g_chr, *(saved[k] for k in ("unit3", "scale3", "unit4", "scale4", "mixed_slope"))]
    return call(
        functools.partial(uniting_back_kernel, layer), plain + [column, group, w["vec"]],
        [*w["conv"]], outs, scratch, 6 + layer,
    )


def feed_back_kernel(
    layer, feat_ref, unit2_ref, scale2_ref, slope_ref, unit1_ref, scale1_ref, vec_ref,
    out_a, out_b, up_a, up_b, down_a, down_b,
    ffn_ref, hidden_ref, first_ref, branch_ref, att_ref, sums_ref, inner_ref,
    out_v, up_v, down_v, sems,
):
    rows, width = feat_ref.shape
    waits = [
        fetch(layer, a, b, v, sems.at[i])
        for i, (a, b, v) in enumerate([(out_a, out_b, out_v), (up_a, up_b, up_v), (down_a, down_b, down_v)])
    ]
    grad = feat_ref[...]
    unit = unit2_ref[...]
    sums_ref[0:1, :] = jnp.sum(grad * unit, axis=0, keepdims=True)
    sums_ref[1:2, :] = jnp.sum(grad, axis=0, keepdims=True)
    d_second = unit_back(unit, scale2_ref[...], grad * vec_ref[6:7, :])
    low = d_second.astype(BF16)
    ffn_ref[...] = low
    sums_ref[2:3, :] = jnp.sum(low.astype(F32), axis=0, keepdims=True)
    waits[2].wait()
    waits[1].wait()
    d_normed = d_second
    for begin in range(0, hidden_ref.shape[1], width):
        at = slice(begin, begin + width)
        hidden = (mt(low, down_v[at, :]) * slope_ref[:, at].astype(F32)).astype(BF16)
        hidden_ref[:, at] = hidden
        inner_ref[:, at] = jnp.sum(hidden.astype(F32), axis=0, keepdims=True)
        d_normed = d_normed + mt(hidden, up_v[:, at])
    unit = unit1_ref[...]
    sums_ref[3:4, :] = jnp.sum(d_normed * unit, axis=0, keepdims=True)
    sums_ref[4:5, :] = jnp.sum(d_normed, axis=0, keepdims=True)
    d_first = unit_back(unit, scale1_ref[...], d_normed * vec_ref[5:6, :])
    first_ref[...] = d_first
    low = d_first.astype(BF16)
    branch_ref[...] = low
    sums_ref[5:6, :] = jnp.sum(low.astype(F32), axis=0, keepdims=True)
    sums_ref[6:8, :] = jnp.zeros((2, width), F32)
    waits[0].wait()
    att_ref[...] = mt(low, out_v[...]).astype(BF16)


def feed_back(layer, w, d_feat, saved):
    rows, width = d_feat.shape
    inner = w["up"][0].shape[1]
    outs = [
        ((rows, width), BF16), ((rows, inner), BF16), ((rows, width), F32), ((rows, width), BF16),
        ((rows, width), BF16), ((8, width), F32), ((1, inner), F32),
    ]
    names = ("out", "up", "down")
    plain = [d_feat, *(saved[k] for k in ("unit2", "scale2", "slope", "unit1", "scale1"))]
    return call(
        functools.partial(feed_back_kernel, layer), plain + [w["vec"]],
        [a for name in names for a in w[name]], outs, [room(w[name][0]) for name in names] + [DMA((3,))],
    )


def project_back_kernel(
    layer, first_ref, dq_ref, dk_ref, dv_ref, qkv_a, qkv_b, own_ref, parts_ref, sums_ref, qkv_v, sems
):
    rows, width = dq_ref.shape
    qkv = fetch(layer, qkv_a, qkv_b, qkv_v, sems.at[0])
    sums_ref[...] = jnp.zeros_like(sums_ref)
    sums_ref[0:1, :] = jnp.sum(dq_ref[...].astype(F32), axis=0, keepdims=True)
    sums_ref[1:2, :] = jnp.sum(dv_ref[...].astype(F32), axis=0, keepdims=True)
    qkv.wait()
    for begin in range(0, dk_ref.shape[0], rows):
        at = slice(begin, begin + rows)
        value = mt(dk_ref[at, :], qkv_v[:, width : 2 * width]) + mt(dv_ref[at, :], qkv_v[:, 2 * width :])
        if begin == 0:
            own_ref[...] = first_ref[...] + value + mt(dq_ref[...], qkv_v[:, 0:width])
        else:
            parts_ref[begin - rows : begin, :] = value.astype(BF16)


def project_back(layer, w, d_first, dq, dk, dv):
    rows, width = dq.shape
    outs = [((rows, width), F32), ((dk.shape[0] - rows, width), BF16), ((8, width), F32)]
    return call(
        functools.partial(project_back_kernel, layer), [d_first, dq, dk, dv], [*w["qkv"]], outs,
        [room(w["qkv"][0]), DMA((1,))],
    )


def chars_back_kernel(
    layer, grad_ref, chr_ref, proj_ref, live_ref, before_ref, entering_ref, gru_a, gru_b,
    dproj_ref, dc_ref, sums_ref,
    gru_v, state_ref, decay_ref, carry_ref, total_ref, inbox_ref, fetch_sem, total_sems,
):
    count = lax.axis_size(CTX)
    width = proj_ref.shape[1] // 4
    slots = proj_ref.shape[0]
    steps = slots // CHUNKS
    gru = fetch(layer, gru_a, gru_b, gru_v, fetch_sem.at[0])
    greet(range(1, count))
    unroll = 8

    def step(i, carry):
        state_f, decay_f, state_b, decay_b = carry
        for u in range(unroll):
            at = step_rows(steps - 1 - i * unroll - u)
            keep = gates(proj_ref, live_ref, at, 0, width)[0]
            whole = grad_ref[at, 0:width] + state_f
            state_ref[at, 0:width] = whole
            decay_ref[at, 0:width] = decay_f
            state_f = keep * whole
            decay_f = keep * decay_f
            at = step_rows(i * unroll + u)
            keep = gates(proj_ref, live_ref, at, 2 * width, width)[0]
            whole = grad_ref[at, width : 2 * width] + state_b
            state_ref[at, width : 2 * width] = whole
            decay_ref[at, width : 2 * width] = decay_b
            state_b = keep * whole
            decay_b = keep * decay_b
        return state_f, decay_f, state_b, decay_b

    zero = jnp.zeros((CHUNKS, width), F32)
    one = jnp.ones((CHUNKS, width), F32)
    state_f, decay_f, state_b, decay_b = lax.fori_loop(
        0, steps // unroll, step, (zero, one, zero, one)
    )
    join_chunks(carry_ref, total_ref, 0, state_f, decay_f, range(CHUNKS - 1, -1, -1))
    join_chunks(carry_ref, total_ref, 2, state_b, decay_b, range(CHUNKS))
    entering = entering_chunks(carry_ref, total_ref, inbox_ref, total_sems, True)
    live = live_ref[...] > 0.0
    for side, carried in enumerate(entering):
        at = slice(side * width, (side + 1) * width)
        whole = by_step(state_ref[:, at]) + by_step(decay_ref[:, at]) * carried[None]
        whole = whole.reshape(slots, width)
        edge = entering_ref[:, at]
        if side == 0:
            before = jnp.concatenate([edge, before_ref[0 : slots - CHUNKS, at]], axis=0)
        else:
            before = jnp.concatenate([before_ref[CHUNKS:slots, at], edge], axis=0)
        opened = jax.nn.sigmoid(proj_ref[:, 2 * side * width : (2 * side + 1) * width])
        target = proj_ref[:, (2 * side + 1) * width : (2 * side + 2) * width]
        flow = jnp.where(live, whole * opened, 0.0)
        for part, value in enumerate((flow * (1.0 - opened) * (target - before), flow)):
            column = slice((2 * side + part) * width, (2 * side + part + 1) * width)
            low = value.astype(BF16)
            dproj_ref[:, column] = low
            sums_ref[:, column] = jnp.sum(low.astype(F32), axis=0, keepdims=True)
    gru.wait()
    dc_ref[...] = (chr_ref[...] + mt(dproj_ref[...], gru_v[...])).astype(BF16)


def middle_hop():
    return lax.axis_size(CTX) // 2


def chars_back(layer, w, d_states, d_chr, saved, live):
    slots, width = d_states.shape
    count = lax.axis_size(CTX)
    half = width // 2
    outs = [((slots, 4 * half), BF16), ((slots, width), BF16), ((1, 4 * half), F32)]
    scratch = [
        room(w["gru"][0]), pltpu.VMEM((slots, width), F32), pltpu.VMEM((slots, width), F32),
        pltpu.VMEM((4, CHUNKS, half), F32), pltpu.VMEM((8, half), F32),
        pltpu.VMEM((count - 1, 8, half), F32), DMA((1,)), [DMA((count - 1,))] * 2,
    ]
    plain = [d_states, d_chr, saved["proj"], live, saved["states"], saved["entering"]]
    return call(
        functools.partial(chars_back_kernel, layer), plain, [*w["gru"]], outs, scratch, 8 + layer,
    )


def layer_forward(layer, w, x, c, ids, live, group, column, seen):
    x_all, chars, chars_low, proj, states, entering, pooled = chars_forward(layer, w, x, c, ids, live, group)
    (
        query, keys, values, lse, attended, unit1, scale1, normed_low, active, slope, unit2, scale2, features,
    ) = tokens_forward(layer, w, x_all, seen, x.shape[0])
    tok_out, chr_out, joined, mixed_slope, unit3, scale3, unit4, scale4 = uniting_forward(
        layer, w, features, pooled, chars, states, column
    )
    saved = dict(
        x=x, x_all=x_all, chars_low=chars_low, proj=proj, states=states, entering=entering, query=query,
        keys=keys, values=values, lse=lse, attended=attended, unit1=unit1, scale1=scale1,
        normed_low=normed_low, active=active, slope=slope, unit2=unit2, scale2=scale2, joined=joined,
        mixed_slope=mixed_slope, unit3=unit3, scale3=scale3, unit4=unit4, scale4=scale4,
    )
    return tok_out, chr_out, saved


def bits_of(axis):
    return [(axis, bit) for bit in range(lax.axis_size(axis).bit_length() - 1)]


def exchange_order(x_first):
    dp = bits_of(DP)
    return (dp if x_first else dp[::-1]) + bits_of(CTX)


def shard_at(place, order, n_ctx):
    index = {DP: lax.axis_index(DP), CTX: lax.axis_index(CTX)}
    shard = index[DP] * n_ctx + index[CTX]
    for nth, (axis, bit) in enumerate(order):
        if (place >> (len(order) - 1 - nth)) & 1:
            mine = (index[axis] // (1 << bit)) % 2
            shard = shard + (1 - 2 * mine) * ((1 << bit) * (n_ctx if axis == DP else 1))
    return shard


class Packing:
    def __init__(self, section, unit, groups):
        self.section, self.unit, self.groups = section, unit, groups
        self.arrays, self.moves, self.jobs, self.rows = [], [], [], [0] * len(groups)

    def operand(self, value, pieces=None):
        width = value.shape[1]
        self.arrays.append(value)
        self.moves.append([(0, 0, width)] if pieces is None else [(b, h, h) for b, h in pieces])
        return len(self.arrays) - 1

    def local(self, *values):
        self.arrays.extend(values)
        self.moves.extend([None] * len(values))
        return len(self.arrays) - len(values)

    def product(self, group, left, chunks, size):
        self.jobs.append(dict(group=group, left=left, chunks=chunks, rows=size, row=self.rows[group]))
        self.rows[group] += size * len(chunks)

    def plain(self, group, value, size):
        self.jobs.append(
            dict(group=group, left=None, plain=self.local(value), rows=size, row=self.rows[group])
        )
        self.rows[group] += size

    def run(self, collective_id, parts=None):
        orders = [exchange_order(x_first) for x_first in self.groups]
        n_ctx = lax.axis_size(CTX)
        count = lax.axis_size(DP) * n_ctx
        unit = self.unit
        if any(job["rows"] % 16 for job in self.jobs):
            results = self.run_plainly(orders, n_ctx, count)
            return results if parts is None else (results, came_back(parts))
        outs = [((count // 2, rows, unit), BF16) for rows in self.rows for _ in (0, 1)]
        most = max(job["rows"] * len(job.get("chunks", (0,))) for job in self.jobs) * count
        coming = [
            pltpu.VMEM((a.shape[0], sum(piece[2] for piece in move)), a.dtype)
            for a, move in zip(self.arrays, self.moves)
            if move
        ]
        copies = sum(len(move) for move in self.moves if move)
        scratch = [pltpu.VMEM((most, unit), BF16), coming, [DMA((copies,))] * 2]
        kernel = functools.partial(pack_kernel, self.jobs, self.moves, count, orders, n_ctx, parts is not None)
        plain = list(self.arrays)
        if parts is not None:
            plain.append(parts)
            outs.append((parts.shape, parts.dtype))
            scratch.append([DMA((n_ctx - 1,))] * 2)
        results = call(kernel, plain, [], outs, scratch, collective_id)
        packs = [(results[2 * i], results[2 * i + 1]) for i in range(len(orders))]
        return packs if parts is None else (packs, results[-1])

    def run_plainly(self, orders, n_ctx, count):
        blocks = [[] for _ in orders]
        for job in self.jobs:
            if job["left"] is None:
                blocks[job["group"]].append(self.arrays[job["plain"]].reshape(count, job["rows"], self.unit))
                continue
            for right, begin, half, _ in job["chunks"]:
                parts = []
                for core in (0, 1):
                    one = self.arrays[job["left"]]
                    if self.moves[right] is None:
                        two = self.arrays[right + core]
                    else:
                        two = swap(self.arrays[right]) if core else self.arrays[right]
                    two = lax.dynamic_slice_in_dim(two, begin + self.section * half, self.unit, 1)
                    parts.append(tm(swap(one) if core else one, two))
                value = (parts[0] + parts[1]).astype(BF16)
                blocks[job["group"]].append(value.reshape(count, job["rows"], self.unit))
        results = []
        for order, parts in zip(orders, blocks):
            shards = jnp.stack([shard_at(place, order, n_ctx) for place in range(count)])
            whole = jnp.take(jnp.concatenate(parts, axis=1), shards, axis=0)
            results.append((whole[count // 2 :], whole[: count // 2]))
        return results


def pack_kernel(jobs, moves, count, orders, n_ctx, beside, *refs):
    arrays, rest = refs[: len(moves)], refs[len(moves) :]
    if beside:
        parts_ref, rest, part_sems = rest[0], rest[1:-1], rest[-1]
    outs, rest = rest[: 2 * len(orders)], rest[2 * len(orders) :]
    if beside:
        back_ref, rest = rest[0], rest[1:]
    held, coming, semaphores = rest
    send_sems, recv_sems = semaphores
    section = lax.axis_index(SEC)
    unit = held.shape[1]
    barrier = pltpu.get_barrier_semaphore()
    pl.semaphore_signal(barrier, inc=1, device_id={SEC: 1 - section}, device_id_type=MESH)
    if beside:
        for hop in range(1, n_ctx):
            to = lax.rem(lax.axis_index(CTX) + hop, n_ctx)
            pl.semaphore_signal(barrier, inc=1, device_id={CTX: to}, device_id_type=MESH)
    pl.semaphore_wait(barrier, n_ctx if beside else 1)
    sides = []
    if beside:
        rows = parts_ref.shape[0] // (n_ctx - 1)
        for j in range(1, n_ctx):
            if j == middle_hop():
                continue
            at = slice((j - 1) * rows, j * rows)
            sems = [sem.at[j - 1] for sem in part_sems]
            sides.append(send(parts_ref.at[at, :], back_ref.at[at, :], n_ctx - j, *sems))
    places, copies, pending, nth, slot = {}, [], {}, 0, 0
    for index, move in enumerate(moves):
        if not move:
            continue
        target, at = coming[slot], 0
        places[index] = target
        pending[index] = []
        slot += 1
        for begin, half, width in move:
            source = arrays[index]
            if half:
                source = source.at[:, pl.ds(pl.multiple_of(begin + (1 - section) * half, 128), width)]
            copy = pltpu.make_async_remote_copy(
                src_ref=source,
                dst_ref=target.at[:, at : at + width] if half else target,
                send_sem=send_sems.at[nth],
                recv_sem=recv_sems.at[nth],
                device_id={SEC: 1 - section},
                device_id_type=MESH,
            )
            copy.start()
            copies.append(copy)
            pending[index].append(copy)
            at += width
            nth += 1
    for job in jobs:
        at, size = job["row"], job["rows"]
        total = count * size
        if job["left"] is None:
            held[0:total, :] = arrays[job["plain"]][...]
            chunks = [None]
        else:
            left, chunks = job["left"], job["chunks"]
            mine, theirs = [], []
            for index in [left] + [chunk[0] for chunk in chunks]:
                for copy in pending.pop(index, ()):
                    copy.wait_recv()
            for right, begin, half, there in chunks:
                if moves[right]:
                    column = pl.multiple_of(begin + section * half, 128)
                    mine.append(arrays[right][:, pl.ds(column, unit)])
                    theirs.append(places[right][:, there : there + unit])
                else:
                    mine.append(arrays[right][:, begin : begin + unit])
                    theirs.append(arrays[right + 1][:, begin : begin + unit])
            mine = jnp.concatenate(mine, axis=1)
            theirs = jnp.concatenate(theirs, axis=1)
            for begin in range(0, total, 768):
                span = slice(begin, begin + 768)
                value = tm(arrays[left][:, span], mine) + tm(places[left][:, span], theirs)
                for nth in range(len(chunks)):
                    held[nth * total + begin : nth * total + begin + 768, :] = value[
                        :, nth * unit : (nth + 1) * unit
                    ].astype(BF16)
        sent_ref, kept_ref = outs[2 * job["group"] : 2 * job["group"] + 2]
        for place in range(count):
            shard = shard_at(place, orders[job["group"]], n_ctx) * size
            target = kept_ref if place < count // 2 else sent_ref
            for nth in range(len(chunks)):
                begin = pl.multiple_of(shard + nth * total, 16)
                row = at + nth * size
                target[place % (count // 2), row : row + size, :] = held[pl.ds(begin, size), :]
    for copy in copies:
        copy.wait_send()
    for copy in sides:
        copy.wait()


class Halving:
    def __init__(self, packed, x_first):
        self.sent, self.kept = packed
        self.order = exchange_order(x_first)
        self.total = None

    def step(self, after):
        key, self.order = self.order[0], self.order[1:]
        got = flip(self.sent, *key)
        got, kept, after = lax.optimization_barrier((got, self.kept, after))
        if not self.order:
            self.total = kept[0].astype(F32) + got[0].astype(F32)
            self.total, after = lax.optimization_barrier((self.total, after))
            return after
        cut = kept.shape[0] // 2
        sent = (kept[cut:].astype(F32) + got[cut:].astype(F32)).astype(BF16)
        kept = (kept[:cut].astype(F32) + got[:cut].astype(F32)).astype(BF16)
        self.sent, self.kept, after = lax.optimization_barrier((sent, kept, after))
        return after


class Queue:
    def __init__(self):
        self.chains = []

    def add(self, chains):
        self.chains.extend(chains)

    def advance(self, value, layer, part):
        for chain in PLAN.get((layer, part), ()):
            if self.chains[chain].order:
                value = self.chains[chain].step(value)
        return value

    def round(self, after):
        for chain in TAIL:
            if self.chains[chain].order:
                after = self.chains[chain].step(after)
        return after

    def finish(self, after):
        while any(chain.order for chain in self.chains):
            after = self.round(after)
        return after


PLAN = {
    (1, 1): (0, 1),
    (0, 3): (0, 1),
    (0, 4): (0, 1, 2, 3),
    (0, 0): (0, 1, 2, 3),
    (0, 1): (4,),
}
TAIL = (0, 1, 2, 3, 4, 5, 6, 7)


def came_back(parts):
    n_ctx = lax.axis_size(CTX)
    rows = parts.shape[0] // (n_ctx - 1)
    return jnp.concatenate([turned(parts[(j - 1) * rows : j * rows], n_ctx - j) for j in range(1, n_ctx)])


def layer_backward(layer, w, saved, g_tok, g_chr, ids_both, live, group_row, column, seen, section, queue):
    rows, width = g_tok.shape
    count = lax.axis_size(DP) * lax.axis_size(CTX)
    unit = width // 2
    block = width // count
    d_feat, d_chr, d_states, around, sums_a = uniting_back(layer, w, g_tok, g_chr, saved, column, group_row)
    d_feat = queue.advance(d_feat, layer, 3)
    d_ffn, d_hidden, d_first, d_branch, d_attended, sums_b, inner_sums = feed_back(layer, w, d_feat, saved)
    d_attended = queue.advance(d_attended, layer, 4)
    early = Packing(section, unit, (True, False))
    taps = around.shape[1] // width
    right = early.operand(around, [(t * width, unit) for t in range(taps)])
    chunks = [(right, t * width, unit, t * unit) for t in range(taps)]
    early.product(0, early.operand(saved["joined"]), chunks, 2 * block)
    ups = d_hidden.shape[1] // 2
    right = early.operand(d_hidden, [(0, ups)])
    chunks = [(right, begin, ups, begin) for begin in range(0, ups, unit)]
    early.product(1, early.operand(saved["normed_low"]), chunks, block)
    right = early.operand(d_branch, [(0, unit)])
    early.product(1, early.operand(saved["attended"]), [(right, 0, unit, 0)], block)
    packs = early.run(0)
    packs, d_attended = lax.optimization_barrier((packs, d_attended))
    chains = [Halving(pack, x_first) for pack, x_first in zip(packs, early.groups)]
    queue.add(chains)
    dq, dk, dv = attend_back(
        saved["query"], saved["keys"], saved["values"], seen, saved["lse"], d_attended
    )
    dq = queue.advance(dq, layer, 0)
    if layer:
        d_states, dq = lax.optimization_barrier((d_states, dq))
    d_proj, d_c, proj_sums = chars_back(layer, w, d_states, d_chr, saved, live)
    dq, d_proj = lax.optimization_barrier((dq, d_proj))
    d_x, parts, sums_c = project_back(layer, w, d_first, dq, dk, dv)
    middle = middle_hop() - 1
    part_back = turned(parts[middle * rows : (middle + 1) * rows], lax.axis_size(CTX) - middle_hop())
    d_proj = queue.advance(d_proj, layer, 1)
    small = (
        jnp.stack([sums_c[0], sums_c[1], sums_b[5], sums_b[2], sums_a[0]]),
        inner_sums,
        jnp.stack([sums_b[3], sums_b[0], sums_a[1], sums_a[3]]),
        jnp.stack([sums_b[4], sums_b[1], sums_a[2], sums_a[4]]),
        proj_sums,
    )
    packed = jnp.concatenate(
        [jnp.swapaxes(p.reshape(p.shape[0], count, -1), 0, 1).reshape(count, -1) for p in small], axis=1
    )
    packed = jnp.pad(packed, ((0, 0), (0, 16 * unit - packed.shape[1])))
    late = Packing(section, unit, (True, False))
    right = late.operand(d_ffn, [(0, unit)])
    late.product(0, late.operand(saved["active"]), [(right, 0, unit, 0)], 4 * block)
    left = late.operand(d_c)
    split = w["table"][0].shape[0] // 2
    named = []
    for names in ids_both:
        names = names - section * split
        named.append((names == jnp.arange(2 * unit)[None, :]).astype(BF16))
    right = late.local(*named)
    late.product(0, left, [(right, 0, 0, 0), (right, unit, 0, 0)], block)
    right = late.operand(dq, [(0, unit)])
    late.product(1, late.operand(saved["x"]), [(right, 0, unit, 0)], block)
    rights = [late.operand(grad, [(0, unit)]) for grad in (dk, dv)]
    late.product(1, late.operand(saved["x_all"]), [(right, 0, unit, 0) for right in rights], block)
    right = late.operand(d_proj, [(0, width)])
    chunks = [(right, begin, width, begin) for begin in range(0, width, unit)]
    late.product(1, late.operand(saved["chars_low"]), chunks, block)
    late.plain(1, packed.astype(BF16).reshape(-1, unit), 16)
    packs, back = late.run(1, parts)
    packs, d_c, back = lax.optimization_barrier((packs, d_c, back))
    g_x = d_x + part_back.astype(F32)
    for j in range(len(back) // rows):
        if j != middle:
            g_x = g_x + back[j * rows : (j + 1) * rows].astype(F32)
    g_x = g_x.astype(BF16)
    more = [Halving(pack, x_first) for pack, x_first in zip(packs, late.groups)]
    queue.add(more)
    d_c = queue.advance(d_c, layer, 2)
    sizes = [(p.shape[0], p.size // count // p.shape[0]) for p in small]
    return g_x, d_c, chains + more, sizes


def on_device(
    ends, char_ends, char_ids, groups, lengths, w_qkv, biases, w_out, w_up, b_up, w_down,
    ln_gain, ln_shift, char_table, w_gru, b_gru, w_conv,
):
    section = lax.axis_index(SEC)
    n_dp, n_ctx = lax.axis_size(DP), lax.axis_size(CTX)
    is_first = section == 0
    def turned_rows(value):
        shape = value.shape
        return jnp.swapaxes(value.reshape((shape[0], CHUNKS, -1) + shape[2:]), 1, 2).reshape(shape)

    padded = jnp.pad(char_table[0], ((0, -char_table.shape[1] % 256), (0, 0)))
    rows_16 = jnp.concatenate([biases[0], ln_gain[0], ln_shift[0], jnp.zeros_like(biases[0, :3])])
    inner_own = jnp.concatenate([b_up, b_gru], axis=1)
    indices = turned_rows(jnp.concatenate([char_ids, groups]))
    (
        x, cot_tok, c, cot_chr, vec0, vec1, inner0, inner1, ids, ids_other, live, group_row, column, seen,
        gru_other, table_other,
    ) = deal(lengths, ends[0], turned_rows(char_ends[0]), indices, rows_16, inner_own, w_gru[0], padded)
    ids_both = (ids, ids_other)
    weights = {"gru": (w_gru[0], gru_other), "table": (padded, table_other)}
    for name, own in (
        ("qkv", w_qkv[0]), ("out", w_out[0]), ("up", w_up[0]), ("down", w_down[0]),
        ("conv", w_conv[0].reshape(-1, w_conv.shape[3])),
    ):
        tied, x = lax.optimization_barrier((own, x))
        weights[name] = (own, swap(tied))
    layers = [
        dict(weights, vec=vec, b_up=inner[:, : b_up.shape[1]], b_gru=inner[:, b_up.shape[1] :])
        for vec, inner in ((vec0, inner0), (vec1, inner1))
    ]
    rows, width = x.shape

    kept = []
    for layer in (0, 1):
        x, c, saved = layer_forward(
            layer, layers[layer], x, c, ids, live, group_row, column, seen
        )
        kept.append(saved)
    g_x, g_c = cot_tok, cot_chr
    queue = Queue()
    chains = [None, None]
    for layer in (1, 0):
        g_x, g_c, chains[layer], sizes = layer_backward(
            layer, layers[layer], kept[layer], g_x, g_c, ids_both, live, group_row, column, seen, section, queue
        )
    queue.finish(jnp.zeros((), F32))
    packs = [[chain.total for chain in four] for four in chains]

    def gathered(grad, value):
        got = swap(jnp.where(is_first, value, grad))
        return jnp.where(is_first, jnp.stack([grad, got]), jnp.stack([got, value]))[None]

    ends_out = gathered(g_x, x)
    char_ends_out = gathered(restore(g_c), restore(c))

    both = []
    for one, two in zip(*packs):
        mine = jnp.where(is_first, one, two)
        got = swap(jnp.where(is_first, two, one))
        both.append((jnp.where(is_first, mine, got), jnp.where(is_first, got, mine)))
    block = width // (n_dp * n_ctx)

    def columns(which, at, size, parts, crossed=False):
        cut = [[half[at + i * size : at + (i + 1) * size] for i in range(parts)] for half in both[which]]
        if crossed:
            return jnp.concatenate([half[i] for i in range(parts) for half in cut], axis=1)
        return jnp.concatenate(cut[0] + cut[1], axis=1)

    d_conv = jnp.stack([columns(0, tap * 2 * block, 2 * block, 1) for tap in range(w_conv.shape[1])])
    ups = w_up.shape[2] // width
    d_up = columns(1, 0, block, ups)
    d_out = columns(1, ups * block, block, 1)
    d_down = columns(2, 0, ups * block, 1)
    at = ups * block
    split = padded.shape[0] // 2
    d_table = jnp.concatenate(
        [
            jnp.concatenate([half[at : at + block], half[at + block : at + 2 * block]], axis=1)[:, :take]
            for half, take in zip(both[2], (split, char_table.shape[1] - split))
        ],
        axis=1,
    ).T
    d_qkv = columns(3, 0, block, 3, True)
    d_gru = columns(3, 3 * block, block, 2)
    vectors = (both[3][0][5 * block :] + both[3][1][5 * block :]).reshape(-1)
    sums, at = [], 0
    for parts, size in sizes:
        sums.append(vectors[at : at + parts * size].reshape(parts, size))
        at += parts * size
    return (
        ends_out,
        char_ends_out,
        d_qkv[None],
        sums[0][None],
        d_out[None],
        d_up[None],
        sums[1],
        d_down[None],
        sums[2][None],
        sums[3][None],
        d_table[None],
        d_gru[None],
        sums[4],
        d_conv[None],
    )


def solution(mesh):
    both = (DP, CTX)
    held, rows, columns = P(SEC, DP, CTX), P(SEC, both), P(SEC, None, both)
    layer = P(SEC)
    in_specs = (held, held, P(DP, CTX), P(DP, CTX), P(DP)) + (layer,) * 12
    out_specs = (
        held, held, rows, columns, rows, rows, rows, rows, columns, columns, columns, rows, rows, columns,
    )
    return jax.shard_map(
        on_device, mesh=mesh, in_specs=in_specs, out_specs=out_specs, check_vma=False
    )
```

```python
import functools

import jax
import jax.numpy as jnp
from jax import lax
from jax.experimental import pallas as pl
from jax.experimental.pallas import tpu as pltpu
from jax.sharding import PartitionSpec as P

HEADS = 12
CHUNKS = 8
NORM_EPS = 1e-06
MASKED = -1000000000.0
SEC, DP, CTX = "section", "dp", "ctx"
F32, BF16 = jnp.float32, jnp.bfloat16
MIB = 2**20


def contract(left, right, dims):
    return lax.dot_general(left, right, (dims, ((), ())), preferred_element_type=F32)


def mm(left, right):
    return contract(left, right, ((1,), (0,)))


def mt(left, right):
    return contract(left, right, ((1,), (1,)))


def tm(left, right):
    return contract(left, right, ((0,), (0,)))


def flip(value, axis, bit):
    return lax.ppermute(value, axis, [(i, i ^ (1 << bit)) for i in range(lax.axis_size(axis))])


def swap(value):
    return flip(value, SEC, 0)


def turned(value, by):
    count = lax.axis_size(CTX)
    return lax.ppermute(value, CTX, [(i, (i + by) % count) for i in range(count)])


def pick(value, index, axis=0):
    return lax.dynamic_index_in_dim(value, index, axis, keepdims=False)


def interleave(value):
    rows = value.shape[0]
    return jnp.swapaxes(
        value.reshape((CHUNKS, rows // CHUNKS) + value.shape[1:]), 0, 1
    ).reshape(value.shape)


def restore(value):
    rows = value.shape[0]
    return jnp.swapaxes(
        value.reshape((rows // CHUNKS, CHUNKS) + value.shape[1:]), 0, 1
    ).reshape(value.shape)


def params(mib):
    return pltpu.CompilerParams(vmem_limit_bytes=mib * MIB)


def attend_back_kernel(
    size, q_ref, k_ref, v_ref, seen_ref, lse_ref, do_ref, dq_ref, dk_ref, dv_ref
):
    seen = seen_ref[...] > 0.0
    scale = size**-0.5
    for head in range(q_ref.shape[1] // size):
        at = slice(head * size, (head + 1) * size)
        query, keys, grad = q_ref[:, at], k_ref[:, at], do_ref[:, at]
        scores = jnp.where(seen, mt(keys, query), MASKED)
        probs = jnp.exp(scores - lse_ref[0, head : head + 1, :])
        g_probs = mt(v_ref[:, at], grad)
        row = jnp.sum(g_probs * probs, axis=0, keepdims=True)
        g_scores = (probs * (g_probs - row)).astype(BF16)
        dv_ref[:, at] = mm(probs.astype(BF16), grad).astype(BF16)
        dk_ref[:, at] = mm(g_scores, query).astype(BF16)
        dq_ref[:, at] = (tm(g_scores, keys) * scale).astype(BF16)


def attend_back(query, keys, values, seen, lse, grad):
    rows, width = query.shape
    count = keys.shape[0]
    size = width // HEADS
    block = 2 * size
    steps = width // block
    by_rows = pl.BlockSpec((rows, block), lambda i: (0, i))
    by_keys = pl.BlockSpec((count, block), lambda i: (0, i))
    return pl.pallas_call(
        functools.partial(attend_back_kernel, size),
        grid=(steps,),
        in_specs=[
            by_rows,
            by_keys,
            by_keys,
            pl.BlockSpec((count, 1), lambda i: (0, 0)),
            pl.BlockSpec((1, 8, rows), lambda i: (i, 0, 0)),
            by_rows,
        ],
        out_specs=[by_rows, by_keys, by_keys],
        out_shape=[
            jax.ShapeDtypeStruct((rows, width), BF16),
            jax.ShapeDtypeStruct((count, width), BF16),
            jax.ShapeDtypeStruct((count, width), BF16),
        ],
        compiler_params=params(40),
        cost_estimate=pl.CostEstimate(flops=1, bytes_accessed=1, transcendentals=0),
    )(query, keys, values, seen, lse, grad)


MESH = pl.DeviceIdType.MESH


def fetch(layer, own, other, target, semaphore):
    section = lax.axis_index(SEC)
    copies = [pltpu.make_async_copy(source, target, semaphore) for source in (own, other)]

    @pl.when(section == layer)
    def _():
        copies[0].start()

    @pl.when(section != layer)
    def _():
        copies[1].start()

    return copies[0]


def greet(hops):
    barrier = pltpu.get_barrier_semaphore()
    count = lax.axis_size(CTX)
    for hop in hops:
        to = lax.rem(lax.axis_index(CTX) + hop, count)
        pl.semaphore_signal(barrier, inc=1, device_id={CTX: to}, device_id_type=MESH)
    pl.semaphore_wait(barrier, len(hops))


def send(source, target, hop, send_sem, recv_sem):
    to = lax.rem(lax.axis_index(CTX) + hop, lax.axis_size(CTX))
    copy = pltpu.make_async_remote_copy(
        src_ref=source, dst_ref=target, send_sem=send_sem, recv_sem=recv_sem,
        device_id={CTX: to}, device_id_type=MESH,
    )
    copy.start()
    return copy


class Relay:
    def __init__(self, source, slots, sems):
        self.source, self.slots, self.sems = source, slots, sems
        self.rows, self.count, self.place = source.shape[0], lax.axis_size(CTX), lax.axis_index(CTX)

    def slot(self, j):
        return self.slots.at[j * self.rows : (j + 1) * self.rows, :]

    def copies(self, step):
        n, me = self.count, self.place
        right = (me < n - 1) & (me >= step - 1)
        left = (me > 0) & (me <= n - step)
        for nth, (there, going, to, slot, held) in enumerate(
            ((1, right, step, step, step - 1), (n - 1, left, n - step, n - step, n - step + 1))
        ):
            source = self.source if step == 1 else self.slot(held)
            copy = pltpu.make_async_remote_copy(
                src_ref=source, dst_ref=self.slot(slot),
                send_sem=self.sems[0].at[2 * step - 2 + nth], recv_sem=self.sems[1].at[slot - 1],
                device_id={CTX: lax.rem(me + there, n)}, device_id_type=MESH,
            )
            yield going, held, copy

    def wait(self, slot):
        pltpu.make_async_remote_copy(
            src_ref=self.source, dst_ref=self.slot(slot),
            send_sem=self.sems[0].at[0], recv_sem=self.sems[1].at[slot - 1],
            device_id={CTX: lax.rem(self.place + 1, self.count)}, device_id_type=MESH,
        ).wait_recv()

    def start(self, step):
        for nth, (going, held, copy) in enumerate(self.copies(step)):
            if step > 1:
                came = (self.place >= step - 1) if nth == 0 else (self.place <= self.count - step)
                pl.when(came)(functools.partial(self.wait, held))
            pl.when(going)(copy.start)

    def finish(self):
        n, me = self.count, self.place
        pl.when(me == n - 1)(functools.partial(self.wait, n - 1))
        pl.when(me == 0)(functools.partial(self.wait, 1))
        for step in range(1, n):
            for going, _, copy in self.copies(step):
                pl.when(going)(copy.wait_send)


def unit_of(values):
    centred = values - jnp.mean(values, axis=1, keepdims=True)
    scale = lax.rsqrt(jnp.mean(centred * centred, axis=1, keepdims=True) + NORM_EPS)
    return centred * scale, scale


def unit_back(unit, scale, inner):
    mean = jnp.mean(inner, axis=1, keepdims=True)
    along = jnp.mean(inner * unit, axis=1, keepdims=True)
    return scale * (inner - mean - unit * along)


def gelu_pair(values):
    size = jnp.abs(values)
    bell = jnp.exp(-0.5 * values * values)
    t = 1.0 / (1.0 + (0.3275911 * 0.7071067811865476) * size)
    poly = t * (
        0.254829592 + t * (-0.284496736 + t * (1.421413741 + t * (-1.453152027 + t * 1.061405429)))
    )
    tail = 0.5 * poly * bell
    cdf = jnp.where(values >= 0.0, 1.0 - tail, tail)
    return values * cdf, cdf + values * (bell * 0.3989422804014327)


def gates(proj_ref, live_ref, at, rate, width):
    live = live_ref[at, :] > 0.0
    opened = jax.nn.sigmoid(proj_ref[at, rate : rate + width])
    return jnp.where(live, 1.0 - opened, 1.0), live, opened


def step_rows(step):
    return pl.ds(pl.multiple_of(step * CHUNKS, CHUNKS), CHUNKS)


def join_chunks(carry_ref, total_ref, slot, state, decay, order):
    width = state.shape[1]
    before = jnp.zeros((1, width), F32)
    faded = jnp.ones((1, width), F32)
    for chunk in order:
        carry_ref[slot, chunk : chunk + 1, :] = before
        carry_ref[slot + 1, chunk : chunk + 1, :] = faded
        own = decay[chunk : chunk + 1, :]
        before = own * before + state[chunk : chunk + 1, :]
        faded = own * faded
    total_ref[slot : slot + 1, :] = before
    total_ref[slot + 1 : slot + 2, :] = faded
    if slot:
        total_ref[4:8, :] = jnp.zeros((4, width), F32)


def entering_chunks(carry_ref, total_ref, inbox_ref, sems, reverse):
    count, place = lax.axis_size(CTX), lax.axis_index(CTX)
    width = total_ref.shape[1]
    copies = [
        send(total_ref, inbox_ref.at[j - 1], j, sems[0].at[j - 1], sems[1].at[j - 1])
        for j in range(1, count)
    ]
    for copy in copies:
        copy.wait()
    entering = []
    for slot in (0, 2):
        so_far = jnp.zeros((1, width), F32)
        rising = (slot == 0) != reverse
        for hop in range(count - 1, 0, -1):
            there = inbox_ref.at[(hop if rising else count - hop) - 1]
            valid = (place >= hop) if rising else (place + hop < count)
            longer = there[slot + 1 : slot + 2, :] * so_far + there[slot : slot + 1, :]
            so_far = jnp.where(valid, longer, so_far)
        entering.append(carry_ref[slot] + carry_ref[slot + 1] * so_far)
    return entering


def by_step(values):
    return values.reshape(values.shape[0] // CHUNKS, CHUNKS, values.shape[1])


def chars_kernel(
    layer, x_ref, c_ref, ids_ref, live_ref, group_ref, bias_ref, table_a, table_b, gru_a, gru_b,
    all_ref, chars_ref, low_ref, proj_ref, state_ref, entering_ref, pooled_ref,
    table_v, gru_v, decay_ref, carry_ref, total_ref, inbox_ref, fetch_sems, x_sems, total_sems,
):
    count = lax.axis_size(CTX)
    rows = x_ref.shape[0]
    width = proj_ref.shape[1] // 4
    steps = proj_ref.shape[0] // CHUNKS
    table = fetch(layer, table_a, table_b, table_v, fetch_sems.at[0])
    gru = fetch(layer, gru_a, gru_b, gru_v, fetch_sems.at[1])
    greet(range(1, count))
    relay = Relay(x_ref, all_ref, x_sems)
    relay.start(1)
    all_ref[0:rows, :] = x_ref[...]
    table.wait()
    names = lax.broadcasted_iota(jnp.int32, (c_ref.shape[0], table_v.shape[0]), 1)
    named = jnp.where(names == ids_ref[...], 1.0, 0.0).astype(BF16)
    chars = c_ref[...].astype(F32) + mm(named, table_v[...])
    chars_ref[...] = chars
    low_ref[...] = chars.astype(BF16)
    gru.wait()
    proj_ref[...] = mm(low_ref[...], gru_v[...]) + bias_ref[...]
    relay.start(2)
    unroll = 8

    def step(i, carry):
        state_f, decay_f, state_b, decay_b = carry
        for u in range(unroll):
            at = step_rows(i * unroll + u)
            keep, live, opened = gates(proj_ref, live_ref, at, 0, width)
            inflow = jnp.where(live, opened * proj_ref[at, width : 2 * width], 0.0)
            state_f = keep * state_f + inflow
            decay_f = keep * decay_f
            state_ref[at, 0:width] = state_f
            decay_ref[at, 0:width] = decay_f
            at = step_rows(steps - 1 - i * unroll - u)
            keep, live, opened = gates(proj_ref, live_ref, at, 2 * width, width)
            inflow = jnp.where(live, opened * proj_ref[at, 3 * width : 4 * width], 0.0)
            state_b = keep * state_b + inflow
            decay_b = keep * decay_b
            state_ref[at, width : 2 * width] = state_b
            decay_ref[at, width : 2 * width] = decay_b
        return state_f, decay_f, state_b, decay_b

    zero = jnp.zeros((CHUNKS, width), F32)
    one = jnp.ones((CHUNKS, width), F32)
    state_f, decay_f, state_b, decay_b = lax.fori_loop(
        0, steps // unroll, step, (zero, one, zero, one)
    )
    join_chunks(carry_ref, total_ref, 0, state_f, decay_f, range(CHUNKS))
    join_chunks(carry_ref, total_ref, 2, state_b, decay_b, range(CHUNKS - 1, -1, -1))
    entering = entering_chunks(carry_ref, total_ref, inbox_ref, total_sems, False)
    for side, carried in enumerate(entering):
        at = slice(side * width, (side + 1) * width)
        entering_ref[:, at] = carried
        whole = by_step(state_ref[:, at]) + by_step(decay_ref[:, at]) * carried[None]
        state_ref[:, at] = whole.reshape(steps * CHUNKS, width)
    tokens = lax.broadcasted_iota(jnp.int32, (rows, group_ref.shape[1]), 0)
    onehot = jnp.where(tokens == group_ref[...], 1.0, 0.0)
    counts = jnp.sum(onehot, axis=1, keepdims=True)
    pooled_ref[...] = (mm(onehot.astype(BF16), state_ref[...].astype(BF16)) / counts).astype(BF16)
    for step in range(3, count):
        relay.start(step)
    relay.finish()


VMEM_SPEC = pl.BlockSpec(memory_space=pltpu.VMEM)
ANY_SPEC = pl.BlockSpec(memory_space=pl.ANY)
DMA = pltpu.SemaphoreType.DMA


def call(kernel, plain, weights, outs, scratch, collective_id=None):
    options = {} if collective_id is None else dict(collective_id=collective_id, has_side_effects=True)
    return pl.pallas_call(
        kernel,
        in_specs=[VMEM_SPEC] * len(plain) + [ANY_SPEC] * len(weights),
        out_specs=[VMEM_SPEC] * len(outs),
        out_shape=[jax.ShapeDtypeStruct(*o) for o in outs],
        scratch_shapes=scratch,
        compiler_params=pltpu.CompilerParams(vmem_limit_bytes=58 * MIB, **options),
        cost_estimate=pl.CostEstimate(flops=1, bytes_accessed=1, transcendentals=0),
    )(*plain, *weights)


def room(weight):
    return pltpu.VMEM(weight.shape, weight.dtype)


def deal_kernel(
    lengths_ref, e_ref, ce_ref, rows_ref, columns_ref, vec_ref, inner_ref, gru_ref, table_ref,
    x_ref, cot_ref, c_ref, ccot_ref, vec0_ref, vec1_ref, inner0_ref, inner1_ref,
    ids_ref, other_ref, live_ref, row_ref, column_ref, seen_ref, gru_out, table_out,
    e_in, ce_in, vec_in, inner_in, sems,
):
    section, place = lax.axis_index(SEC), lax.axis_index(CTX)
    rows = x_ref.shape[0]
    barrier = pltpu.get_barrier_semaphore()
    pl.semaphore_signal(barrier, inc=1, device_id={SEC: 1 - section}, device_id_type=MESH)
    pl.semaphore_wait(barrier, 1)
    copies = []
    for nth, (source, target) in enumerate(
        (
            (e_ref.at[1 - section], e_in), (ce_ref.at[1 - section], ce_in), (vec_ref, vec_in),
            (inner_ref, inner_in), (table_ref, table_out), (gru_ref, gru_out),
        )
    ):
        copy = pltpu.make_async_remote_copy(
            src_ref=source, dst_ref=target, send_sem=sems[0].at[nth], recv_sem=sems[1].at[nth],
            device_id={SEC: 1 - section}, device_id_type=MESH,
        )
        copy.start()
        copies.append(copy)
    first = section == 0
    ids_ref[...] = jnp.where(first, columns_ref[:, 0:1], columns_ref[:, 1:2])
    other_ref[...] = jnp.where(first, columns_ref[:, 1:2], columns_ref[:, 0:1])
    group = jnp.where(first, columns_ref[:, 2:3], columns_ref[:, 3:4])
    live_ref[...] = jnp.where(group >= 0, 1.0, 0.0)
    column_ref[...] = group - place * rows
    row_ref[...] = jnp.where(first, rows_ref[2:3, :], rows_ref[3:4, :]) - place * rows
    length = jnp.where(first, lengths_ref[0], lengths_ref[1])
    count = lax.axis_size(CTX)
    for j in range(count):
        spots = lax.broadcasted_iota(jnp.int32, (rows, 1), 0) + lax.rem(place - j + count, count) * rows
        seen_ref[j * rows : (j + 1) * rows, :] = jnp.where(spots < length, 1.0, 0.0)
    for copy in copies:
        copy.wait()
    x_ref[...] = jnp.where(first, e_ref[0], e_in[...])
    cot_ref[...] = jnp.where(first, e_in[...], e_ref[1])
    c_ref[...] = jnp.where(first, ce_ref[0], ce_in[...])
    ccot_ref[...] = jnp.where(first, ce_in[...], ce_ref[1])
    vec0_ref[...] = jnp.where(first, vec_ref[...], vec_in[...])
    vec1_ref[...] = jnp.where(first, vec_in[...], vec_ref[...])
    inner0_ref[...] = jnp.where(first, inner_ref[...], inner_in[...])
    inner1_ref[...] = jnp.where(first, inner_in[...], inner_ref[...])


def deal(lengths, e, ce, indices, vec, inner, gru, table):
    _, rows, width = e.shape
    slots, keys = ce.shape[1], rows * lax.axis_size(CTX)
    tok, char = ((rows, width), BF16), ((slots, width), BF16)
    thin = ((slots, 1), jnp.int32)
    outs = [
        tok, tok, char, char, (vec.shape, F32), (vec.shape, F32), (inner.shape, F32), (inner.shape, F32),
        thin, thin, ((slots, 1), F32), ((1, slots), jnp.int32), thin, ((keys, 1), F32),
        (gru.shape, BF16), (table.shape, BF16),
    ]
    plain = [e, ce, indices, indices.T, vec, inner]
    return pl.pallas_call(
        deal_kernel,
        in_specs=[pl.BlockSpec(memory_space=pltpu.SMEM)] + [VMEM_SPEC] * len(plain) + [ANY_SPEC] * 2,
        out_specs=[VMEM_SPEC] * 14 + [ANY_SPEC] * 2,
        out_shape=[jax.ShapeDtypeStruct(*o) for o in outs],
        scratch_shapes=[
            pltpu.VMEM(*tok), pltpu.VMEM(*char), pltpu.VMEM(vec.shape, F32), pltpu.VMEM(inner.shape, F32),
            [DMA((6,))] * 2,
        ],
        compiler_params=pltpu.CompilerParams(
            vmem_limit_bytes=58 * MIB, collective_id=10, has_side_effects=True
        ),
        cost_estimate=pl.CostEstimate(flops=1, bytes_accessed=1, transcendentals=0),
    )(lengths, *plain, gru, table)


def chars_forward(layer, w, x, c, ids, live, group):
    rows, width = x.shape
    slots = c.shape[0]
    count = lax.axis_size(CTX)
    half = width // 2
    outs = [
        ((count * rows, width), BF16), ((slots, width), F32), ((slots, width), BF16),
        ((slots, 4 * half), F32), ((slots, width), F32), ((CHUNKS, width), F32), ((rows, width), BF16),
    ]
    pair = [DMA((count - 1,))] * 2
    scratch = [
        room(w["table"][0]), room(w["gru"][0]), pltpu.VMEM((slots, width), F32),
        pltpu.VMEM((4, CHUNKS, half), F32), pltpu.VMEM((8, half), F32),
        pltpu.VMEM((count - 1, 8, half), F32), DMA((2,)), [DMA((2 * count - 2,)), DMA((count - 1,))], pair,
    ]
    return call(
        functools.partial(chars_kernel, layer), [x, c, ids, live, group, w["b_gru"]],
        [*w["table"], *w["gru"]], outs, scratch, 2 + layer,
    )


def heads_of(block, size, head):
    lanes = lax.broadcasted_iota(jnp.int32, block.shape, 1)
    return jnp.where(lanes // size == head, block, jnp.zeros_like(block))


def tokens_kernel(
    layer, size, x_ref, seen_ref, vec_ref, bias_ref,
    qkv_a, qkv_b, out_a, out_b, up_a, up_b, down_a, down_b,
    q_ref, k_ref, v_ref, lse_ref, att_ref, unit1_ref, scale1_ref, low_ref, active_ref, slope_ref,
    unit2_ref, scale2_ref, features_ref,
    qkv_v, out_v, up_v, down_v, scores_ref, sems,
):
    rows, width = q_ref.shape
    keys = x_ref.shape[0]
    waits = [
        fetch(layer, a, b, v, sems.at[i])
        for i, (a, b, v) in enumerate(
            [(qkv_a, qkv_b, qkv_v), (out_a, out_b, out_v), (up_a, up_b, up_v), (down_a, down_b, down_v)]
        )
    ]
    waits[0].wait()
    query = (mm(x_ref[0:rows, :], qkv_v[:, 0:width]) + vec_ref[0:1, :]).astype(BF16)
    q_ref[...] = query * jnp.asarray(size**-0.5, BF16)
    for begin in range(0, keys, 256):
        at = slice(begin, begin + 256)
        k_ref[at, :] = mm(x_ref[at, :], qkv_v[:, width : 2 * width]).astype(BF16)
        v_ref[at, :] = (mm(x_ref[at, :], qkv_v[:, 2 * width : 3 * width]) + vec_ref[1:2, :]).astype(BF16)
    block = 128
    heads = block // size

    def pair(i, carry):
        at = pl.ds(pl.multiple_of(i * block, block), block)
        query = q_ref[:, at]
        lanes = lax.broadcasted_iota(jnp.int32, (rows, block), 1)
        result = None
        for head in range(heads):
            mine = heads_of(query, size, head)
            top = jnp.full((1, rows), MASKED, F32)
            for begin in range(0, keys, 256):
                span = slice(begin, begin + 256)
                scores = mt(k_ref[span, at], mine)
                scores = jnp.where(seen_ref[span, :] > 0.0, scores, MASKED)
                scores_ref[span, :] = scores
                top = jnp.maximum(top, jnp.max(scores, axis=0, keepdims=True))
            total = jnp.zeros((1, rows), F32)
            for begin in range(0, keys, 256):
                span = slice(begin, begin + 256)
                weights = jnp.exp(scores_ref[span, :] - top)
                scores_ref[span, :] = weights
                total = total + jnp.sum(weights, axis=0, keepdims=True)
            lse_ref[i, head : head + 1, :] = top + jnp.log(total)
            share = 1.0 / total
            mixed = jnp.zeros((rows, block), F32)
            for begin in range(0, keys, 256):
                span = slice(begin, begin + 256)
                probs = (scores_ref[span, :] * share).astype(BF16)
                mixed = mixed + tm(probs, v_ref[span, at])
            result = mixed if head == 0 else jnp.where(lanes // size == head, mixed, result)
        att_ref[:, at] = result.astype(BF16)
        return carry

    lax.fori_loop(0, width // block, pair, 0)
    waits[1].wait()
    first = x_ref[0:rows, :].astype(F32) + mm(att_ref[...], out_v[...]) + vec_ref[2:3, :]
    unit, scale = unit_of(first)
    unit1_ref[...] = unit
    scale1_ref[...] = scale
    normed = unit * vec_ref[5:6, :] + vec_ref[9:10, :]
    low_ref[...] = normed.astype(BF16)
    waits[2].wait()
    waits[3].wait()
    second = normed + vec_ref[3:4, :]
    for begin in range(0, active_ref.shape[1], width):
        at = slice(begin, begin + width)
        hidden = mm(low_ref[...], up_v[:, at]) + bias_ref[:, at]
        active, slope = gelu_pair(hidden)
        active_ref[:, at] = active.astype(BF16)
        slope_ref[:, at] = slope.astype(BF16)
        second = second + mm(active_ref[:, at], down_v[at, :])
    unit, scale = unit_of(second)
    unit2_ref[...] = unit
    scale2_ref[...] = scale
    features_ref[...] = unit * vec_ref[6:7, :] + vec_ref[10:11, :]


def tokens_forward(layer, w, x_all, seen, rows):
    keys, width = x_all.shape
    inner = w["up"][0].shape[1]
    size = width // HEADS
    outs = [
        ((rows, width), BF16), ((keys, width), BF16), ((keys, width), BF16), ((width // 128, 8, rows), F32),
        ((rows, width), BF16), ((rows, width), F32), ((rows, 1), F32), ((rows, width), BF16),
        ((rows, inner), BF16), ((rows, inner), BF16), ((rows, width), F32), ((rows, 1), F32),
        ((rows, width), F32),
    ]
    names = ("qkv", "out", "up", "down")
    scratch = [room(w[name][0]) for name in names] + [pltpu.VMEM((keys, rows), F32), DMA((4,))]
    return call(
        functools.partial(tokens_kernel, layer, size), [x_all, seen, w["vec"], w["b_up"]],
        [a for name in names for a in w[name]], outs, scratch,
    )


def edges(values_ref, before_ref, after_ref, sems):
    rows, count = values_ref.shape[0], lax.axis_size(CTX)
    return [
        send(values_ref.at[rows - 16 : rows, :], before_ref, 1, sems[0].at[0], sems[1].at[0]),
        send(values_ref.at[0:16, :], after_ref, count - 1, sems[0].at[1], sems[1].at[1]),
    ]


def moved(values, edge, by):
    rows = values.shape[0]
    at = lax.broadcasted_iota(jnp.int32, values.shape, 0)
    rolled = pltpu.roll(values, by % rows, 0)
    return jnp.where(at == (0 if by > 0 else rows - 1), edge, rolled)


def edge_masks():
    place = lax.axis_index(CTX)
    before = jnp.where(place > 0, 1.0, 0.0)
    after = jnp.where(place < lax.axis_size(CTX) - 1, 1.0, 0.0)
    return before, after


def uniting_kernel(
    layer, features_ref, pooled_ref, chars_ref, state_ref, column_ref, vec_ref, conv_a, conv_b,
    tok_ref, chr_ref, joined_ref, slope_ref, unit3_ref, scale3_ref, unit4_ref, scale4_ref,
    conv_v, before_ref, after_ref, fetch_sem, sems,
):
    rows, width = features_ref.shape
    conv = fetch(layer, conv_a, conv_b, conv_v, fetch_sem.at[0])
    joined_ref[:, 0:width] = features_ref[...].astype(BF16)
    joined_ref[:, width : 2 * width] = pooled_ref[...]
    greet((1, lax.axis_size(CTX) - 1))
    copies = edges(joined_ref, before_ref, after_ref, sems)
    conv.wait()
    deep = 2 * width
    taps = [conv_v.at[tap * deep : (tap + 1) * deep, :] for tap in range(3)]
    joined = joined_ref[...]
    mixed = mm(joined, taps[1][...]) + vec_ref[4:5, :]
    lower = mm(joined, taps[0][...])
    upper = mm(joined, taps[2][...])
    for copy in copies:
        copy.wait()
    has_before, has_after = edge_masks()
    edge = mm(before_ref[...], taps[0][...])[15:16, :] * has_before
    mixed = mixed + moved(lower, edge, 1)
    edge = mm(after_ref[...], taps[2][...])[0:1, :] * has_after
    mixed = mixed + moved(upper, edge, -1)
    lifted, slope = gelu_pair(mixed)
    slope_ref[...] = slope
    unit, scale = unit_of(features_ref[...] + lifted)
    unit3_ref[...] = unit
    scale3_ref[...] = scale
    tok_ref[...] = (unit * vec_ref[7:8, :] + vec_ref[11:12, :]).astype(BF16)
    slots = column_ref.shape[0]
    tokens = lax.broadcasted_iota(jnp.int32, (slots, rows), 1)
    onehot = jnp.where(tokens == column_ref[...], 1.0, 0.0).astype(BF16)
    unit, scale = unit_of(chars_ref[...] + state_ref[...] + mm(onehot, lifted.astype(BF16)))
    unit4_ref[...] = unit
    scale4_ref[...] = scale
    chr_ref[...] = (unit * vec_ref[8:9, :] + vec_ref[12:13, :]).astype(BF16)


def uniting_forward(layer, w, features, pooled, chars, states, column):
    rows, width = features.shape
    slots = chars.shape[0]
    outs = [
        ((rows, width), BF16), ((slots, width), BF16), ((rows, 2 * width), BF16), ((rows, width), F32),
        ((rows, width), F32), ((rows, 1), F32), ((slots, width), F32), ((slots, 1), F32),
    ]
    edge = pltpu.VMEM((16, 2 * width), BF16)
    scratch = [room(w["conv"][0]), edge, edge, DMA((1,)), [DMA((2,))] * 2]
    return call(
        functools.partial(uniting_kernel, layer), [features, pooled, chars, states, column, w["vec"]],
        [*w["conv"]], outs, scratch, 4 + layer,
    )


def uniting_back_kernel(
    layer, gt_ref, gc_ref, unit3_ref, scale3_ref, unit4_ref, scale4_ref, slope_ref, column_ref, group_ref,
    vec_ref, conv_a, conv_b,
    feat_ref, chr_ref, states_ref, around_ref, sums_ref,
    conv_v, mixed_ref, before_ref, after_ref, fetch_sem, sems,
):
    rows, width = gt_ref.shape
    slots = gc_ref.shape[0]
    conv = fetch(layer, conv_a, conv_b, conv_v, fetch_sem.at[0])
    grad = gt_ref[...].astype(F32)
    unit = unit3_ref[...]
    sums_ref[1:2, :] = jnp.sum(grad * unit, axis=0, keepdims=True)
    sums_ref[2:3, :] = jnp.sum(grad, axis=0, keepdims=True)
    d_tok = unit_back(unit, scale3_ref[...], grad * vec_ref[7:8, :])
    grad = gc_ref[...].astype(F32)
    unit = unit4_ref[...]
    sums_ref[3:4, :] = jnp.sum(grad * unit, axis=0, keepdims=True)
    sums_ref[4:5, :] = jnp.sum(grad, axis=0, keepdims=True)
    d_chr = unit_back(unit, scale4_ref[...], grad * vec_ref[8:9, :])
    chr_ref[...] = d_chr
    tokens = lax.broadcasted_iota(jnp.int32, (rows, slots), 0)
    onehot = jnp.where(tokens == group_ref[...], 1.0, 0.0)
    counts = jnp.sum(onehot, axis=1, keepdims=True)
    d_lifted = d_tok + mm(onehot.astype(BF16), d_chr.astype(BF16))
    low = (d_lifted * slope_ref[...]).astype(BF16)
    mixed_ref[...] = low
    greet((1, lax.axis_size(CTX) - 1))
    copies = edges(mixed_ref, before_ref, after_ref, sems)
    d_mixed = low.astype(F32)
    sums_ref[0:1, :] = jnp.sum(d_mixed, axis=0, keepdims=True)
    sums_ref[5:8, :] = jnp.zeros((3, width), F32)
    conv.wait()
    deep = 2 * width
    taps = [conv_v.at[tap * deep : (tap + 1) * deep, :] for tap in range(3)]
    joined = mt(low, taps[1][...])
    earlier = mt(low, taps[0][...])
    later = mt(low, taps[2][...])
    for copy in copies:
        copy.wait()
    has_before, has_after = edge_masks()
    before = before_ref[...].astype(F32)[15:16, :] * has_before
    after = after_ref[...].astype(F32)[0:1, :] * has_after
    around_ref[:, 0:width] = moved(d_mixed, after, -1).astype(BF16)
    around_ref[:, width : 2 * width] = low
    around_ref[:, 2 * width : 3 * width] = moved(d_mixed, before, 1).astype(BF16)
    edge = mt(after_ref[...], taps[0][...])[0:1, :] * has_after
    joined = joined + moved(earlier, edge, -1)
    edge = mt(before_ref[...], taps[2][...])[15:16, :] * has_before
    joined = joined + moved(later, edge, 1)
    feat_ref[...] = d_tok + joined[:, 0:width]
    pool = (joined[:, width : 2 * width] / counts).astype(BF16)
    tokens = lax.broadcasted_iota(jnp.int32, (slots, rows), 1)
    across = jnp.where(tokens == column_ref[...], 1.0, 0.0).astype(BF16)
    states_ref[...] = chr_ref[...] + mm(across, pool)


def uniting_back(layer, w, g_tok, g_chr, saved, column, group):
    rows, width = g_tok.shape
    slots = g_chr.shape[0]
    outs = [
        ((rows, width), F32), ((slots, width), F32), ((slots, width), F32), ((rows, 3 * width), BF16),
        ((8, width), F32),
    ]
    edge = pltpu.VMEM((16, width), BF16)
    scratch = [
        room(w["conv"][0]), pltpu.VMEM((rows, width), BF16), edge, edge, DMA((1,)), [DMA((2,))] * 2,
    ]
    plain = [g_tok, g_chr, *(saved[k] for k in ("unit3", "scale3", "unit4", "scale4", "mixed_slope"))]
    return call(
        functools.partial(uniting_back_kernel, layer), plain + [column, group, w["vec"]],
        [*w["conv"]], outs, scratch, 6 + layer,
    )


def feed_back_kernel(
    layer, feat_ref, unit2_ref, scale2_ref, slope_ref, unit1_ref, scale1_ref, vec_ref,
    out_a, out_b, up_a, up_b, down_a, down_b,
    ffn_ref, hidden_ref, first_ref, branch_ref, att_ref, sums_ref, inner_ref,
    out_v, up_v, down_v, sems,
):
    rows, width = feat_ref.shape
    waits = [
        fetch(layer, a, b, v, sems.at[i])
        for i, (a, b, v) in enumerate([(out_a, out_b, out_v), (up_a, up_b, up_v), (down_a, down_b, down_v)])
    ]
    grad = feat_ref[...]
    unit = unit2_ref[...]
    sums_ref[0:1, :] = jnp.sum(grad * unit, axis=0, keepdims=True)
    sums_ref[1:2, :] = jnp.sum(grad, axis=0, keepdims=True)
    d_second = unit_back(unit, scale2_ref[...], grad * vec_ref[6:7, :])
    low = d_second.astype(BF16)
    ffn_ref[...] = low
    sums_ref[2:3, :] = jnp.sum(low.astype(F32), axis=0, keepdims=True)
    waits[2].wait()
    waits[1].wait()
    d_normed = d_second
    for begin in range(0, hidden_ref.shape[1], width):
        at = slice(begin, begin + width)
        hidden = (mt(low, down_v[at, :]) * slope_ref[:, at].astype(F32)).astype(BF16)
        hidden_ref[:, at] = hidden
        inner_ref[:, at] = jnp.sum(hidden.astype(F32), axis=0, keepdims=True)
        d_normed = d_normed + mt(hidden, up_v[:, at])
    unit = unit1_ref[...]
    sums_ref[3:4, :] = jnp.sum(d_normed * unit, axis=0, keepdims=True)
    sums_ref[4:5, :] = jnp.sum(d_normed, axis=0, keepdims=True)
    d_first = unit_back(unit, scale1_ref[...], d_normed * vec_ref[5:6, :])
    first_ref[...] = d_first
    low = d_first.astype(BF16)
    branch_ref[...] = low
    sums_ref[5:6, :] = jnp.sum(low.astype(F32), axis=0, keepdims=True)
    sums_ref[6:8, :] = jnp.zeros((2, width), F32)
    waits[0].wait()
    att_ref[...] = mt(low, out_v[...]).astype(BF16)


def feed_back(layer, w, d_feat, saved):
    rows, width = d_feat.shape
    inner = w["up"][0].shape[1]
    outs = [
        ((rows, width), BF16), ((rows, inner), BF16), ((rows, width), F32), ((rows, width), BF16),
        ((rows, width), BF16), ((8, width), F32), ((1, inner), F32),
    ]
    names = ("out", "up", "down")
    plain = [d_feat, *(saved[k] for k in ("unit2", "scale2", "slope", "unit1", "scale1"))]
    return call(
        functools.partial(feed_back_kernel, layer), plain + [w["vec"]],
        [a for name in names for a in w[name]], outs, [room(w[name][0]) for name in names] + [DMA((3,))],
    )


def project_back_kernel(
    layer, first_ref, dq_ref, dk_ref, dv_ref, qkv_a, qkv_b, own_ref, parts_ref, sums_ref, qkv_v, sems
):
    rows, width = dq_ref.shape
    qkv = fetch(layer, qkv_a, qkv_b, qkv_v, sems.at[0])
    sums_ref[...] = jnp.zeros_like(sums_ref)
    sums_ref[0:1, :] = jnp.sum(dq_ref[...].astype(F32), axis=0, keepdims=True)
    sums_ref[1:2, :] = jnp.sum(dv_ref[...].astype(F32), axis=0, keepdims=True)
    qkv.wait()
    for begin in range(0, dk_ref.shape[0], rows):
        at = slice(begin, begin + rows)
        value = mt(dk_ref[at, :], qkv_v[:, width : 2 * width]) + mt(dv_ref[at, :], qkv_v[:, 2 * width :])
        if begin == 0:
            own_ref[...] = first_ref[...] + value + mt(dq_ref[...], qkv_v[:, 0:width])
        else:
            parts_ref[begin - rows : begin, :] = value.astype(BF16)


def project_back(layer, w, d_first, dq, dk, dv):
    rows, width = dq.shape
    outs = [((rows, width), F32), ((dk.shape[0] - rows, width), BF16), ((8, width), F32)]
    return call(
        functools.partial(project_back_kernel, layer), [d_first, dq, dk, dv], [*w["qkv"]], outs,
        [room(w["qkv"][0]), DMA((1,))],
    )


def chars_back_kernel(
    layer, grad_ref, chr_ref, proj_ref, live_ref, before_ref, entering_ref, gru_a, gru_b,
    dproj_ref, dc_ref, sums_ref,
    gru_v, state_ref, decay_ref, carry_ref, total_ref, inbox_ref, fetch_sem, total_sems,
):
    count = lax.axis_size(CTX)
    width = proj_ref.shape[1] // 4
    slots = proj_ref.shape[0]
    steps = slots // CHUNKS
    gru = fetch(layer, gru_a, gru_b, gru_v, fetch_sem.at[0])
    greet(range(1, count))
    unroll = 8

    def step(i, carry):
        state_f, decay_f, state_b, decay_b = carry
        for u in range(unroll):
            at = step_rows(steps - 1 - i * unroll - u)
            keep = gates(proj_ref, live_ref, at, 0, width)[0]
            whole = grad_ref[at, 0:width] + state_f
            state_ref[at, 0:width] = whole
            decay_ref[at, 0:width] = decay_f
            state_f = keep * whole
            decay_f = keep * decay_f
            at = step_rows(i * unroll + u)
            keep = gates(proj_ref, live_ref, at, 2 * width, width)[0]
            whole = grad_ref[at, width : 2 * width] + state_b
            state_ref[at, width : 2 * width] = whole
            decay_ref[at, width : 2 * width] = decay_b
            state_b = keep * whole
            decay_b = keep * decay_b
        return state_f, decay_f, state_b, decay_b

    zero = jnp.zeros((CHUNKS, width), F32)
    one = jnp.ones((CHUNKS, width), F32)
    state_f, decay_f, state_b, decay_b = lax.fori_loop(
        0, steps // unroll, step, (zero, one, zero, one)
    )
    join_chunks(carry_ref, total_ref, 0, state_f, decay_f, range(CHUNKS - 1, -1, -1))
    join_chunks(carry_ref, total_ref, 2, state_b, decay_b, range(CHUNKS))
    entering = entering_chunks(carry_ref, total_ref, inbox_ref, total_sems, True)
    live = live_ref[...] > 0.0
    for side, carried in enumerate(entering):
        at = slice(side * width, (side + 1) * width)
        whole = by_step(state_ref[:, at]) + by_step(decay_ref[:, at]) * carried[None]
        whole = whole.reshape(slots, width)
        edge = entering_ref[:, at]
        if side == 0:
            before = jnp.concatenate([edge, before_ref[0 : slots - CHUNKS, at]], axis=0)
        else:
            before = jnp.concatenate([before_ref[CHUNKS:slots, at], edge], axis=0)
        opened = jax.nn.sigmoid(proj_ref[:, 2 * side * width : (2 * side + 1) * width])
        target = proj_ref[:, (2 * side + 1) * width : (2 * side + 2) * width]
        flow = jnp.where(live, whole * opened, 0.0)
        for part, value in enumerate((flow * (1.0 - opened) * (target - before), flow)):
            column = slice((2 * side + part) * width, (2 * side + part + 1) * width)
            low = value.astype(BF16)
            dproj_ref[:, column] = low
            sums_ref[:, column] = jnp.sum(low.astype(F32), axis=0, keepdims=True)
    gru.wait()
    dc_ref[...] = (chr_ref[...] + mt(dproj_ref[...], gru_v[...])).astype(BF16)


def middle_hop():
    return lax.axis_size(CTX) // 2


def chars_back(layer, w, d_states, d_chr, saved, live):
    slots, width = d_states.shape
    count = lax.axis_size(CTX)
    half = width // 2
    outs = [((slots, 4 * half), BF16), ((slots, width), BF16), ((1, 4 * half), F32)]
    scratch = [
        room(w["gru"][0]), pltpu.VMEM((slots, width), F32), pltpu.VMEM((slots, width), F32),
        pltpu.VMEM((4, CHUNKS, half), F32), pltpu.VMEM((8, half), F32),
        pltpu.VMEM((count - 1, 8, half), F32), DMA((1,)), [DMA((count - 1,))] * 2,
    ]
    plain = [d_states, d_chr, saved["proj"], live, saved["states"], saved["entering"]]
    return call(
        functools.partial(chars_back_kernel, layer), plain, [*w["gru"]], outs, scratch, 8 + layer,
    )


def layer_forward(layer, w, x, c, ids, live, group, column, seen):
    x_all, chars, chars_low, proj, states, entering, pooled = chars_forward(layer, w, x, c, ids, live, group)
    (
        query, keys, values, lse, attended, unit1, scale1, normed_low, active, slope, unit2, scale2, features,
    ) = tokens_forward(layer, w, x_all, seen, x.shape[0])
    tok_out, chr_out, joined, mixed_slope, unit3, scale3, unit4, scale4 = uniting_forward(
        layer, w, features, pooled, chars, states, column
    )
    saved = dict(
        x=x, x_all=x_all, chars_low=chars_low, proj=proj, states=states, entering=entering, query=query,
        keys=keys, values=values, lse=lse, attended=attended, unit1=unit1, scale1=scale1,
        normed_low=normed_low, active=active, slope=slope, unit2=unit2, scale2=scale2, joined=joined,
        mixed_slope=mixed_slope, unit3=unit3, scale3=scale3, unit4=unit4, scale4=scale4,
    )
    return tok_out, chr_out, saved


def bits_of(axis):
    return [(axis, bit) for bit in range(lax.axis_size(axis).bit_length() - 1)]


def exchange_order(x_first):
    dp = bits_of(DP)
    return (dp if x_first else dp[::-1]) + bits_of(CTX)


def shard_at(place, order, n_ctx):
    index = {DP: lax.axis_index(DP), CTX: lax.axis_index(CTX)}
    shard = index[DP] * n_ctx + index[CTX]
    for nth, (axis, bit) in enumerate(order):
        if (place >> (len(order) - 1 - nth)) & 1:
            mine = (index[axis] // (1 << bit)) % 2
            shard = shard + (1 - 2 * mine) * ((1 << bit) * (n_ctx if axis == DP else 1))
    return shard


class Packing:
    def __init__(self, section, unit, groups):
        self.section, self.unit, self.groups = section, unit, groups
        self.arrays, self.moves, self.jobs, self.rows = [], [], [], [0] * len(groups)

    def operand(self, value, pieces=None):
        width = value.shape[1]
        self.arrays.append(value)
        self.moves.append([(0, 0, width)] if pieces is None else [(b, h, h) for b, h in pieces])
        return len(self.arrays) - 1

    def local(self, *values):
        self.arrays.extend(values)
        self.moves.extend([None] * len(values))
        return len(self.arrays) - len(values)

    def product(self, group, left, chunks, size):
        self.jobs.append(dict(group=group, left=left, chunks=chunks, rows=size, row=self.rows[group]))
        self.rows[group] += size * len(chunks)

    def plain(self, group, value, size):
        self.jobs.append(
            dict(group=group, left=None, plain=self.local(value), rows=size, row=self.rows[group])
        )
        self.rows[group] += size

    def run(self, collective_id, parts=None):
        orders = [exchange_order(x_first) for x_first in self.groups]
        n_ctx = lax.axis_size(CTX)
        count = lax.axis_size(DP) * n_ctx
        unit = self.unit
        if any(job["rows"] % 16 for job in self.jobs):
            results = self.run_plainly(orders, n_ctx, count)
            return results if parts is None else (results, came_back(parts))
        outs = [((count // 2, rows, unit), BF16) for rows in self.rows for _ in (0, 1)]
        most = max(job["rows"] * len(job.get("chunks", (0,))) for job in self.jobs) * count
        coming = [
            pltpu.VMEM((a.shape[0], sum(piece[2] for piece in move)), a.dtype)
            for a, move in zip(self.arrays, self.moves)
            if move
        ]
        copies = sum(len(move) for move in self.moves if move)
        scratch = [pltpu.VMEM((most, unit), BF16), coming, [DMA((copies,))] * 2]
        kernel = functools.partial(pack_kernel, self.jobs, self.moves, count, orders, n_ctx, parts is not None)
        plain = list(self.arrays)
        if parts is not None:
            plain.append(parts)
            outs.append((parts.shape, parts.dtype))
            scratch.append([DMA((n_ctx - 1,))] * 2)
        results = call(kernel, plain, [], outs, scratch, collective_id)
        packs = [(results[2 * i], results[2 * i + 1]) for i in range(len(orders))]
        return packs if parts is None else (packs, results[-1])

    def run_plainly(self, orders, n_ctx, count):
        blocks = [[] for _ in orders]
        for job in self.jobs:
            if job["left"] is None:
                blocks[job["group"]].append(self.arrays[job["plain"]].reshape(count, job["rows"], self.unit))
                continue
            for right, begin, half, _ in job["chunks"]:
                parts = []
                for core in (0, 1):
                    one = self.arrays[job["left"]]
                    if self.moves[right] is None:
                        two = self.arrays[right + core]
                    else:
                        two = swap(self.arrays[right]) if core else self.arrays[right]
                    two = lax.dynamic_slice_in_dim(two, begin + self.section * half, self.unit, 1)
                    parts.append(tm(swap(one) if core else one, two))
                value = (parts[0] + parts[1]).astype(BF16)
                blocks[job["group"]].append(value.reshape(count, job["rows"], self.unit))
        results = []
        for order, parts in zip(orders, blocks):
            shards = jnp.stack([shard_at(place, order, n_ctx) for place in range(count)])
            whole = jnp.take(jnp.concatenate(parts, axis=1), shards, axis=0)
            results.append((whole[count // 2 :], whole[: count // 2]))
        return results


def pack_kernel(jobs, moves, count, orders, n_ctx, beside, *refs):
    arrays, rest = refs[: len(moves)], refs[len(moves) :]
    if beside:
        parts_ref, rest, part_sems = rest[0], rest[1:-1], rest[-1]
    outs, rest = rest[: 2 * len(orders)], rest[2 * len(orders) :]
    if beside:
        back_ref, rest = rest[0], rest[1:]
    held, coming, semaphores = rest
    send_sems, recv_sems = semaphores
    section = lax.axis_index(SEC)
    unit = held.shape[1]
    barrier = pltpu.get_barrier_semaphore()
    pl.semaphore_signal(barrier, inc=1, device_id={SEC: 1 - section}, device_id_type=MESH)
    if beside:
        for hop in range(1, n_ctx):
            to = lax.rem(lax.axis_index(CTX) + hop, n_ctx)
            pl.semaphore_signal(barrier, inc=1, device_id={CTX: to}, device_id_type=MESH)
    pl.semaphore_wait(barrier, n_ctx if beside else 1)
    sides = []
    if beside:
        rows = parts_ref.shape[0] // (n_ctx - 1)
        for j in range(1, n_ctx):
            if j == middle_hop():
                continue
            at = slice((j - 1) * rows, j * rows)
            sems = [sem.at[j - 1] for sem in part_sems]
            sides.append(send(parts_ref.at[at, :], back_ref.at[at, :], n_ctx - j, *sems))
    places, copies, pending, nth, slot = {}, [], {}, 0, 0
    for index, move in enumerate(moves):
        if not move:
            continue
        target, at = coming[slot], 0
        places[index] = target
        pending[index] = []
        slot += 1
        for begin, half, width in move:
            source = arrays[index]
            if half:
                source = source.at[:, pl.ds(pl.multiple_of(begin + (1 - section) * half, 128), width)]
            copy = pltpu.make_async_remote_copy(
                src_ref=source,
                dst_ref=target.at[:, at : at + width] if half else target,
                send_sem=send_sems.at[nth],
                recv_sem=recv_sems.at[nth],
                device_id={SEC: 1 - section},
                device_id_type=MESH,
            )
            copy.start()
            copies.append(copy)
            pending[index].append(copy)
            at += width
            nth += 1
    for job in jobs:
        at, size = job["row"], job["rows"]
        total = count * size
        if job["left"] is None:
            held[0:total, :] = arrays[job["plain"]][...]
            chunks = [None]
        else:
            left, chunks = job["left"], job["chunks"]
            mine, theirs = [], []
            for index in [left] + [chunk[0] for chunk in chunks]:
                for copy in pending.pop(index, ()):
                    copy.wait_recv()
            for right, begin, half, there in chunks:
                if moves[right]:
                    column = pl.multiple_of(begin + section * half, 128)
                    mine.append(arrays[right][:, pl.ds(column, unit)])
                    theirs.append(places[right][:, there : there + unit])
                else:
                    mine.append(arrays[right][:, begin : begin + unit])
                    theirs.append(arrays[right + 1][:, begin : begin + unit])
            mine = jnp.concatenate(mine, axis=1)
            theirs = jnp.concatenate(theirs, axis=1)
            for begin in range(0, total, 768):
                span = slice(begin, begin + 768)
                value = tm(arrays[left][:, span], mine) + tm(places[left][:, span], theirs)
                for nth in range(len(chunks)):
                    held[nth * total + begin : nth * total + begin + 768, :] = value[
                        :, nth * unit : (nth + 1) * unit
                    ].astype(BF16)
        sent_ref, kept_ref = outs[2 * job["group"] : 2 * job["group"] + 2]
        for place in range(count):
            shard = shard_at(place, orders[job["group"]], n_ctx) * size
            target = kept_ref if place < count // 2 else sent_ref
            for nth in range(len(chunks)):
                begin = pl.multiple_of(shard + nth * total, 16)
                row = at + nth * size
                target[place % (count // 2), row : row + size, :] = held[pl.ds(begin, size), :]
    for copy in copies:
        copy.wait_send()
    for copy in sides:
        copy.wait()


class Halving:
    def __init__(self, packed, x_first):
        self.sent, self.kept = packed
        self.order = exchange_order(x_first)
        self.total = None

    def step(self, after):
        key, self.order = self.order[0], self.order[1:]
        got = flip(self.sent, *key)
        got, kept, after = lax.optimization_barrier((got, self.kept, after))
        if not self.order:
            self.total = kept[0].astype(F32) + got[0].astype(F32)
            self.total, after = lax.optimization_barrier((self.total, after))
            return after
        cut = kept.shape[0] // 2
        sent = (kept[cut:].astype(F32) + got[cut:].astype(F32)).astype(BF16)
        kept = (kept[:cut].astype(F32) + got[:cut].astype(F32)).astype(BF16)
        self.sent, self.kept, after = lax.optimization_barrier((sent, kept, after))
        return after


class Queue:
    def __init__(self):
        self.chains = []

    def add(self, chains):
        self.chains.extend(chains)

    def advance(self, value, layer, part):
        for chain in PLAN.get((layer, part), ()):
            if self.chains[chain].order:
                value = self.chains[chain].step(value)
        return value

    def round(self, after):
        for chain in TAIL:
            if self.chains[chain].order:
                after = self.chains[chain].step(after)
        return after

    def finish(self, after):
        while any(chain.order for chain in self.chains):
            after = self.round(after)
        return after


PLAN = {
    (1, 1): (0, 1),
    (0, 3): (0, 1),
    (0, 4): (0, 1, 2, 3),
    (0, 0): (0, 1, 2, 3),
}
TAIL = (0, 1, 2, 3, 4, 5, 6, 7)


def came_back(parts):
    n_ctx = lax.axis_size(CTX)
    rows = parts.shape[0] // (n_ctx - 1)
    return jnp.concatenate([turned(parts[(j - 1) * rows : j * rows], n_ctx - j) for j in range(1, n_ctx)])


def layer_backward(layer, w, saved, g_tok, g_chr, ids_both, live, group_row, column, seen, section, queue):
    rows, width = g_tok.shape
    count = lax.axis_size(DP) * lax.axis_size(CTX)
    unit = width // 2
    block = width // count
    d_feat, d_chr, d_states, around, sums_a = uniting_back(layer, w, g_tok, g_chr, saved, column, group_row)
    d_feat = queue.advance(d_feat, layer, 3)
    d_ffn, d_hidden, d_first, d_branch, d_attended, sums_b, inner_sums = feed_back(layer, w, d_feat, saved)
    d_attended = queue.advance(d_attended, layer, 4)
    early = Packing(section, unit, (True, False))
    taps = around.shape[1] // width
    right = early.operand(around, [(t * width, unit) for t in range(taps)])
    chunks = [(right, t * width, unit, t * unit) for t in range(taps)]
    early.product(0, early.operand(saved["joined"]), chunks, 2 * block)
    ups = d_hidden.shape[1] // 2
    right = early.operand(d_hidden, [(0, ups)])
    chunks = [(right, begin, ups, begin) for begin in range(0, ups, unit)]
    early.product(1, early.operand(saved["normed_low"]), chunks, block)
    right = early.operand(d_branch, [(0, unit)])
    early.product(1, early.operand(saved["attended"]), [(right, 0, unit, 0)], block)
    packs = early.run(0)
    packs, d_attended = lax.optimization_barrier((packs, d_attended))
    chains = [Halving(pack, x_first) for pack, x_first in zip(packs, early.groups)]
    queue.add(chains)
    dq, dk, dv = attend_back(
        saved["query"], saved["keys"], saved["values"], seen, saved["lse"], d_attended
    )
    dq = queue.advance(dq, layer, 0)
    if layer:
        d_states, dq = lax.optimization_barrier((d_states, dq))
    d_proj, d_c, proj_sums = chars_back(layer, w, d_states, d_chr, saved, live)
    dq, d_proj = lax.optimization_barrier((dq, d_proj))
    d_x, parts, sums_c = project_back(layer, w, d_first, dq, dk, dv)
    middle = middle_hop() - 1
    part_back = turned(parts[middle * rows : (middle + 1) * rows], lax.axis_size(CTX) - middle_hop())
    d_proj = queue.advance(d_proj, layer, 1)
    small = (
        jnp.stack([sums_c[0], sums_c[1], sums_b[5], sums_b[2], sums_a[0]]),
        inner_sums,
        jnp.stack([sums_b[3], sums_b[0], sums_a[1], sums_a[3]]),
        jnp.stack([sums_b[4], sums_b[1], sums_a[2], sums_a[4]]),
        proj_sums,
    )
    packed = jnp.concatenate(
        [jnp.swapaxes(p.reshape(p.shape[0], count, -1), 0, 1).reshape(count, -1) for p in small], axis=1
    )
    packed = jnp.pad(packed, ((0, 0), (0, 16 * unit - packed.shape[1])))
    late = Packing(section, unit, (True, False))
    right = late.operand(d_ffn, [(0, unit)])
    late.product(0, late.operand(saved["active"]), [(right, 0, unit, 0)], 4 * block)
    left = late.operand(d_c)
    split = w["table"][0].shape[0] // 2
    named = []
    for names in ids_both:
        names = names - section * split
        named.append((names == jnp.arange(2 * unit)[None, :]).astype(BF16))
    right = late.local(*named)
    late.product(0, left, [(right, 0, 0, 0), (right, unit, 0, 0)], block)
    right = late.operand(dq, [(0, unit)])
    late.product(1, late.operand(saved["x"]), [(right, 0, unit, 0)], block)
    rights = [late.operand(grad, [(0, unit)]) for grad in (dk, dv)]
    late.product(1, late.operand(saved["x_all"]), [(right, 0, unit, 0) for right in rights], block)
    right = late.operand(d_proj, [(0, width)])
    chunks = [(right, begin, width, begin) for begin in range(0, width, unit)]
    late.product(1, late.operand(saved["chars_low"]), chunks, block)
    late.plain(1, packed.astype(BF16).reshape(-1, unit), 16)
    packs, back = late.run(1, parts)
    packs, d_c, back = lax.optimization_barrier((packs, d_c, back))
    g_x = d_x + part_back.astype(F32)
    for j in range(len(back) // rows):
        if j != middle:
            g_x = g_x + back[j * rows : (j + 1) * rows].astype(F32)
    g_x = g_x.astype(BF16)
    more = [Halving(pack, x_first) for pack, x_first in zip(packs, late.groups)]
    queue.add(more)
    d_c = queue.advance(d_c, layer, 2)
    sizes = [(p.shape[0], p.size // count // p.shape[0]) for p in small]
    return g_x, d_c, chains + more, sizes


def on_device(
    ends, char_ends, char_ids, groups, lengths, w_qkv, biases, w_out, w_up, b_up, w_down,
    ln_gain, ln_shift, char_table, w_gru, b_gru, w_conv,
):
    section = lax.axis_index(SEC)
    n_dp, n_ctx = lax.axis_size(DP), lax.axis_size(CTX)
    is_first = section == 0
    def turned_rows(value):
        shape = value.shape
        return jnp.swapaxes(value.reshape((shape[0], CHUNKS, -1) + shape[2:]), 1, 2).reshape(shape)

    padded = jnp.pad(char_table[0], ((0, -char_table.shape[1] % 256), (0, 0)))
    rows_16 = jnp.concatenate([biases[0], ln_gain[0], ln_shift[0], jnp.zeros_like(biases[0, :3])])
    inner_own = jnp.concatenate([b_up, b_gru], axis=1)
    indices = turned_rows(jnp.concatenate([char_ids, groups]))
    (
        x, cot_tok, c, cot_chr, vec0, vec1, inner0, inner1, ids, ids_other, live, group_row, column, seen,
        gru_other, table_other,
    ) = deal(lengths, ends[0], turned_rows(char_ends[0]), indices, rows_16, inner_own, w_gru[0], padded)
    ids_both = (ids, ids_other)
    weights = {"gru": (w_gru[0], gru_other), "table": (padded, table_other)}
    for name, own in (
        ("qkv", w_qkv[0]), ("out", w_out[0]), ("up", w_up[0]), ("down", w_down[0]),
        ("conv", w_conv[0].reshape(-1, w_conv.shape[3])),
    ):
        tied, x = lax.optimization_barrier((own, x))
        weights[name] = (own, swap(tied))
    layers = [
        dict(weights, vec=vec, b_up=inner[:, : b_up.shape[1]], b_gru=inner[:, b_up.shape[1] :])
        for vec, inner in ((vec0, inner0), (vec1, inner1))
    ]
    rows, width = x.shape

    kept = []
    for layer in (0, 1):
        x, c, saved = layer_forward(
            layer, layers[layer], x, c, ids, live, group_row, column, seen
        )
        kept.append(saved)
    g_x, g_c = cot_tok, cot_chr
    queue = Queue()
    chains = [None, None]
    for layer in (1, 0):
        g_x, g_c, chains[layer], sizes = layer_backward(
            layer, layers[layer], kept[layer], g_x, g_c, ids_both, live, group_row, column, seen, section, queue
        )
    queue.finish(jnp.zeros((), F32))
    packs = [[chain.total for chain in four] for four in chains]

    def gathered(grad, value):
        got = swap(jnp.where(is_first, value, grad))
        return jnp.where(is_first, jnp.stack([grad, got]), jnp.stack([got, value]))[None]

    ends_out = gathered(g_x, x)
    char_ends_out = gathered(restore(g_c), restore(c))

    both = []
    for one, two in zip(*packs):
        mine = jnp.where(is_first, one, two)
        got = swap(jnp.where(is_first, two, one))
        both.append((jnp.where(is_first, mine, got), jnp.where(is_first, got, mine)))
    block = width // (n_dp * n_ctx)

    def columns(which, at, size, parts, crossed=False):
        cut = [[half[at + i * size : at + (i + 1) * size] for i in range(parts)] for half in both[which]]
        if crossed:
            return jnp.concatenate([half[i] for i in range(parts) for half in cut], axis=1)
        return jnp.concatenate(cut[0] + cut[1], axis=1)

    d_conv = jnp.stack([columns(0, tap * 2 * block, 2 * block, 1) for tap in range(w_conv.shape[1])])
    ups = w_up.shape[2] // width
    d_up = columns(1, 0, block, ups)
    d_out = columns(1, ups * block, block, 1)
    d_down = columns(2, 0, ups * block, 1)
    at = ups * block
    split = padded.shape[0] // 2
    d_table = jnp.concatenate(
        [
            jnp.concatenate([half[at : at + block], half[at + block : at + 2 * block]], axis=1)[:, :take]
            for half, take in zip(both[2], (split, char_table.shape[1] - split))
        ],
        axis=1,
    ).T
    d_qkv = columns(3, 0, block, 3, True)
    d_gru = columns(3, 3 * block, block, 2)
    vectors = (both[3][0][5 * block :] + both[3][1][5 * block :]).reshape(-1)
    sums, at = [], 0
    for parts, size in sizes:
        sums.append(vectors[at : at + parts * size].reshape(parts, size))
        at += parts * size
    return (
        ends_out,
        char_ends_out,
        d_qkv[None],
        sums[0][None],
        d_out[None],
        d_up[None],
        sums[1],
        d_down[None],
        sums[2][None],
        sums[3][None],
        d_table[None],
        d_gru[None],
        sums[4],
        d_conv[None],
    )


def solution(mesh):
    both = (DP, CTX)
    held, rows, columns = P(SEC, DP, CTX), P(SEC, both), P(SEC, None, both)
    layer = P(SEC)
    in_specs = (held, held, P(DP, CTX), P(DP, CTX), P(DP)) + (layer,) * 12
    out_specs = (
        held, held, rows, columns, rows, rows, rows, rows, columns, columns, columns, rows, rows, columns,
    )
    return jax.shard_map(
        on_device, mesh=mesh, in_specs=in_specs, out_specs=out_specs, check_vma=False
    )
```
